32 devices in a mesh: rad: 4 (over y, x), azi: 8 (over z, core).
Axes of the slice: x: 2, y: 2, z: 4, core: 2. Of those that a mesh axis runs over, the one named last changes fastest.
Arguments:
- tokens: bfloat16 [32, 128, 8, 512], P('rad', 'azi'), may hold values from -6 to 6
- cotangent: bfloat16 [32, 128, 8, 512], P('rad', 'azi'), may hold values from -6 to 6
- ln_gain: float32 [512], replicated, may hold values from 0.5 to 1.5
- qkv_weight: bfloat16 [512, 1536], P('azi'), may hold values from -2 to 2
- out_weight: bfloat16 [512, 512], P('azi'), may hold values from -0.25 to 0.25
- shear_offset: int32 [1], replicated, may hold values from 0 to 127
- window_shift: int32 [3], replicated, may hold values from 1 to 7, as said below
Outputs:
- block_out: bfloat16 [32, 128, 8, 512], P('rad', 'azi')
- grad_tokens: bfloat16 [32, 128, 8, 512], P('rad', 'azi')
- grad_qkv: float32 [512, 1536], P('azi')
- grad_out: float32 [512, 512], P('azi')
- grad_gain: float32 [512], replicated
The draws below stay inside these ranges and needn't reach their ends.
Inputs may be any that keep to these rules, and one draw needn't show every extreme that they name: `window_shift`: the radial entry lies in 1 to 3; the azimuthal and vertical entries lie in 1 to 7, and one of these two equals 7.
All inputs are finite; a program needn't handle non-finite values.
Results may differ from the reference program's by a relative error of at most 0.025.
Values may be sent and summed in bfloat16 or wider, within the bound.
No kernel may reach another device: no remote copies, remote signals or barrier semaphores. Data moves between devices by JAX's collectives and lax.ppermute only.
A program may use at most 192 MiB of HBM per device.

```python
import jax
import jax.numpy as jnp
from jax import lax

D = 512
HEADS = 16
HD = 32
WR = 4
WA = 8
WZ = 8
NR = 32
NA = 128
NZ = 8
TOKENS = 32768


def draw_qkv_weight(key, part):
    first_key = jax.random.fold_in(jax.random.fold_in(key, 11), 0)
    drawn = jax.random.normal(first_key, (D, 3 * D), jnp.float32) / D ** 0.5
    return jnp.clip(drawn, -2.0, 2.0).astype(jnp.bfloat16)


def draw_window_shift(key, part):
    first_key, second_key, third_key, fourth_key = jax.random.split(jax.random.fold_in(key, 23), 4)
    radial = jax.random.randint(first_key, (1,), 1, WR)
    azimuthal = jax.random.randint(second_key, (1,), 1, WA)
    vertical = jax.random.randint(third_key, (1,), 1, WZ)
    picker = jax.random.randint(fourth_key, (1,), 0, 2)
    azimuthal = jnp.where(picker == 1, WA - 1, azimuthal)
    vertical = jnp.where(picker == 0, WZ - 1, vertical)
    return jnp.concatenate([radial, azimuthal, vertical]).astype(jnp.int32)


def raised(result, stream_key, source, target, blocks, factor):
    def block_of(axis_at):
        return (jnp.arange(result.shape[axis_at]) // (result.shape[axis_at] // blocks)).reshape((-1,) + (1,) * (result.ndim - 1 - axis_at))

    first = jax.random.permutation(stream_key, blocks)[block_of(target)]
    second = (block_of(target) + blocks // 2) % blocks
    return jnp.where((block_of(source) == first) | (block_of(source) == second), factor * result, result)


def level_of(own_key, extent, cuts, low, largest):
    factor_of, own = 1.0, jax.random.fold_in(own_key, 6)
    for axis_at, blocks in cuts:
        steps = jnp.exp(jax.random.uniform(jax.random.fold_in(own, axis_at), (blocks,), jnp.float32, low / len(cuts), largest / len(cuts)))
        factor_of = factor_of * jnp.repeat(steps, extent[axis_at] // blocks).reshape([-1 if axis == axis_at else 1 for axis in range(len(extent))])
    return factor_of


def bell_draw(rng, shape, deviation, limit, shards=(), held_as=jnp.bfloat16):
    values = jax.random.normal(rng, shape, jnp.float32) * deviation
    if len(shards) > 0:
        values = level_of(rng, shape, shards, -0.22, 0.18) * values
    return jnp.clip(values, min=-limit, max=limit).astype(held_as)


def gaussian_with(key, shape, deviation, limit, pieces, heavy, kind=jnp.bfloat16):
    drawn = deviation * jax.random.normal(key, shape, jnp.float32)
    if pieces:
        drawn = drawn * level_of(key, shape, pieces, -0.22, 0.18)
    return jnp.clip(raised(drawn, jax.random.fold_in(key, 3), *heavy), -limit, limit).astype(kind)


def setup_inputs(seed: int = 0) -> dict:
    key_of = jax.random.split(jax.random.key(seed), 8)
    tokens = gaussian_with(key_of[0], (NR, NA, NZ, D), 1.0, 6.0, ((0, 4), (1, 8)), (1, 3, 8, 2.0))
    cotangent = bell_draw(key_of[1], (NR, NA, NZ, D), 1.0, 6.0, ((0, 4), (1, 8)))
    ln_gain = jnp.clip(1.0 + 0.1 * jax.random.normal(key_of[2], (D,), jnp.float32), 0.5, 1.5)
    qkv_weight = draw_qkv_weight(jax.random.fold_in(key_of[7], 71), 0)
    out_weight = bell_draw(key_of[4], (D, D), D ** -0.5, 0.25, ((0, 8),))
    shear_offset = jax.random.randint(key_of[5], (1,), 0, NA).astype(jnp.int32)
    window_shift = draw_window_shift(jax.random.fold_in(key_of[7], 71), 0)
    return {"tokens": tokens, "cotangent": cotangent, "ln_gain": ln_gain, "qkv_weight": qkv_weight, "out_weight": out_weight, "shear_offset": shear_offset, "window_shift": window_shift}


EPS = 1e-05

def to_windows(tensor, parts):
    extent_r, extent_a, extent_z, channels = tensor.shape
    tensor = tensor.reshape(extent_r // WR, WR, extent_a // WA, WA, extent_z // WZ, WZ, parts, HEADS, HD)
    tensor = tensor.transpose(0, 2, 4, 6, 7, 1, 3, 5, 8)
    return tensor.reshape(-1, parts, HEADS, WR * WA * WZ, HD)

def from_windows(windows, extent_r, extent_a, extent_z):
    parts = windows.shape[1]
    windows = windows.reshape(extent_r // WR, extent_a // WA, extent_z // WZ, parts, HEADS, WR, WA, WZ, HD)
    windows = windows.transpose(0, 5, 1, 6, 2, 7, 3, 4, 8)
    return windows.reshape(extent_r, extent_a, extent_z, parts * HEADS * HD)

def block_pass(shifted, grad_in, ln_gain, qkv_weight, out_weight):
    extent_r, extent_a, extent_z, width = shifted.shape
    number = extent_r * extent_a * extent_z
    contract = (((0,), (0,)), ((), ()))
    scaling = HD ** (-0.5)
    inputs_f = shifted.astype(jnp.float32).reshape(number, width)
    centre = lax.optimization_barrier(jnp.mean(inputs_f, axis=1, keepdims=True))
    centred = inputs_f - centre
    variance = lax.optimization_barrier(jnp.mean(centred * centred, axis=1, keepdims=True))
    inverse_std = lax.rsqrt(variance + EPS)
    normed = centred * inverse_std
    hidden = (normed * ln_gain).astype(jnp.bfloat16)
    qkv = jnp.dot(hidden, qkv_weight, preferred_element_type=jnp.float32).astype(jnp.bfloat16)
    qkv = lax.optimization_barrier(qkv)
    windows = to_windows(qkv.reshape(extent_r, extent_a, extent_z, 3 * width), 3).astype(jnp.float32)
    queries, keys_win, values = (windows[:, 0], windows[:, 1], windows[:, 2])
    scores = jnp.einsum('nhqd,nhkd->nhqk', queries, keys_win) * scaling
    weights = jax.nn.softmax(scores, axis=-1)
    weights_low = lax.optimization_barrier(weights.astype(jnp.bfloat16))
    weights_lf = weights_low.astype(jnp.float32)
    mixed = jnp.einsum('nhqk,nhkd->nhqd', weights_lf, values).astype(jnp.bfloat16)
    attended = from_windows(mixed[:, None], extent_r, extent_a, extent_z).reshape(number, width)
    branch = jnp.dot(attended, out_weight, preferred_element_type=jnp.float32)
    out_shifted = (inputs_f + branch).astype(jnp.bfloat16)
    grad_low = grad_in.reshape(number, width)
    d_attended = jnp.dot(grad_low, out_weight.T, preferred_element_type=jnp.float32).astype(jnp.bfloat16)
    d_attended = lax.optimization_barrier(d_attended)
    d_windows = to_windows(d_attended.reshape(extent_r, extent_a, extent_z, width), 1)[:, 0].astype(jnp.float32)
    d_weights = jnp.einsum('nhqd,nhkd->nhqk', d_windows, values)
    d_values = jnp.einsum('nhqk,nhqd->nhkd', weights_lf, d_windows)
    d_scores = weights * (d_weights - lax.optimization_barrier(jnp.sum(weights * d_weights, axis=-1, keepdims=True)))
    d_scores = lax.optimization_barrier(d_scores.astype(jnp.bfloat16)).astype(jnp.float32)
    d_queries = jnp.einsum('nhqk,nhkd->nhqd', d_scores, keys_win) * scaling
    d_keys = jnp.einsum('nhqk,nhqd->nhkd', d_scores, queries) * scaling
    d_stack = jnp.stack([d_queries, d_keys, d_values], axis=1).astype(jnp.bfloat16)
    d_qkv = from_windows(d_stack, extent_r, extent_a, extent_z).reshape(number, 3 * width)
    d_hidden = jnp.dot(d_qkv, qkv_weight.T, preferred_element_type=jnp.float32)
    grad_qkv = lax.dot_general(hidden, d_qkv, contract, preferred_element_type=jnp.float32)
    grad_out = lax.dot_general(attended, grad_low, contract, preferred_element_type=jnp.float32)
    grad_gain = lax.optimization_barrier(jnp.sum(d_hidden * normed, axis=0))
    d_normed = d_hidden * ln_gain
    d_branch = inverse_std * (d_normed - lax.optimization_barrier(jnp.mean(d_normed, axis=1, keepdims=True)) - normed * lax.optimization_barrier(jnp.mean(d_normed * normed, axis=1, keepdims=True)))
    grad_shifted = (grad_low.astype(jnp.float32) + d_branch).astype(jnp.bfloat16)
    shape_out = (extent_r, extent_a, extent_z, width)
    return (out_shifted.reshape(shape_out), grad_shifted.reshape(shape_out), grad_qkv, grad_out, grad_gain)

def reference(tokens, cotangent, ln_gain, qkv_weight, out_weight, shear_offset, window_shift):
    shift_rad = window_shift[0]
    shift_azi = window_shift[1]
    shift_ver = window_shift[2]
    offset = shear_offset[0]
    rows_fwd = jnp.arange(NR, dtype=jnp.int32) + shift_rad
    wrap_fwd = (rows_fwd >= NR).astype(jnp.int32)
    rows_fwd = rows_fwd % NR
    cols_fwd = (jnp.arange(NA, dtype=jnp.int32)[None, :] + shift_azi + offset * wrap_fwd[:, None]) % NA
    levels_fwd = (jnp.arange(NZ, dtype=jnp.int32) + shift_ver) % NZ
    shifted = tokens[rows_fwd[:, None], cols_fwd][:, :, levels_fwd]
    grad_shift = cotangent[rows_fwd[:, None], cols_fwd][:, :, levels_fwd]
    blocks = NR // WR
    shifted = shifted.reshape(blocks, WR, NA, NZ, D)
    grad_shift = grad_shift.reshape(blocks, WR, NA, NZ, D)

    def scan_step(totals, block_pair):
        out_block, grad_block, term_qkv, term_out, term_gain = block_pass(block_pair[0], block_pair[1], ln_gain, qkv_weight, out_weight)
        return ((totals[0] + term_qkv, totals[1] + term_out, totals[2] + term_gain), (out_block, grad_block))
    start = (jnp.zeros((D, 3 * D), jnp.float32), jnp.zeros((D, D), jnp.float32), jnp.zeros((D,), jnp.float32))
    totals, outputs = lax.scan(scan_step, start, (shifted, grad_shift))
    out_shifted = outputs[0].reshape(NR, NA, NZ, D)
    grad_shifted = outputs[1].reshape(NR, NA, NZ, D)
    rows_back = jnp.arange(NR, dtype=jnp.int32) - shift_rad
    wrap_back = (rows_back < 0).astype(jnp.int32)
    rows_back = rows_back % NR
    cols_back = (jnp.arange(NA, dtype=jnp.int32)[None, :] - shift_azi - offset * wrap_back[:, None]) % NA
    levels_back = (jnp.arange(NZ, dtype=jnp.int32) - shift_ver) % NZ
    block_out = out_shifted[rows_back[:, None], cols_back][:, :, levels_back]
    grad_tokens = grad_shifted[rows_back[:, None], cols_back][:, :, levels_back]
    factor = float(TOKENS) ** (-0.5)
    return (block_out, grad_tokens, totals[0] * factor, totals[1] * factor, totals[2] * factor)
```

```python
import jax
import jax.numpy as jnp
from jax import lax
from jax.experimental import pallas as pl
from jax.experimental.pallas import tpu as pltpu
from jax.sharding import PartitionSpec as P

HEADS = 16
HD = 32
WR = 4
WA = 8
WZ = 8
LANES = 128
LOG2E = 1.4426950408889634

EPS = 1e-05
NT = (((1,), (1,)), ((), ()))
TN = (((0,), (0,)), ((), ()))


def mm(a, b, dims=(((1,), (0,)), ((), ()))):
    return lax.dot_general(a, b, dims, preferred_element_type=jnp.float32)


def block_kernel(
    x_ref, g_ref, gain_ref, wqkv_ref, wout_ref,
    y_ref, dx_ref, gw_ref, gg_ref,
    xhat_s, qkv_s, da_s, att_s, dqkv_s, hid_all, att_all, gs_all, dqkv_all, gain_s,
):
    step = pl.program_id(0)
    steps = pl.num_programs(0)
    width = x_ref.shape[-1]
    tokens = WR * WA * WZ
    x = x_ref[...].astype(jnp.float32).reshape(tokens, width)
    gs_f = g_ref[...].astype(jnp.float32).reshape(tokens, width)
    gs = gs_f.astype(jnp.bfloat16)
    gain = gain_ref[...]
    centred = x - jnp.mean(x, axis=1, keepdims=True)
    inv = lax.rsqrt(jnp.mean(centred * centred, axis=1, keepdims=True) + EPS)
    xhat = centred * inv
    xhat_s[...] = xhat
    hidden = (xhat * gain).astype(jnp.bfloat16)
    qkv_s[...] = mm(hidden, wqkv_ref[...]).astype(jnp.bfloat16)
    da_s[...] = mm(gs, wout_ref[...], NT).astype(jnp.bfloat16)
    scaling = HD ** (-0.5)
    lane = lax.broadcasted_iota(jnp.int32, (1, LANES), 1)
    per_group = LANES // HD

    def group(g, carry):
        base = pl.multiple_of(g * LANES, LANES)
        q = qkv_s[:, pl.ds(base, LANES)]
        k = qkv_s[:, pl.ds(width + base, LANES)]
        v = qkv_s[:, pl.ds(2 * width + base, LANES)]
        da = da_s[:, pl.ds(base, LANES)]
        k_t = k.astype(jnp.float32).T.astype(jnp.bfloat16)
        v_t = v.astype(jnp.float32).T.astype(jnp.bfloat16)
        dv = jnp.zeros((tokens, LANES), jnp.float32)
        dk = jnp.zeros((tokens, LANES), jnp.float32)
        att_t, dq_t = [], []
        for h in range(per_group):
            mine = (lane >= h * HD) & (lane < (h + 1) * HD)
            mask = jnp.where(mine, 1.0, 0.0).astype(jnp.bfloat16)
            qm = q * mask
            dam = da * mask
            s = mm(k, qm, NT) * (scaling * LOG2E)
            e = jnp.exp2(s - jnp.max(s, axis=0, keepdims=True))
            p = e * (1.0 / jnp.sum(e, axis=0, keepdims=True))
            p_low = p.astype(jnp.bfloat16)
            dp = mm(v, dam, NT)
            ds = p * (dp - jnp.sum(p * dp, axis=0, keepdims=True))
            ds = ds.astype(jnp.bfloat16)
            dv += mm(p_low, dam)
            dk += mm(ds, qm)
            att_t.append(mm(v_t[h * HD:(h + 1) * HD], p_low))
            dq_t.append(mm(k_t[h * HD:(h + 1) * HD], ds))
        att_s[:, pl.ds(base, LANES)] = jnp.concatenate(att_t, axis=0).T.astype(jnp.bfloat16)
        dqkv_s[:, pl.ds(base, LANES)] = (
            jnp.concatenate(dq_t, axis=0).T * scaling
        ).astype(jnp.bfloat16)
        dqkv_s[:, pl.ds(width + base, LANES)] = (dk * scaling).astype(jnp.bfloat16)
        dqkv_s[:, pl.ds(2 * width + base, LANES)] = dv.astype(jnp.bfloat16)
        return carry

    lax.fori_loop(0, width // LANES, group, 0)
    att = att_s[...]
    y = x + mm(att, wout_ref[...])
    y_ref[...] = y.reshape(y_ref.shape).astype(jnp.bfloat16)
    d_qkv = dqkv_s[...]
    d_hidden = mm(d_qkv, wqkv_ref[...], NT)
    xhat = xhat_s[...]
    term_gain = jnp.sum(d_hidden * xhat, axis=0, keepdims=True)
    d_normed = d_hidden * gain
    dx = gs_f + inv * (
        d_normed
        - jnp.mean(d_normed, axis=1, keepdims=True)
        - xhat * jnp.mean(d_normed * xhat, axis=1, keepdims=True)
    )
    dx_ref[...] = dx.reshape(dx_ref.shape).astype(jnp.bfloat16)
    here = pl.ds(pl.multiple_of(step * tokens, tokens), tokens)
    hid_all[here, :] = hidden
    att_all[here, :] = att
    gs_all[here, :] = gs
    dqkv_all[here, :] = d_qkv

    @pl.when(step == 0)
    def _():
        gain_s[...] = jnp.zeros_like(gain_s)

    gain_s[...] += term_gain

    @pl.when(step == steps - 1)
    def _():
        gw_ref[:, : 3 * width] = mm(hid_all[...], dqkv_all[...], TN).astype(jnp.bfloat16)
        gw_ref[:, 3 * width:] = mm(att_all[...], gs_all[...], TN).astype(jnp.bfloat16)
        gg_ref[...] = gain_s[...]


def block_pass(x, g, gain, wqkv, wout):
    rows, cols, depth, width = x.shape
    tokens = WR * WA * WZ
    grid_r, grid_a = rows // WR, cols // WA
    number = rows * cols * depth
    field = pl.BlockSpec((WR, WA, depth, width), lambda i: (i // grid_a, i % grid_a, 0, 0))

    def whole(shape):
        return pl.BlockSpec(shape, lambda i: (0,) * len(shape))

    bf, f32 = jnp.bfloat16, jnp.float32
    return pl.pallas_call(
        block_kernel,
        grid=(grid_r * grid_a,),
        in_specs=[field, field, whole((1, width)), whole(wqkv.shape), whole(wout.shape)],
        out_specs=[field, field, whole((width, 4 * width)), whole((1, width))],
        out_shape=[
            jax.ShapeDtypeStruct(x.shape, bf),
            jax.ShapeDtypeStruct(x.shape, bf),
            jax.ShapeDtypeStruct((width, 4 * width), bf),
            jax.ShapeDtypeStruct((1, width), f32),
        ],
        scratch_shapes=[
            pltpu.VMEM((tokens, width), f32),
            pltpu.VMEM((tokens, 3 * width), bf),
            pltpu.VMEM((tokens, width), bf),
            pltpu.VMEM((tokens, width), bf),
            pltpu.VMEM((tokens, 3 * width), bf),
            pltpu.VMEM((number, width), bf),
            pltpu.VMEM((number, width), bf),
            pltpu.VMEM((number, width), bf),
            pltpu.VMEM((number, 3 * width), bf),
            pltpu.VMEM((1, width), f32),
        ],
        compiler_params=pltpu.CompilerParams(vmem_limit_bytes=48 * 1024 * 1024),
        cost_estimate=pl.CostEstimate(
            flops=number * width * width * 24, bytes_accessed=12 * 2 ** 20, transcendentals=0
        ),
        name="block_pass",
    )(x, g, gain, wqkv, wout)


def shifted_2(block, axis, distance):
    devices = range(lax.axis_size(axis))
    route = [((i - distance) % len(devices), i) for i in devices]
    return lax.ppermute(block, axis, route)


def azi_roll(pieces, amount):
    cols_dev = pieces[0].shape[1]
    device_hops = amount // cols_dev
    remainder = amount % cols_dev
    current = pieces
    bit_count = (lax.axis_size("azi") - 1).bit_length()
    for bit_level in range(bit_count):
        hopped = shifted_2((current[0], current[1]), "azi", -(1 << bit_level))
        chosen = device_hops >> bit_level & 1 == 1
        current = (
            jnp.where(chosen, hopped[0], current[0]),
            jnp.where(chosen, hopped[1], current[1]),
        )
    following = shifted_2((current[0], current[1]), "azi", -1)
    return tuple(
        (
            lax.dynamic_slice_in_dim(
                jnp.concatenate([mine, theirs], axis=1), remainder, cols_dev, 1
            )
            for mine, theirs in zip(current, following)
        )
    )


def shift_in(first, second, shift_rad, shift_azi, offset, total_cols):
    rim_rows = WR - 1
    rows_dev, cols_dev, depth, width = first.shape
    below = shifted_2((first[:rim_rows], second[:rim_rows]), "rad", -1)
    extended = (
        jnp.concatenate([first, below[0]], axis=0),
        jnp.concatenate([second, below[1]], axis=0),
    )
    leading = shifted_2((extended[0][:, : WA - 1], extended[1][:, : WA - 1]), "azi", -1)
    rolled = tuple(
        (
            lax.dynamic_slice_in_dim(
                jnp.concatenate([own_part, lead_part], axis=1), shift_azi, cols_dev, 1
            )
            for own_part, lead_part in zip(extended, leading)
        )
    )
    wrapped = azi_roll(below, (offset + shift_azi) % total_cols)
    last_row = lax.axis_index("rad") == lax.axis_size("rad") - 1
    results = []
    for rolled_part, wrapped_part in zip(rolled, wrapped):
        joined = jnp.concatenate(
            [rolled_part[:rows_dev], jnp.where(last_row, wrapped_part, rolled_part[rows_dev:])],
            axis=0,
        )
        results.append(lax.dynamic_slice_in_dim(joined, shift_rad, rows_dev, 0))
    return (results[0], results[1])


def shift_out(first, second, shift_rad, shift_azi, offset, total_cols):
    rim_rows = WR - 1
    rows_dev, cols_dev, depth, width = first.shape
    above = shifted_2((first[rows_dev - rim_rows :], second[rows_dev - rim_rows :]), "rad", 1)
    extended = (
        jnp.concatenate([above[0], first], axis=0),
        jnp.concatenate([above[1], second], axis=0),
    )
    trailing = shifted_2(
        (extended[0][:, cols_dev - (WA - 1) :], extended[1][:, cols_dev - (WA - 1) :]), "azi", 1
    )
    rolled = tuple(
        (
            lax.dynamic_slice_in_dim(
                jnp.concatenate([trail_part, own_part], axis=1), WA - 1 - shift_azi, cols_dev, 1
            )
            for own_part, trail_part in zip(extended, trailing)
        )
    )
    amount = (total_cols - (offset + shift_azi) % total_cols) % total_cols
    wrapped = azi_roll(above, amount)
    first_row = lax.axis_index("rad") == 0
    results = []
    for rolled_part, wrapped_part in zip(rolled, wrapped):
        joined = jnp.concatenate(
            [jnp.where(first_row, wrapped_part, rolled_part[:rim_rows]), rolled_part[rim_rows:]],
            axis=0,
        )
        results.append(lax.dynamic_slice_in_dim(joined, rim_rows - shift_rad, rows_dev, 0))
    return (results[0], results[1])


def on_device(tokens, cotangent, ln_gain, qkv_weight, out_weight, shear_offset, window_shift):
    rows_dev, cols_dev, depth, width = tokens.shape
    assert depth == WZ
    number = rows_dev * cols_dev * depth
    n_rad = lax.axis_size("rad")
    n_azi = lax.axis_size("azi")
    total_cols = cols_dev * n_azi
    shift_rad = window_shift[0]
    shift_azi = window_shift[1]
    offset = shear_offset[0]
    weights = lax.all_gather(
        jnp.concatenate([qkv_weight, out_weight], axis=1), "azi", axis=0, tiled=True
    )
    qkv_full = weights[:, : 3 * width]
    out_full = weights[:, 3 * width :]
    shifted, grad_in = shift_in(tokens, cotangent, shift_rad, shift_azi, offset, total_cols)
    out_shifted, grad_shifted, term, term_gain = block_pass(
        shifted, grad_in, ln_gain.reshape(1, width), qkv_full, out_full
    )
    block_out, grad_tokens = shift_out(
        out_shifted, grad_shifted, shift_rad, shift_azi, offset, total_cols
    )
    share = lax.psum_scatter(term, "azi", scatter_dimension=0, tiled=True)
    share = lax.psum(share, "rad").astype(jnp.float32)
    gain_total = lax.psum(term_gain[0], ("rad", "azi"))
    factor = float(number * n_rad * n_azi) ** (-0.5)
    grad_qkv = share[:, : 3 * width] * factor
    grad_out = share[:, 3 * width :] * factor
    return (block_out, grad_tokens, grad_qkv, grad_out, gain_total * factor)


def solution(mesh):
    in_specs = (
        P("rad", "azi", None, None),
        P("rad", "azi", None, None),
        P(),
        P("azi", None),
        P("azi", None),
        P(),
        P(),
    )
    out_specs = (
        P("rad", "azi", None, None),
        P("rad", "azi", None, None),
        P("azi", None),
        P("azi", None),
        P(),
    )
    return jax.shard_map(
        on_device, mesh=mesh, in_specs=in_specs, out_specs=out_specs, check_vma=False
    )
```

```python
import jax
import jax.numpy as jnp
from jax import lax
from jax.experimental import pallas as pl
from jax.experimental.pallas import tpu as pltpu
from jax.sharding import PartitionSpec as P

HEADS = 16
HD = 32
WR = 4
WA = 8
WZ = 8
LANES = 128
LOG2E = 1.4426950408889634

EPS = 1e-05
NT = (((1,), (1,)), ((), ()))
TN = (((0,), (0,)), ((), ()))


def mm(a, b, dims=(((1,), (0,)), ((), ()))):
    return lax.dot_general(a, b, dims, preferred_element_type=jnp.float32)


def block_kernel(
    info_ref, f_ref, gain_ref, wqkv_ref, wout_ref,
    o_ref, gw_ref, gg_ref,
    x_s, g_s, xhat_s, qkv_s, da_s, att_s, dqkv_s, hid_all, att_all, gs_all, dqkv_all, gain_s,
):
    step = pl.program_id(0)
    steps = pl.num_programs(0)
    _, rows, cols, depth, width = f_ref.shape
    grid_a = cols // WA
    tokens = WR * WA * WZ
    first_row, first_col, wrap_col = info_ref[0], info_ref[1], info_ref[2]
    places = []
    for k in range(WR):
        row = lax.rem(first_row + (step // grid_a) * WR + k, rows)
        start = jnp.where(row < first_row, wrap_col, first_col) + (step % grid_a) * WA
        for m in range(WA):
            places.append((row, lax.rem(start + m, cols)))
    for at, (row, col) in enumerate(places):
        x_s[at * WZ:(at + 1) * WZ, :] = f_ref[0, row, col].astype(jnp.float32)
        g_s[at * WZ:(at + 1) * WZ, :] = f_ref[1, row, col].astype(jnp.float32)
    x = x_s[...]
    gs = g_s[...].astype(jnp.bfloat16)
    gain = gain_ref[...]
    centred = x - jnp.mean(x, axis=1, keepdims=True)
    inv = lax.rsqrt(jnp.mean(centred * centred, axis=1, keepdims=True) + EPS)
    xhat = centred * inv
    xhat_s[...] = xhat
    hidden = (xhat * gain).astype(jnp.bfloat16)
    qkv_s[...] = mm(hidden, wqkv_ref[...]).astype(jnp.bfloat16)
    da_s[...] = mm(gs, wout_ref[...], NT).astype(jnp.bfloat16)
    scaling = HD ** (-0.5)
    lane = lax.broadcasted_iota(jnp.int32, (1, LANES), 1)
    per_group = LANES // HD

    def group(g, carry):
        base = pl.multiple_of(g * LANES, LANES)
        q = qkv_s[:, pl.ds(base, LANES)]
        k = qkv_s[:, pl.ds(width + base, LANES)]
        v = qkv_s[:, pl.ds(2 * width + base, LANES)]
        da = da_s[:, pl.ds(base, LANES)]
        k_t = k.astype(jnp.float32).T.astype(jnp.bfloat16)
        v_t = v.astype(jnp.float32).T.astype(jnp.bfloat16)
        dv = jnp.zeros((tokens, LANES), jnp.float32)
        dk = jnp.zeros((tokens, LANES), jnp.float32)
        att_t, dq_t = [], []
        for h in range(per_group):
            mine = (lane >= h * HD) & (lane < (h + 1) * HD)
            mask = jnp.where(mine, 1.0, 0.0).astype(jnp.bfloat16)
            qm = q * mask
            dam = da * mask
            s = mm(k, qm, NT) * (scaling * LOG2E)
            e = jnp.exp2(s - jnp.max(s, axis=0, keepdims=True))
            p = e * (1.0 / jnp.sum(e, axis=0, keepdims=True))
            p_low = p.astype(jnp.bfloat16)
            dp = mm(v, dam, NT)
            ds = p * (dp - jnp.sum(p * dp, axis=0, keepdims=True))
            ds = ds.astype(jnp.bfloat16)
            dv += mm(p_low, dam)
            dk += mm(ds, qm)
            att_t.append(mm(v_t[h * HD:(h + 1) * HD], p_low))
            dq_t.append(mm(k_t[h * HD:(h + 1) * HD], ds))
        att_s[:, pl.ds(base, LANES)] = jnp.concatenate(att_t, axis=0).T.astype(jnp.bfloat16)
        dqkv_s[:, pl.ds(base, LANES)] = (
            jnp.concatenate(dq_t, axis=0).T * scaling
        ).astype(jnp.bfloat16)
        dqkv_s[:, pl.ds(width + base, LANES)] = (dk * scaling).astype(jnp.bfloat16)
        dqkv_s[:, pl.ds(2 * width + base, LANES)] = dv.astype(jnp.bfloat16)
        return carry

    lax.fori_loop(0, width // LANES, group, 0)
    att = att_s[...]
    d_qkv = dqkv_s[...]
    d_hidden = mm(d_qkv, wqkv_ref[...], NT)
    xhat = xhat_s[...]
    term_gain = jnp.sum(d_hidden * xhat, axis=0, keepdims=True)
    d_normed = d_hidden * gain
    y = x_s[...] + mm(att, wout_ref[...])
    dx = g_s[...] + inv * (
        d_normed
        - jnp.mean(d_normed, axis=1, keepdims=True)
        - xhat * jnp.mean(d_normed * xhat, axis=1, keepdims=True)
    )
    for at, (row, col) in enumerate(places):
        o_ref[0, row, col] = y[at * WZ:(at + 1) * WZ].astype(jnp.bfloat16)
        o_ref[1, row, col] = dx[at * WZ:(at + 1) * WZ].astype(jnp.bfloat16)
    here = pl.ds(pl.multiple_of(step * tokens, tokens), tokens)
    hid_all[here, :] = hidden
    att_all[here, :] = att
    gs_all[here, :] = gs
    dqkv_all[here, :] = d_qkv

    @pl.when(step == 0)
    def _():
        gain_s[...] = jnp.zeros_like(gain_s)

    gain_s[...] += term_gain

    @pl.when(step == steps - 1)
    def _():
        gw_ref[:, : 3 * width] = mm(hid_all[...], dqkv_all[...], TN).astype(jnp.bfloat16)
        gw_ref[:, 3 * width:] = mm(att_all[...], gs_all[...], TN).astype(jnp.bfloat16)
        gg_ref[...] = gain_s[...]


def block_pass(info, fields, gain, wqkv, wout):
    _, rows, cols, depth, width = fields.shape
    tokens = WR * WA * WZ
    number = rows * cols * depth

    def whole(shape):
        return pl.BlockSpec(shape, lambda i, info: (0,) * len(shape))

    bf, f32 = jnp.bfloat16, jnp.float32
    return pl.pallas_call(
        block_kernel,
        grid_spec=pltpu.PrefetchScalarGridSpec(
            num_scalar_prefetch=1,
            grid=(number // tokens,),
            in_specs=[
                whole(fields.shape), whole((1, width)), whole(wqkv.shape), whole(wout.shape)
            ],
            out_specs=[whole(fields.shape), whole((width, 4 * width)), whole((1, width))],
            scratch_shapes=[
                pltpu.VMEM((tokens, width), f32),
                pltpu.VMEM((tokens, width), f32),
                pltpu.VMEM((tokens, width), f32),
                pltpu.VMEM((tokens, 3 * width), bf),
                pltpu.VMEM((tokens, width), bf),
                pltpu.VMEM((tokens, width), bf),
                pltpu.VMEM((tokens, 3 * width), bf),
                pltpu.VMEM((number, width), bf),
                pltpu.VMEM((number, width), bf),
                pltpu.VMEM((number, width), bf),
                pltpu.VMEM((number, 3 * width), bf),
                pltpu.VMEM((1, width), f32),
            ],
        ),
        out_shape=[
            jax.ShapeDtypeStruct(fields.shape, bf),
            jax.ShapeDtypeStruct((width, 4 * width), bf),
            jax.ShapeDtypeStruct((1, width), f32),
        ],
        compiler_params=pltpu.CompilerParams(vmem_limit_bytes=48 * 1024 * 1024),
        cost_estimate=pl.CostEstimate(
            flops=number * width * width * 24, bytes_accessed=12 * 2 ** 20, transcendentals=0
        ),
        name="block_pass",
    )(info, fields, gain, wqkv, wout)


BOTH = ("rad", "azi")


def route(pairs, array, back):
    n_azi = lax.axis_size("azi")
    flat = [(a[0] * n_azi + a[1], b[0] * n_azi + b[1]) for a, b in pairs]
    return lax.ppermute(array, BOTH, [(t, s) if back else (s, t) for s, t in flat])


def wrapped_strip(strip, amount, back):
    n_rad, n_azi = lax.axis_size("rad"), lax.axis_size("azi")
    cols = strip.shape[2]
    parts = 4
    while parts > 1 and (cols % parts or parts * n_azi > 64):
        parts //= 2
    piece = cols // parts
    rem = amount % cols

    def branch(hops, cut):
        def send(strip):
            near = [((0, (j + hops) % n_azi), (n_rad - 1, j)) for j in range(n_azi)]
            far = [((0, (j + hops + 1) % n_azi), (n_rad - 1, j)) for j in range(n_azi)]
            upper = route(near, strip[:, :, cut * piece:], back)
            lower = route(far, strip[:, :, : (cut + 1) * piece], back)
            at = cut * piece + jnp.arange(piece, dtype=jnp.int32).reshape(1, 1, piece, 1, 1)
            mixed = jnp.where(at >= rem, upper[:, :, :piece], lower[:, :, cut * piece:])
            return jnp.concatenate(
                [lower[:, :, : cut * piece], mixed, upper[:, :, piece:]], axis=2
            )

        return send

    branches = [branch(n // parts, n % parts) for n in range(n_azi * parts)]
    return lax.switch(amount // piece, branches, strip)


def exchange(strip, side, corner, amount, back):
    n_rad, n_azi = lax.axis_size("rad"), lax.axis_size("azi")
    near = [((i + 1, j), (i, j)) for i in range(n_rad - 1) for j in range(n_azi)]
    diagonal = [
        ((i + 1, (j + 1) % n_azi), (i, j)) for i in range(n_rad - 1) for j in range(n_azi)
    ]
    beside = [((i, (j + 1) % n_azi), (i, j)) for i in range(n_rad) for j in range(n_azi)]
    got_strip = route(near, strip, back)
    got_side = route(beside, side, back)
    got_corner = route(diagonal, corner, back)
    got_wrapped = wrapped_strip(strip, amount, back)
    return got_strip, got_side, got_corner, got_wrapped


def merge(fields, got, shift_rad, shift_azi, outer):
    strip, side, corner, wrapped = got
    rim_rows, rim_cols = WR - 1, WA - 1
    row = jnp.arange(rim_rows, dtype=jnp.int32).reshape(1, rim_rows, 1, 1, 1)
    col = jnp.arange(rim_cols, dtype=jnp.int32).reshape(1, 1, rim_cols, 1, 1)
    fields = jnp.concatenate(
        [jnp.where(col < shift_azi, side, fields[:, :, :rim_cols]), fields[:, :, rim_cols:]],
        axis=2,
    )
    strip = jnp.concatenate(
        [jnp.where(col < shift_azi, corner, strip[:, :, :rim_cols]), strip[:, :, rim_cols:]],
        axis=2,
    )
    strip = jnp.where(outer, wrapped, strip)
    return jnp.concatenate(
        [jnp.where(row < shift_rad, strip, fields[:, :rim_rows]), fields[:, rim_rows:]], axis=1
    )


def scatter_sum(pieces, count, index, shift):
    total = lax.dynamic_index_in_dim(pieces, index, 0, keepdims=False).astype(jnp.float32)
    for d in range(1, count):
        out = lax.dynamic_index_in_dim(pieces, (index + d) % count, 0, keepdims=False)
        total = total + shift(out, d).astype(jnp.float32)
    return total


def sum_gradients(term, gain):
    n_rad, n_azi = lax.axis_size("rad"), lax.axis_size("azi")
    i, j = lax.axis_index("rad"), lax.axis_index("azi")
    bf = jnp.bfloat16
    cores = 2 if n_azi % 2 == 0 else 1
    n_z = n_azi // cores
    z, core = j // cores, j % cores
    rows = term.shape[0] // n_azi
    columns = term.shape[1]

    def over_core(array, d):
        return lax.ppermute(
            array, "azi", [(n, n - n % cores + (n + d) % cores) for n in range(n_azi)]
        )

    def over_z(array, d):
        return lax.ppermute(array, "azi", [(n, (n + d * cores) % n_azi) for n in range(n_azi)])

    def over_rad(array, d):
        return lax.ppermute(array, "rad", [(n, (n + d) % n_rad) for n in range(n_rad)])

    def everyone(array, count, shift):
        total = array
        for d in range(1, count):
            total = total + shift(array, d)
        return total

    gain = everyone(gain, cores, over_core)
    gain = everyone(gain, n_rad, over_rad)
    gain = everyone(gain, n_z, over_z)
    pieces = term.reshape(n_z, cores, rows, columns).swapaxes(0, 1)
    pieces = scatter_sum(pieces, cores, core, over_core).astype(bf)
    pieces = pieces.reshape(n_z, n_rad, rows // n_rad, columns).swapaxes(0, 1)
    pieces = scatter_sum(pieces, n_rad, i, over_rad).astype(bf)
    mine = scatter_sum(pieces, n_z, z, over_z).astype(bf)
    ordered = [mine] + [over_rad(mine, n_rad - d) for d in range(1, n_rad)]
    ordered = jnp.stack(ordered)
    share = jnp.roll(ordered, i, axis=0).reshape(rows, columns)
    return share.astype(jnp.float32), gain


def on_device(tokens, cotangent, ln_gain, qkv_weight, out_weight, shear_offset, window_shift):
    rows_dev, cols_dev, depth, width = tokens.shape
    assert depth == WZ
    number = rows_dev * cols_dev * depth
    n_rad = lax.axis_size("rad")
    n_azi = lax.axis_size("azi")
    total_cols = cols_dev * n_azi
    shift_rad = window_shift[0]
    shift_azi = window_shift[1]
    offset = shear_offset[0]
    rim_rows, rim_cols = WR - 1, WA - 1
    amount = (offset + shift_azi) % total_cols
    weights = lax.all_gather(
        jnp.concatenate([qkv_weight, out_weight], axis=1), "azi", axis=0, tiled=True
    )
    qkv_full = weights[:, : 3 * width]
    out_full = weights[:, 3 * width :]

    def pieces(both):
        return both[:, :rim_rows], both[:, :, :rim_cols], both[:, :rim_rows, :rim_cols]

    own = jnp.stack([tokens, cotangent])
    last = lax.axis_index("rad") == n_rad - 1
    got = exchange(*pieces(own), amount, False)
    fields = merge(own, got, shift_rad, shift_azi, last)
    info = jnp.stack(
        [shift_rad, shift_azi, jnp.where(last, amount % cols_dev, shift_azi)]
    ).astype(jnp.int32)
    result, term, gain = block_pass(info, fields, ln_gain.reshape(1, width), qkv_full, out_full)
    got = exchange(*pieces(result), amount, True)
    result = merge(result, got, shift_rad, shift_azi, lax.axis_index("rad") == 0)
    share, gain = sum_gradients(term, gain[0])
    factor = float(number * n_rad * n_azi) ** (-0.5)
    grad_qkv = share[:, : 3 * width] * factor
    grad_out = share[:, 3 * width :] * factor
    return (result[0], result[1], grad_qkv, grad_out, gain * factor)


def solution(mesh):
    in_specs = (
        P("rad", "azi", None, None),
        P("rad", "azi", None, None),
        P(),
        P("azi", None),
        P("azi", None),
        P(),
        P(),
    )
    out_specs = (
        P("rad", "azi", None, None),
        P("rad", "azi", None, None),
        P("azi", None),
        P("azi", None),
        P(),
    )
    return jax.shard_map(
        on_device, mesh=mesh, in_specs=in_specs, out_specs=out_specs, check_vma=False
    )
```

```python
import jax
import jax.numpy as jnp
from jax import lax
from jax.experimental import pallas as pl
from jax.experimental.pallas import tpu as pltpu
from jax.sharding import PartitionSpec as P

HEADS = 16
HD = 32
WR = 4
WA = 8
WZ = 8
LANES = 128
LOG2E = 1.4426950408889634

EPS = 1e-05
NT = (((1,), (1,)), ((), ()))
TN = (((0,), (0,)), ((), ()))


def mm(a, b, dims=(((1,), (0,)), ((), ()))):
    return lax.dot_general(a, b, dims, preferred_element_type=jnp.float32)


def block_kernel(
    info_ref, x_ref, g_ref, side_ref, main_ref, next_ref, gain_ref, w_ref,
    y_ref, dx_ref, strip_ref, rim_ref, gw_ref, gg_ref,
    f_s, wqkv_s, wout_s,
    x_s, g_s, xhat_s, qkv_s, da_s, att_s, dqkv_s, hid_all, att_all, gs_all, dqkv_all, gain_s,
):
    step = pl.program_id(0)
    steps = pl.num_programs(0)
    rows, cols, depth, width = x_ref.shape
    rim_rows, rim_cols = strip_ref.shape[1], rim_ref.shape[2]
    grid_a = cols // WA
    tokens = WR * WA * WZ
    first_row, first_col, wrap_col = info_ref[0], info_ref[1], info_ref[2]
    placed = len(w_ref.shape) == 4

    @pl.when(step == 0)
    def _():
        f_s[0] = x_ref[...]
        f_s[1] = g_ref[...]

        def put_strip(n, carry):
            row, col = n // cols, lax.rem(n, cols)
            for f in range(2):
                f_s[f, row, col] = jnp.where(
                    col < wrap_col, next_ref[f, row, col], main_ref[f, row, col]
                )
            return carry

        def put_side(col, carry):
            def put(row, carry):
                for f in range(2):
                    f_s[f, row, col] = side_ref[f, row, col]
                return carry

            return lax.fori_loop(first_row, rows, put, carry)

        lax.fori_loop(0, first_row * cols, put_strip, 0)
        lax.fori_loop(0, first_col, put_side, 0)
        if placed:
            n_rad, n_azi, part, _ = w_ref.shape
            for j in range(n_azi):
                for i in range(n_rad):
                    at = (j * n_rad + i) * part
                    wqkv_s[at:at + part, :] = w_ref[i, j, :, : 3 * width]
                    wout_s[at:at + part, :] = w_ref[i, j, :, 3 * width:]
        else:
            wqkv_s[...] = w_ref[:, : 3 * width]
            wout_s[...] = w_ref[:, 3 * width:]

    places = []
    for k in range(WR):
        row = lax.rem(first_row + (step // grid_a) * WR + k, rows)
        start = jnp.where(row < first_row, wrap_col, first_col) + (step % grid_a) * WA
        for m in range(WA):
            places.append((row, lax.rem(start + m, cols)))
    for at, (row, col) in enumerate(places):
        x_s[at * WZ:(at + 1) * WZ, :] = f_s[0, row, col].astype(jnp.float32)
        g_s[at * WZ:(at + 1) * WZ, :] = f_s[1, row, col].astype(jnp.float32)
    x = x_s[...]
    gs = g_s[...].astype(jnp.bfloat16)
    gain = gain_ref[...]
    centred = x - jnp.mean(x, axis=1, keepdims=True)
    inv = lax.rsqrt(jnp.mean(centred * centred, axis=1, keepdims=True) + EPS)
    xhat = centred * inv
    xhat_s[...] = xhat
    hidden = (xhat * gain).astype(jnp.bfloat16)
    qkv_s[...] = mm(hidden, wqkv_s[...]).astype(jnp.bfloat16)
    da_s[...] = mm(gs, wout_s[...], NT).astype(jnp.bfloat16)
    scaling = HD ** (-0.5)
    lane = lax.broadcasted_iota(jnp.int32, (1, LANES), 1)
    per_group = LANES // HD

    def group(g, carry):
        base = pl.multiple_of(g * LANES, LANES)
        q = qkv_s[:, pl.ds(base, LANES)]
        k = qkv_s[:, pl.ds(width + base, LANES)]
        v = qkv_s[:, pl.ds(2 * width + base, LANES)]
        da = da_s[:, pl.ds(base, LANES)]
        k_t = k.astype(jnp.float32).T.astype(jnp.bfloat16)
        v_t = v.astype(jnp.float32).T.astype(jnp.bfloat16)
        dv = jnp.zeros((tokens, LANES), jnp.float32)
        dk = jnp.zeros((tokens, LANES), jnp.float32)
        att_t, dq_t = [], []
        for h in range(per_group):
            mine = (lane >= h * HD) & (lane < (h + 1) * HD)
            mask = jnp.where(mine, 1.0, 0.0).astype(jnp.bfloat16)
            qm = q * mask
            dam = da * mask
            s = mm(k, qm, NT) * (scaling * LOG2E)
            e = jnp.exp2(s - jnp.max(s, axis=0, keepdims=True))
            p = e * (1.0 / jnp.sum(e, axis=0, keepdims=True))
            p_low = p.astype(jnp.bfloat16)
            dp = mm(v, dam, NT)
            ds = p * (dp - jnp.sum(p * dp, axis=0, keepdims=True))
            ds = ds.astype(jnp.bfloat16)
            dv += mm(p_low, dam)
            dk += mm(ds, qm)
            att_t.append(mm(v_t[h * HD:(h + 1) * HD], p_low))
            dq_t.append(mm(k_t[h * HD:(h + 1) * HD], ds))
        att_s[:, pl.ds(base, LANES)] = jnp.concatenate(att_t, axis=0).T.astype(jnp.bfloat16)
        dqkv_s[:, pl.ds(base, LANES)] = (
            jnp.concatenate(dq_t, axis=0).T * scaling
        ).astype(jnp.bfloat16)
        dqkv_s[:, pl.ds(width + base, LANES)] = (dk * scaling).astype(jnp.bfloat16)
        dqkv_s[:, pl.ds(2 * width + base, LANES)] = dv.astype(jnp.bfloat16)
        return carry

    lax.fori_loop(0, width // LANES, group, 0)
    att = att_s[...]
    d_qkv = dqkv_s[...]
    d_hidden = mm(d_qkv, wqkv_s[...], NT)
    xhat = xhat_s[...]
    term_gain = jnp.sum(d_hidden * xhat, axis=0, keepdims=True)
    d_normed = d_hidden * gain
    y = x_s[...] + mm(att, wout_s[...])
    dx = g_s[...] + inv * (
        d_normed
        - jnp.mean(d_normed, axis=1, keepdims=True)
        - xhat * jnp.mean(d_normed * xhat, axis=1, keepdims=True)
    )
    for at, (row, col) in enumerate(places):
        y_ref[row, col] = y[at * WZ:(at + 1) * WZ].astype(jnp.bfloat16)
        dx_ref[row, col] = dx[at * WZ:(at + 1) * WZ].astype(jnp.bfloat16)
    here = pl.ds(pl.multiple_of(step * tokens, tokens), tokens)
    hid_all[here, :] = hidden
    att_all[here, :] = att
    gs_all[here, :] = gs
    dqkv_all[here, :] = d_qkv

    @pl.when(step == 0)
    def _():
        gain_s[...] = jnp.zeros_like(gain_s)

    gain_s[...] += term_gain

    @pl.when(step == steps - 1)
    def _():
        for f, ref in enumerate((y_ref, dx_ref)):
            strip_ref[f] = ref[:rim_rows]
            rim_ref[f] = ref[:, :rim_cols]
        g_qkv = mm(hid_all[...], dqkv_all[...], TN).astype(jnp.bfloat16)
        g_out = mm(att_all[...], gs_all[...], TN).astype(jnp.bfloat16)
        gg_ref[...] = gain_s[...]
        if placed:
            n_rad, n_azi, part, _ = w_ref.shape
            for j in range(n_azi):
                for i in range(n_rad):
                    at = (j * n_rad + i) * part
                    gw_ref[i, j, :, : 3 * width] = g_qkv[at:at + part]
                    gw_ref[i, j, :, 3 * width:] = g_out[at:at + part]
        else:
            gw_ref[:, : 3 * width] = g_qkv
            gw_ref[:, 3 * width:] = g_out


def block_pass(info, x, g, side, main, following, gain, weights):
    rows, cols, depth, width = x.shape
    tokens = WR * WA * WZ
    number = rows * cols * depth

    def whole(shape):
        return pl.BlockSpec(shape, lambda i, info: (0,) * len(shape))

    bf, f32 = jnp.bfloat16, jnp.float32
    strip_shape = (2, WR - 1, cols, depth, width)
    rim_shape = (2, rows, WA - 1, depth, width)
    ins = (x, g, side, main, following, gain, weights)
    outs = [
        (x.shape, bf), (x.shape, bf), (strip_shape, bf), (rim_shape, bf),
        (weights.shape, bf), ((1, width), f32),
    ]
    return pl.pallas_call(
        block_kernel,
        grid_spec=pltpu.PrefetchScalarGridSpec(
            num_scalar_prefetch=1,
            grid=(number // tokens,),
            in_specs=[whole(array.shape) for array in ins],
            out_specs=[whole(shape) for shape, _ in outs],
            scratch_shapes=[
                pltpu.VMEM((2,) + x.shape, bf),
                pltpu.VMEM((width, 3 * width), bf),
                pltpu.VMEM((width, width), bf),
                pltpu.VMEM((tokens, width), f32),
                pltpu.VMEM((tokens, width), f32),
                pltpu.VMEM((tokens, width), f32),
                pltpu.VMEM((tokens, 3 * width), bf),
                pltpu.VMEM((tokens, width), bf),
                pltpu.VMEM((tokens, width), bf),
                pltpu.VMEM((tokens, 3 * width), bf),
                pltpu.VMEM((number, width), bf),
                pltpu.VMEM((number, width), bf),
                pltpu.VMEM((number, width), bf),
                pltpu.VMEM((number, 3 * width), bf),
                pltpu.VMEM((1, width), f32),
            ],
        ),
        out_shape=[jax.ShapeDtypeStruct(shape, kind) for shape, kind in outs],
        compiler_params=pltpu.CompilerParams(vmem_limit_bytes=56 * 1024 * 1024),
        cost_estimate=pl.CostEstimate(
            flops=number * width * width * 24, bytes_accessed=16 * 2 ** 20, transcendentals=0
        ),
        name="block_pass",
    )(info, *ins)


BOTH = ("rad", "azi")


def route(pairs, array, back):
    n_azi = lax.axis_size("azi")
    flat = [(a[0] * n_azi + a[1], b[0] * n_azi + b[1]) for a, b in pairs]
    return lax.ppermute(array, BOTH, [(t, s) if back else (s, t) for s, t in flat])


def strip_routes(hops, back):
    n_rad, n_azi = lax.axis_size("rad"), lax.axis_size("azi")
    azi = range(n_azi)
    near = [((i + 1, j), (i, j)) for i in range(n_rad - 1) for j in azi]
    wrap = [((0, (j + hops) % n_azi), (n_rad - 1, j)) for j in azi]
    return near, wrap


def beside(array, back):
    n_rad, n_azi = lax.axis_size("rad"), lax.axis_size("azi")
    pairs = [((i, (j + 1) % n_azi), (i, j)) for i in range(n_rad) for j in range(n_azi)]
    return route(pairs, array, back)


def over_switch(body, arrays, shift_rad, hops):
    n_azi = lax.axis_size("azi")
    branches = [
        body(1 + n // n_azi, n % n_azi) for n in range((WR - 1) * n_azi)
    ]
    return lax.switch((shift_rad - 1) * n_azi + hops, branches, *arrays)


def full_rows(array):
    missing = WR - 1 - array.shape[1]
    return jnp.pad(array, ((0, 0), (0, missing), (0, 0), (0, 0), (0, 0)))


def fetch_strip(strip, shift_rad, hops):
    def body(rows, hops):
        def send(strip):
            sent = strip[:, :rows]
            near, wrap = strip_routes(hops, False)
            main = route(near + wrap, sent, False)
            following = beside(main, False)
            return full_rows(main), full_rows(following)

        return send

    return over_switch(body, (strip,), shift_rad, hops)


def return_strip(strip, wrap_col, shift_rad, hops):
    cols = strip.shape[2]
    col = jnp.arange(cols, dtype=jnp.int32).reshape(1, 1, cols, 1, 1)

    def body(rows, hops):
        def send(strip, wrap_col):
            own = strip[:, :rows]
            main = jnp.where(col < wrap_col, beside(own, True), own)
            near, wrap = strip_routes(hops, True)
            return full_rows(route(near + wrap, main, True))

        return send

    return over_switch(body, (strip, wrap_col), shift_rad, hops)


def on_device(tokens, cotangent, ln_gain, qkv_weight, out_weight, shear_offset, window_shift):
    rows_dev, cols_dev, depth, width = tokens.shape
    assert depth == WZ
    number = rows_dev * cols_dev * depth
    n_rad = lax.axis_size("rad")
    n_azi = lax.axis_size("azi")
    at_rad = lax.axis_index("rad")
    total_cols = cols_dev * n_azi
    rim_rows, rim_cols = WR - 1, WA - 1
    shift_rad = window_shift[0]
    shift_azi = window_shift[1]
    offset = shear_offset[0]
    amount = (offset + shift_azi) % total_cols
    hops = amount // cols_dev
    part_rows = qkv_weight.shape[0] // n_rad
    first = at_rad * part_rows
    part = jnp.concatenate(
        [
            lax.dynamic_slice_in_dim(qkv_weight, first, part_rows, 0),
            lax.dynamic_slice_in_dim(out_weight, first, part_rows, 0),
        ],
        axis=1,
    )
    weights = lax.all_gather(part, BOTH, axis=0)
    weights = weights.reshape(n_rad, n_azi, part_rows, 4 * width)
    placed = part_rows % 16 == 0
    if not placed:
        weights = weights.swapaxes(0, 1).reshape(width, 4 * width)
    side = beside(jnp.stack([tokens[:, :rim_cols], cotangent[:, :rim_cols]]), False)
    strip = jnp.stack([tokens[:rim_rows], cotangent[:rim_rows]])
    main, following = fetch_strip(strip, shift_rad, hops)
    last = at_rad == n_rad - 1
    wrap_col = jnp.where(last, amount % cols_dev, shift_azi)
    info = jnp.stack([shift_rad, shift_azi, wrap_col]).astype(jnp.int32)
    y, dx, strip, side, term, gain = block_pass(
        info, tokens, cotangent, side, main, following, ln_gain.reshape(1, width), weights
    )
    if not placed:
        term = term.reshape(n_azi, n_rad, part_rows, 4 * width).swapaxes(0, 1)
    term = term.reshape(n_rad * n_azi, part_rows, 4 * width)
    share = lax.psum_scatter(term, BOTH, scatter_dimension=0, tiled=False)
    gain = jnp.sum(lax.all_gather(gain[0], BOTH, axis=0), axis=0)
    side = beside(side, True)
    strip = return_strip(strip, wrap_col, shift_rad, hops)
    col = jnp.arange(rim_cols, dtype=jnp.int32).reshape(1, rim_cols, 1, 1)
    row = jnp.arange(rim_rows, dtype=jnp.int32).reshape(rim_rows, 1, 1, 1)

    def finish(array, strip, side):
        edge = jnp.where(col < shift_azi, side, array[:, :rim_cols])
        array = lax.dynamic_update_slice(array, edge, (0, 0, 0, 0))
        edge = jnp.where(row < shift_rad, strip, array[:rim_rows])
        return lax.dynamic_update_slice(array, edge, (0, 0, 0, 0))

    block_out = finish(y, strip[0], side[0])
    grad_tokens = finish(dx, strip[1], side[1])
    share = lax.all_gather(share, "rad", axis=0, tiled=True).astype(jnp.float32)
    factor = float(number * n_rad * n_azi) ** (-0.5)
    grad_qkv = share[:, : 3 * width] * factor
    grad_out = share[:, 3 * width :] * factor
    return (block_out, grad_tokens, grad_qkv, grad_out, gain * factor)


def solution(mesh):
    in_specs = (
        P("rad", "azi", None, None),
        P("rad", "azi", None, None),
        P(),
        P("azi", None),
        P("azi", None),
        P(),
        P(),
    )
    out_specs = (
        P("rad", "azi", None, None),
        P("rad", "azi", None, None),
        P("azi", None),
        P("azi", None),
        P(),
    )
    return jax.shard_map(
        on_device, mesh=mesh, in_specs=in_specs, out_specs=out_specs, check_vma=False
    )
```

```python
import jax
import jax.numpy as jnp
from jax import lax
from jax.experimental import pallas as pl
from jax.experimental.pallas import tpu as pltpu
from jax.sharding import PartitionSpec as P

HEADS = 16
HD = 32
WR = 4
WA = 8
WZ = 8
LANES = 128
LOG2E = 1.4426950408889634

EPS = 1e-05
NT = (((1,), (1,)), ((), ()))
TN = (((0,), (0,)), ((), ()))


def mm(a, b, dims=(((1,), (0,)), ((), ()))):
    return lax.dot_general(a, b, dims, preferred_element_type=jnp.float32)


def block_kernel(
    info_ref, x_ref, g_ref, side_ref, main_ref, next_ref, gain_ref, w_ref,
    y_ref, dx_ref, strip_ref, rim_ref, gw_ref, gg_ref,
    f_s,
    x_s, g_s, xhat_s, qkv_s, da_s, att_s, dqkv_s, hid_all, att_all, gs_all, dqkv_all, gain_s,
):
    step = pl.program_id(0)
    steps = pl.num_programs(0)
    rows, cols, depth, width = x_ref.shape
    rim_rows, rim_cols = strip_ref.shape[1], rim_ref.shape[2]
    grid_a = cols // WA
    tokens = WR * WA * WZ
    first_row, first_col, wrap_col = info_ref[0], info_ref[1], info_ref[2]

    @pl.when(step == 0)
    def _():
        f_s[0] = x_ref[...]
        f_s[1] = g_ref[...]

        def put_strip(n, carry):
            row, col = n // cols, lax.rem(n, cols)
            for f in range(2):
                f_s[f, row, col] = jnp.where(
                    col < wrap_col, next_ref[f, row, col], main_ref[f, row, col]
                )
            return carry

        def put_side(col, carry):
            def put(row, carry):
                for f in range(2):
                    f_s[f, row, col] = side_ref[f, row, col]
                return carry

            return lax.fori_loop(first_row, rows, put, carry)

        lax.fori_loop(0, first_row * cols, put_strip, 0)
        lax.fori_loop(0, first_col, put_side, 0)

    places = []
    for k in range(WR):
        row = lax.rem(first_row + (step // grid_a) * WR + k, rows)
        start = jnp.where(row < first_row, wrap_col, first_col) + (step % grid_a) * WA
        for m in range(WA):
            places.append((row, lax.rem(start + m, cols)))
    for at, (row, col) in enumerate(places):
        x_s[at * WZ:(at + 1) * WZ, :] = f_s[0, row, col].astype(jnp.float32)
        g_s[at * WZ:(at + 1) * WZ, :] = f_s[1, row, col].astype(jnp.float32)
    x = x_s[...]
    gs = g_s[...].astype(jnp.bfloat16)
    gain = gain_ref[...]
    centred = x - jnp.mean(x, axis=1, keepdims=True)
    inv = lax.rsqrt(jnp.mean(centred * centred, axis=1, keepdims=True) + EPS)
    xhat = centred * inv
    xhat_s[...] = xhat
    hidden = (xhat * gain).astype(jnp.bfloat16)
    qkv_s[...] = mm(hidden, w_ref[:, : 3 * width]).astype(jnp.bfloat16)
    da_s[...] = mm(gs, w_ref[:, 3 * width:], NT).astype(jnp.bfloat16)
    scaling = HD ** (-0.5)
    lane = lax.broadcasted_iota(jnp.int32, (1, LANES), 1)
    per_group = LANES // HD

    def group(g, carry):
        base = pl.multiple_of(g * LANES, LANES)
        q = qkv_s[:, pl.ds(base, LANES)]
        k = qkv_s[:, pl.ds(width + base, LANES)]
        v = qkv_s[:, pl.ds(2 * width + base, LANES)]
        da = da_s[:, pl.ds(base, LANES)]
        k_t = k.astype(jnp.float32).T.astype(jnp.bfloat16)
        v_t = v.astype(jnp.float32).T.astype(jnp.bfloat16)
        dv = jnp.zeros((tokens, LANES), jnp.float32)
        dk = jnp.zeros((tokens, LANES), jnp.float32)
        att_t, dq_t = [], []
        for h in range(per_group):
            mine = (lane >= h * HD) & (lane < (h + 1) * HD)
            mask = jnp.where(mine, 1.0, 0.0).astype(jnp.bfloat16)
            qm = q * mask
            dam = da * mask
            s = mm(k, qm, NT) * (scaling * LOG2E)
            e = jnp.exp2(s - jnp.max(s, axis=0, keepdims=True))
            p = e * (1.0 / jnp.sum(e, axis=0, keepdims=True))
            p_low = p.astype(jnp.bfloat16)
            dp = mm(v, dam, NT)
            ds = p * (dp - jnp.sum(p * dp, axis=0, keepdims=True))
            ds = ds.astype(jnp.bfloat16)
            dv += mm(p_low, dam)
            dk += mm(ds, qm)
            att_t.append(mm(v_t[h * HD:(h + 1) * HD], p_low))
            dq_t.append(mm(k_t[h * HD:(h + 1) * HD], ds))
        att_s[:, pl.ds(base, LANES)] = jnp.concatenate(att_t, axis=0).T.astype(jnp.bfloat16)
        dqkv_s[:, pl.ds(base, LANES)] = (
            jnp.concatenate(dq_t, axis=0).T * scaling
        ).astype(jnp.bfloat16)
        dqkv_s[:, pl.ds(width + base, LANES)] = (dk * scaling).astype(jnp.bfloat16)
        dqkv_s[:, pl.ds(2 * width + base, LANES)] = dv.astype(jnp.bfloat16)
        return carry

    lax.fori_loop(0, width // LANES, group, 0)
    att = att_s[...]
    d_qkv = dqkv_s[...]
    d_hidden = mm(d_qkv, w_ref[:, : 3 * width], NT)
    xhat = xhat_s[...]
    term_gain = jnp.sum(d_hidden * xhat, axis=0, keepdims=True)
    d_normed = d_hidden * gain
    y = x_s[...] + mm(att, w_ref[:, 3 * width:])
    dx = g_s[...] + inv * (
        d_normed
        - jnp.mean(d_normed, axis=1, keepdims=True)
        - xhat * jnp.mean(d_normed * xhat, axis=1, keepdims=True)
    )
    for at, (row, col) in enumerate(places):
        y_ref[row, col] = y[at * WZ:(at + 1) * WZ].astype(jnp.bfloat16)
        dx_ref[row, col] = dx[at * WZ:(at + 1) * WZ].astype(jnp.bfloat16)
    here = pl.ds(pl.multiple_of(step * tokens, tokens), tokens)
    hid_all[here, :] = hidden
    att_all[here, :] = att
    gs_all[here, :] = gs
    dqkv_all[here, :] = d_qkv

    @pl.when(step == 0)
    def _():
        gain_s[...] = jnp.zeros_like(gain_s)

    gain_s[...] += term_gain

    @pl.when(step == steps - 1)
    def _():
        for f, ref in enumerate((y_ref, dx_ref)):
            strip_ref[f] = ref[:rim_rows]
            rim_ref[f] = ref[:, :rim_cols]
        g_qkv = mm(hid_all[...], dqkv_all[...], TN).astype(jnp.bfloat16)
        g_out = mm(att_all[...], gs_all[...], TN).astype(jnp.bfloat16)
        gg_ref[...] = gain_s[...]
        if len(gw_ref.shape) == 2:
            gw_ref[:, : 3 * width] = g_qkv
            gw_ref[:, 3 * width:] = g_out
        else:
            cores, n_rad, n_z, part, _ = gw_ref.shape
            extra = jnp.concatenate(
                [gain_s[:, n * LANES:(n + 1) * LANES] for n in range(width // LANES)]
                + [jnp.zeros((part - width // LANES, LANES), jnp.float32)],
                axis=0,
            ).astype(jnp.bfloat16)
            for n in range(cores * n_rad * n_z):
                z, core, i = n // n_rad // cores, n // n_rad % cores, n % n_rad
                here = gw_ref.at[core, i, z]
                here[:, : 3 * width] = g_qkv[n * part:(n + 1) * part]
                here[:, 3 * width: 4 * width] = g_out[n * part:(n + 1) * part]
                here[:, 4 * width:] = extra


def block_pass(info, x, g, side, main, following, gain, weights, term_shape):
    rows, cols, depth, width = x.shape
    tokens = WR * WA * WZ
    number = rows * cols * depth

    def whole(shape):
        return pl.BlockSpec(shape, lambda i, info: (0,) * len(shape))

    bf, f32 = jnp.bfloat16, jnp.float32
    strip_shape = (2, WR - 1, cols, depth, width)
    rim_shape = (2, rows, WA - 1, depth, width)
    ins = (x, g, side, main, following, gain, weights)
    outs = [
        (x.shape, bf), (x.shape, bf), (strip_shape, bf), (rim_shape, bf),
        (term_shape, bf), ((1, width), f32),
    ]
    return pl.pallas_call(
        block_kernel,
        grid_spec=pltpu.PrefetchScalarGridSpec(
            num_scalar_prefetch=1,
            grid=(number // tokens,),
            in_specs=[whole(array.shape) for array in ins],
            out_specs=[whole(shape) for shape, _ in outs],
            scratch_shapes=[
                pltpu.VMEM((2,) + x.shape, bf),
                pltpu.VMEM((tokens, width), f32),
                pltpu.VMEM((tokens, width), f32),
                pltpu.VMEM((tokens, width), f32),
                pltpu.VMEM((tokens, 3 * width), bf),
                pltpu.VMEM((tokens, width), bf),
                pltpu.VMEM((tokens, width), bf),
                pltpu.VMEM((tokens, 3 * width), bf),
                pltpu.VMEM((number, width), bf),
                pltpu.VMEM((number, width), bf),
                pltpu.VMEM((number, width), bf),
                pltpu.VMEM((number, 3 * width), bf),
                pltpu.VMEM((1, width), f32),
            ],
        ),
        out_shape=[jax.ShapeDtypeStruct(shape, kind) for shape, kind in outs],
        compiler_params=pltpu.CompilerParams(vmem_limit_bytes=56 * 1024 * 1024),
        cost_estimate=pl.CostEstimate(
            flops=number * width * width * 24, bytes_accessed=16 * 2 ** 20, transcendentals=0
        ),
        name="block_pass",
    )(info, *ins)


BOTH = ("rad", "azi")


def route(pairs, array, back):
    n_azi = lax.axis_size("azi")
    flat = [(a[0] * n_azi + a[1], b[0] * n_azi + b[1]) for a, b in pairs]
    return lax.ppermute(array, BOTH, [(t, s) if back else (s, t) for s, t in flat])


def strip_routes(hops, back):
    n_rad, n_azi = lax.axis_size("rad"), lax.axis_size("azi")
    azi = range(n_azi)
    near = [((i + 1, j), (i, j)) for i in range(n_rad - 1) for j in azi]
    wrap = [((0, (j + hops) % n_azi), (n_rad - 1, j)) for j in azi]
    return near, wrap


def beside(array, back):
    n_rad, n_azi = lax.axis_size("rad"), lax.axis_size("azi")
    pairs = [((i, (j + 1) % n_azi), (i, j)) for i in range(n_rad) for j in range(n_azi)]
    return route(pairs, array, back)


def over_switch(body, arrays, shift_rad, hops):
    n_azi = lax.axis_size("azi")
    sizes = range(1, WR) if n_azi <= 16 else [WR - 1]
    branches = [body(rows, n) for rows in sizes for n in range(n_azi)]
    index = (shift_rad - 1) * n_azi + hops if len(sizes) > 1 else hops
    return lax.switch(index, branches, *arrays)


def full_rows(array):
    missing = WR - 1 - array.shape[1]
    return jnp.pad(array, ((0, 0), (0, missing), (0, 0), (0, 0), (0, 0)))


def fetch_strip(strip, shift_rad, hops):
    def body(rows, hops):
        def send(strip):
            sent = strip[:, :rows]
            near, wrap = strip_routes(hops, False)
            main = route(near + wrap, sent, False)
            following = beside(main, False)
            return full_rows(main), full_rows(following)

        return send

    return over_switch(body, (strip,), shift_rad, hops)


def permuted(array, axis, target):
    count = lax.axis_size(axis)
    return lax.ppermute(array, axis, [(n, target(n)) for n in range(count)])


def scatter_sum(pieces, index, send):
    count = pieces.shape[0]
    if count > 4 and count % 2 == 0:
        half = count // 2
        halves = pieces.reshape((2, half) + pieces.shape[1:])
        upper = index // half
        kept = lax.dynamic_index_in_dim(halves, upper, 0, keepdims=False)
        given = lax.dynamic_index_in_dim(halves, 1 - upper, 0, keepdims=False)
        got = send(given, lambda n: (n + half) % count)
        kept = (kept.astype(jnp.float32) + got.astype(jnp.float32)).astype(pieces.dtype)
        return scatter_sum(
            kept, index % half, lambda array, to: send(array, lambda n: n // half * half + to(n % half))
        )
    total = lax.dynamic_index_in_dim(pieces, index, 0, keepdims=False).astype(jnp.float32)
    for d in range(1, count):
        given = lax.dynamic_index_in_dim(pieces, (index + d) % count, 0, keepdims=False)
        got = send(given, lambda n: (n + d) % count)
        total = total + got.astype(jnp.float32)
    return total.astype(pieces.dtype)


def sum_gradients(term):
    cores, n_rad, n_z = term.shape[:3]
    i, j = lax.axis_index("rad"), lax.axis_index("azi")

    def over_core(array, to):
        return permuted(array, "azi", lambda n: n // cores * cores + to(n % cores))

    def over_z(array, to):
        return permuted(array, "azi", lambda n: to(n // cores) * cores + n % cores)

    def over_rad(array, to):
        return permuted(array, "rad", to)

    mine = scatter_sum(term, j % cores, over_core)
    mine = scatter_sum(mine, i, over_rad)
    mine = scatter_sum(mine, j // cores, over_z)
    others = [over_rad(mine, lambda n: (n - d) % n_rad) for d in range(1, n_rad)]
    ordered = jnp.roll(jnp.stack([mine] + others), i, axis=0)
    return ordered


def return_all(strip, wrap_col, term, shift_rad, hops):
    cols = strip.shape[2]
    col = jnp.arange(cols, dtype=jnp.int32).reshape(1, 1, cols, 1, 1)

    def body(rows, hops):
        def send(strip, wrap_col, term):
            own = strip[:, :rows]
            main = jnp.where(col < wrap_col, beside(own, True), own)
            near, wrap = strip_routes(hops, True)
            share = sum_gradients(term) if term.ndim > 2 else term
            return full_rows(route(near + wrap, main, True)), share

        return send

    return over_switch(body, (strip, wrap_col, term), shift_rad, hops)


def on_device(tokens, cotangent, ln_gain, qkv_weight, out_weight, shear_offset, window_shift):
    rows_dev, cols_dev, depth, width = tokens.shape
    assert depth == WZ
    number = rows_dev * cols_dev * depth
    n_rad = lax.axis_size("rad")
    n_azi = lax.axis_size("azi")
    at_rad = lax.axis_index("rad")
    total_cols = cols_dev * n_azi
    rim_rows, rim_cols = WR - 1, WA - 1
    shift_rad = window_shift[0]
    shift_azi = window_shift[1]
    offset = shear_offset[0]
    amount = (offset + shift_azi) % total_cols
    hops = amount // cols_dev
    weights = lax.all_gather(
        jnp.concatenate([qkv_weight, out_weight], axis=1), "azi", axis=0, tiled=True
    )
    side = beside(jnp.stack([tokens[:, :rim_cols], cotangent[:, :rim_cols]]), False)
    strip = jnp.stack([tokens[:rim_rows], cotangent[:rim_rows]])
    main, following = fetch_strip(strip, shift_rad, hops)
    last = at_rad == n_rad - 1
    wrap_col = jnp.where(last, amount % cols_dev, shift_azi)
    info = jnp.stack([shift_rad, shift_azi, wrap_col]).astype(jnp.int32)
    cores = 2 if n_azi % 2 == 0 else 1
    part_rows = width // n_azi // n_rad
    placed = part_rows % 16 == 0
    pieces_shape = (cores, n_rad, n_azi // cores, part_rows, 4 * width + LANES)
    y, dx, strip, side, term, gain = block_pass(
        info, tokens, cotangent, side, main, following, ln_gain.reshape(1, width), weights,
        pieces_shape if placed else (width, 4 * width),
    )
    side = beside(side, True)
    strip, share = return_all(strip, wrap_col, term, shift_rad, hops)
    col = jnp.arange(rim_cols, dtype=jnp.int32).reshape(1, rim_cols, 1, 1)
    row = jnp.arange(rim_rows, dtype=jnp.int32).reshape(rim_rows, 1, 1, 1)

    def finish(array, strip, side):
        edge = jnp.where(col < shift_azi, side, array[:, :rim_cols])
        array = lax.dynamic_update_slice(array, edge, (0, 0, 0, 0))
        edge = jnp.where(row < shift_rad, strip, array[:rim_rows])
        return lax.dynamic_update_slice(array, edge, (0, 0, 0, 0))

    block_out = finish(y, strip[0], side[0])
    grad_tokens = finish(dx, strip[1], side[1])
    if placed:
        gain = share[0, :, 4 * width:].reshape(-1)[:width].astype(jnp.float32)
        share = share[:, :, : 4 * width].reshape(n_rad * part_rows, 4 * width)
    else:
        gain = lax.psum(gain[0], BOTH)
        share = lax.psum_scatter(share, "azi", scatter_dimension=0, tiled=True)
        share = lax.psum(share, "rad")
    share = share.astype(jnp.float32)
    factor = float(number * n_rad * n_azi) ** (-0.5)
    grad_qkv = share[:, : 3 * width] * factor
    grad_out = share[:, 3 * width :] * factor
    return (block_out, grad_tokens, grad_qkv, grad_out, gain * factor)


def solution(mesh):
    in_specs = (
        P("rad", "azi", None, None),
        P("rad", "azi", None, None),
        P(),
        P("azi", None),
        P("azi", None),
        P(),
        P(),
    )
    out_specs = (
        P("rad", "azi", None, None),
        P("rad", "azi", None, None),
        P("azi", None),
        P("azi", None),
        P(),
    )
    return jax.shard_map(
        on_device, mesh=mesh, in_specs=in_specs, out_specs=out_specs, check_vma=False
    )
```

```python
import jax
import jax.numpy as jnp
from jax import lax
from jax.experimental import pallas as pl
from jax.experimental.pallas import tpu as pltpu
from jax.sharding import PartitionSpec as P

HEADS = 16
HD = 32
WR = 4
WA = 8
WZ = 8
LANES = 128
LOG2E = 1.4426950408889634

EPS = 1e-05
NT = (((1,), (1,)), ((), ()))
TN = (((0,), (0,)), ((), ()))


def mm(a, b, dims=(((1,), (0,)), ((), ()))):
    return lax.dot_general(a, b, dims, preferred_element_type=jnp.float32)


def block_kernel(
    info_ref, x_ref, g_ref, side_ref, main_ref, next_ref, gain_ref, w_ref,
    y_ref, dx_ref, strip_ref, rim_ref, gw_ref, gg_ref,
    f_s,
    x_s, g_s, xhat_s, qkv_s, da_s, att_s, dqkv_s, hid_all, att_all, gs_all, dqkv_all, gain_s,
):
    step = pl.program_id(0)
    steps = pl.num_programs(0)
    rows, cols, depth, width = x_ref.shape
    rim_rows, rim_cols = strip_ref.shape[1], rim_ref.shape[2]
    grid_a = cols // WA
    tokens = WR * WA * WZ
    first_row, first_col, wrap_col = info_ref[0], info_ref[1], info_ref[2]

    @pl.when(step == 0)
    def _():
        f_s[0] = x_ref[...]
        f_s[1] = g_ref[...]

        def put_strip(n, carry):
            row, col = n // cols, lax.rem(n, cols)
            for f in range(2):
                f_s[f, row, col] = jnp.where(
                    col < wrap_col, next_ref[f, row, col], main_ref[f, row, col]
                )
            return carry

        def put_side(col, carry):
            def put(row, carry):
                for f in range(2):
                    f_s[f, row, col] = side_ref[f, row, col]
                return carry

            return lax.fori_loop(first_row, rows, put, carry)

        lax.fori_loop(0, first_row * cols, put_strip, 0)
        lax.fori_loop(0, first_col, put_side, 0)

    places = []
    for k in range(WR):
        row = lax.rem(first_row + (step // grid_a) * WR + k, rows)
        start = jnp.where(row < first_row, wrap_col, first_col) + (step % grid_a) * WA
        for m in range(WA):
            places.append((row, lax.rem(start + m, cols)))
    for at, (row, col) in enumerate(places):
        x_s[at * WZ:(at + 1) * WZ, :] = f_s[0, row, col].astype(jnp.float32)
        g_s[at * WZ:(at + 1) * WZ, :] = f_s[1, row, col].astype(jnp.float32)
    x = x_s[...]
    gs = g_s[...].astype(jnp.bfloat16)
    gain = gain_ref[...]
    centred = x - jnp.mean(x, axis=1, keepdims=True)
    inv = lax.rsqrt(jnp.mean(centred * centred, axis=1, keepdims=True) + EPS)
    xhat = centred * inv
    xhat_s[...] = xhat
    hidden = (xhat * gain).astype(jnp.bfloat16)
    qkv_s[...] = mm(hidden, w_ref[:, : 3 * width]).astype(jnp.bfloat16)
    da_s[...] = mm(gs, w_ref[:, 3 * width:], NT).astype(jnp.bfloat16)
    scaling = HD ** (-0.5)
    lane = lax.broadcasted_iota(jnp.int32, (1, LANES), 1)
    per_group = LANES // HD

    def group(g, carry):
        base = pl.multiple_of(g * LANES, LANES)
        q = qkv_s[:, pl.ds(base, LANES)]
        k = qkv_s[:, pl.ds(width + base, LANES)]
        v = qkv_s[:, pl.ds(2 * width + base, LANES)]
        da = da_s[:, pl.ds(base, LANES)]
        k_t = k.astype(jnp.float32).T.astype(jnp.bfloat16)
        v_t = v.astype(jnp.float32).T.astype(jnp.bfloat16)
        dv = jnp.zeros((tokens, LANES), jnp.float32)
        dk = jnp.zeros((tokens, LANES), jnp.float32)
        att_t, dq_t = [], []
        for h in range(per_group):
            mine = (lane >= h * HD) & (lane < (h + 1) * HD)
            mask = jnp.where(mine, 1.0, 0.0).astype(jnp.bfloat16)
            qm = q * mask
            dam = da * mask
            s = mm(k, qm, NT) * (scaling * LOG2E)
            e = jnp.exp2(s - jnp.max(s, axis=0, keepdims=True))
            p = e * (1.0 / jnp.sum(e, axis=0, keepdims=True))
            p_low = p.astype(jnp.bfloat16)
            dp = mm(v, dam, NT)
            ds = p * (dp - jnp.sum(p * dp, axis=0, keepdims=True))
            ds = ds.astype(jnp.bfloat16)
            dv += mm(p_low, dam)
            dk += mm(ds, qm)
            att_t.append(mm(v_t[h * HD:(h + 1) * HD], p_low))
            dq_t.append(mm(k_t[h * HD:(h + 1) * HD], ds))
        att_s[:, pl.ds(base, LANES)] = jnp.concatenate(att_t, axis=0).T.astype(jnp.bfloat16)
        dqkv_s[:, pl.ds(base, LANES)] = (
            jnp.concatenate(dq_t, axis=0).T * scaling
        ).astype(jnp.bfloat16)
        dqkv_s[:, pl.ds(width + base, LANES)] = (dk * scaling).astype(jnp.bfloat16)
        dqkv_s[:, pl.ds(2 * width + base, LANES)] = dv.astype(jnp.bfloat16)
        return carry

    lax.fori_loop(0, width // LANES, group, 0)
    att = att_s[...]
    d_qkv = dqkv_s[...]
    d_hidden = mm(d_qkv, w_ref[:, : 3 * width], NT)
    xhat = xhat_s[...]
    term_gain = jnp.sum(d_hidden * xhat, axis=0, keepdims=True)
    d_normed = d_hidden * gain
    y = x_s[...] + mm(att, w_ref[:, 3 * width:])
    dx = g_s[...] + inv * (
        d_normed
        - jnp.mean(d_normed, axis=1, keepdims=True)
        - xhat * jnp.mean(d_normed * xhat, axis=1, keepdims=True)
    )
    for at, (row, col) in enumerate(places):
        y_ref[row, col] = y[at * WZ:(at + 1) * WZ].astype(jnp.bfloat16)
        dx_ref[row, col] = dx[at * WZ:(at + 1) * WZ].astype(jnp.bfloat16)
    here = pl.ds(pl.multiple_of(step * tokens, tokens), tokens)
    hid_all[here, :] = hidden
    att_all[here, :] = att
    gs_all[here, :] = gs
    dqkv_all[here, :] = d_qkv

    @pl.when(step == 0)
    def _():
        gain_s[...] = jnp.zeros_like(gain_s)

    gain_s[...] += term_gain

    @pl.when(step == steps - 1)
    def _():
        for f, ref in enumerate((y_ref, dx_ref)):
            strip_ref[f] = ref[:rim_rows]
            rim_ref[f] = ref[:, :rim_cols]
        g_qkv = mm(hid_all[...], dqkv_all[...], TN).astype(jnp.bfloat16)
        g_out = mm(att_all[...], gs_all[...], TN).astype(jnp.bfloat16)
        gg_ref[...] = gain_s[...]
        if len(gw_ref.shape) == 2:
            gw_ref[:, : 3 * width] = g_qkv
            gw_ref[:, 3 * width:] = g_out
        else:
            cores, n_rad, n_z, part, _ = gw_ref.shape
            extra = jnp.concatenate(
                [gain_s[:, n * LANES:(n + 1) * LANES] for n in range(width // LANES)]
                + [jnp.zeros((part - width // LANES, LANES), jnp.float32)],
                axis=0,
            ).astype(jnp.bfloat16)
            for n in range(cores * n_rad * n_z):
                z, core, i = n // n_rad // cores, n // n_rad % cores, n % n_rad
                here = gw_ref.at[core, i, z]
                here[:, : 3 * width] = g_qkv[n * part:(n + 1) * part]
                here[:, 3 * width: 4 * width] = g_out[n * part:(n + 1) * part]
                here[:, 4 * width:] = extra


def block_pass(info, x, g, side, main, following, gain, weights, term_shape):
    rows, cols, depth, width = x.shape
    tokens = WR * WA * WZ
    number = rows * cols * depth

    def whole(shape):
        return pl.BlockSpec(shape, lambda i, info: (0,) * len(shape))

    bf, f32 = jnp.bfloat16, jnp.float32
    strip_shape = (2, WR - 1, cols, depth, width)
    rim_shape = (2, rows, WA - 1, depth, width)
    ins = (x, g, side, main, following, gain, weights)
    outs = [
        (x.shape, bf), (x.shape, bf), (strip_shape, bf), (rim_shape, bf),
        (term_shape, bf), ((1, width), f32),
    ]
    return pl.pallas_call(
        block_kernel,
        grid_spec=pltpu.PrefetchScalarGridSpec(
            num_scalar_prefetch=1,
            grid=(number // tokens,),
            in_specs=[whole(array.shape) for array in ins],
            out_specs=[whole(shape) for shape, _ in outs],
            scratch_shapes=[
                pltpu.VMEM((2,) + x.shape, bf),
                pltpu.VMEM((tokens, width), f32),
                pltpu.VMEM((tokens, width), f32),
                pltpu.VMEM((tokens, width), f32),
                pltpu.VMEM((tokens, 3 * width), bf),
                pltpu.VMEM((tokens, width), bf),
                pltpu.VMEM((tokens, width), bf),
                pltpu.VMEM((tokens, 3 * width), bf),
                pltpu.VMEM((number, width), bf),
                pltpu.VMEM((number, width), bf),
                pltpu.VMEM((number, width), bf),
                pltpu.VMEM((number, 3 * width), bf),
                pltpu.VMEM((1, width), f32),
            ],
        ),
        out_shape=[jax.ShapeDtypeStruct(shape, kind) for shape, kind in outs],
        compiler_params=pltpu.CompilerParams(vmem_limit_bytes=56 * 1024 * 1024),
        cost_estimate=pl.CostEstimate(
            flops=number * width * width * 24, bytes_accessed=16 * 2 ** 20, transcendentals=0
        ),
        name="block_pass",
    )(info, *ins)


BOTH = ("rad", "azi")


def route(pairs, array, back):
    n_azi = lax.axis_size("azi")
    flat = [(a[0] * n_azi + a[1], b[0] * n_azi + b[1]) for a, b in pairs]
    return lax.ppermute(array, BOTH, [(t, s) if back else (s, t) for s, t in flat])


def strip_routes(hops, back):
    n_rad, n_azi = lax.axis_size("rad"), lax.axis_size("azi")
    azi = range(n_azi)
    near = [((i + 1, j), (i, j)) for i in range(n_rad - 1) for j in azi]
    wrap = [((0, (j + hops) % n_azi), (n_rad - 1, j)) for j in azi]
    return near, wrap


def beside(array, back):
    n_rad, n_azi = lax.axis_size("rad"), lax.axis_size("azi")
    pairs = [((i, (j + 1) % n_azi), (i, j)) for i in range(n_rad) for j in range(n_azi)]
    return route(pairs, array, back)


def over_switch(body, arrays, shift_rad, hops):
    n_azi = lax.axis_size("azi")
    sizes = range(1, WR) if n_azi <= 16 else [WR - 1]
    branches = [body(rows, n) for rows in sizes for n in range(n_azi)]
    index = (shift_rad - 1) * n_azi + hops if len(sizes) > 1 else hops
    return lax.switch(index, branches, *arrays)


def full_rows(array):
    missing = WR - 1 - array.shape[1]
    return jnp.pad(array, ((0, 0), (0, missing), (0, 0), (0, 0), (0, 0)))


def radial_strip(strip, shift_rad, hops, back):
    def body(rows, hops):
        def send(strip):
            near, wrap = strip_routes(hops, back)
            return full_rows(route(near + wrap, strip[:, :rows], back))

        return send

    return over_switch(body, (strip,), shift_rad, hops)


def permuted(array, axis, target):
    count = lax.axis_size(axis)
    return lax.ppermute(array, axis, [(n, target(n)) for n in range(count)])


def scatter_sum(pieces, index, send, hold=lambda arrays: arrays):
    count = pieces.shape[0]
    if count > 4 and count % 2 == 0:
        half = count // 2
        halves = pieces.reshape((2, half) + pieces.shape[1:])
        upper = index // half
        kept = lax.dynamic_index_in_dim(halves, upper, 0, keepdims=False)
        given = lax.dynamic_index_in_dim(halves, 1 - upper, 0, keepdims=False)
        got = send(given, lambda n: (n + half) % count)
        kept = (kept.astype(jnp.float32) + got.astype(jnp.float32)).astype(pieces.dtype)
        return scatter_sum(
            kept,
            index % half,
            lambda array, to: send(array, lambda n: n // half * half + to(n % half)),
            hold,
        )
    total = lax.dynamic_index_in_dim(pieces, index, 0, keepdims=False).astype(jnp.float32)
    arrived = []
    for d in range(1, count):
        given = lax.dynamic_index_in_dim(pieces, (index + d) % count, 0, keepdims=False)
        arrived.append(send(given, lambda n: (n + d) % count))
    for got in hold(arrived):
        total = total + got.astype(jnp.float32)
    return total.astype(pieces.dtype)


def over_core(cores):
    return lambda array, to: permuted(
        array, "azi", lambda n: n // cores * cores + to(n % cores)
    )


def over_z(cores):
    return lambda array, to: permuted(
        array, "azi", lambda n: to(n // cores) * cores + n % cores
    )


def over_rad(array, to):
    return permuted(array, "rad", to)


def gather_over_z(shard, cores):
    groups = [list(range(core, lax.axis_size("azi"), cores)) for core in range(cores)]
    return lax.all_gather(shard, "azi", axis=0, axis_index_groups=groups)


def swap_over_cores(mine, cores):
    if cores == 1:
        return mine.reshape((-1,) + mine.shape[2:])
    other = over_core(cores)(mine, lambda n: (n + 1) % cores)
    core = lax.axis_index("azi") % cores
    both = jnp.where(core == 0, jnp.stack([mine, other], 1), jnp.stack([other, mine], 1))
    return both.reshape((-1,) + mine.shape[2:])


def on_device(tokens, cotangent, ln_gain, qkv_weight, out_weight, shear_offset, window_shift):
    rows_dev, cols_dev, depth, width = tokens.shape
    assert depth == WZ
    number = rows_dev * cols_dev * depth
    n_rad = lax.axis_size("rad")
    n_azi = lax.axis_size("azi")
    at_rad = lax.axis_index("rad")
    total_cols = cols_dev * n_azi
    rim_rows, rim_cols = WR - 1, WA - 1
    shift_rad = window_shift[0]
    shift_azi = window_shift[1]
    offset = shear_offset[0]
    amount = (offset + shift_azi) % total_cols
    hops = amount // cols_dev
    cores = 2 if n_azi % 2 == 0 else 1
    weights = gather_over_z(jnp.concatenate([qkv_weight, out_weight], axis=1), cores)
    side = beside(jnp.stack([tokens[:, :rim_cols], cotangent[:, :rim_cols]]), False)
    strip = jnp.stack([tokens[:rim_rows], cotangent[:rim_rows]])
    main = radial_strip(strip, shift_rad, hops, False)
    main, weights = lax.optimization_barrier((main, weights))
    following = beside(main, False)
    weights = swap_over_cores(weights, cores)
    last = at_rad == n_rad - 1
    wrap_col = jnp.where(last, amount % cols_dev, shift_azi)
    info = jnp.stack([shift_rad, shift_azi, wrap_col]).astype(jnp.int32)
    part_rows = width // n_azi // n_rad
    placed = part_rows % 16 == 0
    pieces_shape = (cores, n_rad, n_azi // cores, part_rows, 4 * width + LANES)
    y, dx, strip, side, term, gain = block_pass(
        info, tokens, cotangent, side, main, following, ln_gain.reshape(1, width), weights,
        pieces_shape if placed else (width, 4 * width),
    )
    following = beside(strip, True)
    side = beside(side, True)
    col = jnp.arange(cols_dev, dtype=jnp.int32).reshape(1, 1, cols_dev, 1, 1)
    strip = jnp.where(col < wrap_col, following, strip)
    if placed:
        at_azi = lax.axis_index("azi")
        term = scatter_sum(term, at_azi % cores, over_core(cores))
        strip, term = lax.optimization_barrier((strip, term))
        strip_back = []

        def beside_strip(arrays):
            arrays, back = lax.optimization_barrier(
                (arrays, radial_strip(strip, shift_rad, hops, True))
            )
            strip_back.append(back)
            return arrays

        term = scatter_sum(term, at_rad, over_rad, beside_strip)
        strip = strip_back[0]
    else:
        strip = radial_strip(strip, shift_rad, hops, True)
    if placed:
        mine = scatter_sum(term, at_azi // cores, over_z(cores))
        others = [over_rad(mine, lambda n: (n - d) % n_rad) for d in range(1, n_rad)]
        share = jnp.roll(jnp.stack([mine] + others), at_rad, axis=0)
    col = jnp.arange(rim_cols, dtype=jnp.int32).reshape(1, rim_cols, 1, 1)
    row = jnp.arange(rim_rows, dtype=jnp.int32).reshape(rim_rows, 1, 1, 1)

    def finish(array, strip, side):
        edge = jnp.where(col < shift_azi, side, array[:, :rim_cols])
        array = lax.dynamic_update_slice(array, edge, (0, 0, 0, 0))
        edge = jnp.where(row < shift_rad, strip, array[:rim_rows])
        return lax.dynamic_update_slice(array, edge, (0, 0, 0, 0))

    block_out = finish(y, strip[0], side[0])
    grad_tokens = finish(dx, strip[1], side[1])
    if placed:
        gain = share[0, :, 4 * width:].reshape(-1)[:width].astype(jnp.float32)
        share = share[:, :, : 4 * width].reshape(n_rad * part_rows, 4 * width)
    else:
        gain = lax.psum(gain[0], BOTH)
        share = lax.psum_scatter(term, "azi", scatter_dimension=0, tiled=True)
        share = lax.psum(share, "rad")
    share = share.astype(jnp.float32)
    factor = float(number * n_rad * n_azi) ** (-0.5)
    grad_qkv = share[:, : 3 * width] * factor
    grad_out = share[:, 3 * width :] * factor
    return (block_out, grad_tokens, grad_qkv, grad_out, gain * factor)


def solution(mesh):
    in_specs = (
        P("rad", "azi", None, None),
        P("rad", "azi", None, None),
        P(),
        P("azi", None),
        P("azi", None),
        P(),
        P(),
    )
    out_specs = (
        P("rad", "azi", None, None),
        P("rad", "azi", None, None),
        P("azi", None),
        P("azi", None),
        P(),
    )
    return jax.shard_map(
        on_device, mesh=mesh, in_specs=in_specs, out_specs=out_specs, check_vma=False
    )
```

```python
import jax
import jax.numpy as jnp
from jax import lax
from jax.experimental import pallas as pl
from jax.experimental.pallas import tpu as pltpu
from jax.sharding import PartitionSpec as P

HEADS = 16
HD = 32
WR = 4
WA = 8
WZ = 8
LANES = 128
LOG2E = 1.4426950408889634

EPS = 1e-05
NT = (((1,), (1,)), ((), ()))
TN = (((0,), (0,)), ((), ()))


def mm(a, b, dims=(((1,), (0,)), ((), ()))):
    return lax.dot_general(a, b, dims, preferred_element_type=jnp.float32)


def block_kernel(
    info_ref, x_ref, g_ref, side_ref, main_ref, next_ref, gain_ref, mine_ref, other_ref,
    y_ref, dx_ref, strip_ref, rim_ref, gw_ref, gg_ref,
    f_s, w_ref,
    x_s, g_s, xhat_s, qkv_s, da_s, att_s, dqkv_s, hid_all, att_all, gs_all, dqkv_all, gain_s,
):
    step = pl.program_id(0)
    steps = pl.num_programs(0)
    rows, cols, depth, width = x_ref.shape
    rim_rows, rim_cols = strip_ref.shape[1], rim_ref.shape[2]
    grid_a = cols // WA
    tokens = WR * WA * WZ
    first_row, first_col, wrap_col = info_ref[0], info_ref[1], info_ref[2]

    @pl.when(step == 0)
    def _():
        f_s[0] = x_ref[...]
        f_s[1] = g_ref[...]

        def put_strip(n, carry):
            row, col = n // cols, lax.rem(n, cols)
            for f in range(2):
                f_s[f, row, col] = jnp.where(
                    col < wrap_col, next_ref[f, row, col], main_ref[f, row, col]
                )
            return carry

        def put_side(col, carry):
            def put(row, carry):
                for f in range(2):
                    f_s[f, row, col] = side_ref[f, row, col]
                return carry

            return lax.fori_loop(first_row, rows, put, carry)

        lax.fori_loop(0, first_row * cols, put_strip, 0)
        lax.fori_loop(0, first_col, put_side, 0)
        n_z, shard, _ = mine_ref.shape
        for d in range(n_z):
            z = lax.rem(info_ref[3] + d, n_z)
            for ref, core in ((mine_ref, info_ref[4]), (other_ref, 1 - info_ref[4])):
                at = pl.multiple_of((z * 2 + core) * shard, shard)
                w_ref[pl.ds(at, shard), :] = ref[d]

    places = []
    for k in range(WR):
        row = lax.rem(first_row + (step // grid_a) * WR + k, rows)
        start = jnp.where(row < first_row, wrap_col, first_col) + (step % grid_a) * WA
        for m in range(WA):
            places.append((row, lax.rem(start + m, cols)))
    for at, (row, col) in enumerate(places):
        x_s[at * WZ:(at + 1) * WZ, :] = f_s[0, row, col].astype(jnp.float32)
        g_s[at * WZ:(at + 1) * WZ, :] = f_s[1, row, col].astype(jnp.float32)
    x = x_s[...]
    gs = g_s[...].astype(jnp.bfloat16)
    gain = gain_ref[...]
    centred = x - jnp.mean(x, axis=1, keepdims=True)
    inv = lax.rsqrt(jnp.mean(centred * centred, axis=1, keepdims=True) + EPS)
    xhat = centred * inv
    xhat_s[...] = xhat
    hidden = (xhat * gain).astype(jnp.bfloat16)
    scaling = HD ** (-0.5)
    q_scaled = mm(hidden, w_ref[:, :width]) * (scaling * LOG2E)
    qkv_s[:, :width] = q_scaled.astype(jnp.bfloat16)
    qkv_s[:, width:] = mm(hidden, w_ref[:, width: 3 * width]).astype(jnp.bfloat16)
    da_s[...] = mm(gs, w_ref[:, 3 * width:], NT).astype(jnp.bfloat16)
    lane = lax.broadcasted_iota(jnp.int32, (1, LANES), 1)
    per_group = LANES // HD

    def group(g, carry):
        base = pl.multiple_of(g * LANES, LANES)
        q = qkv_s[:, pl.ds(base, LANES)]
        k = qkv_s[:, pl.ds(width + base, LANES)]
        v = qkv_s[:, pl.ds(2 * width + base, LANES)]
        da = da_s[:, pl.ds(base, LANES)]
        k_t = k.astype(jnp.float32).T.astype(jnp.bfloat16)
        v_t = v.astype(jnp.float32).T.astype(jnp.bfloat16)
        da_t = da.astype(jnp.float32).T
        dv = jnp.zeros((tokens, LANES), jnp.float32)
        dk = jnp.zeros((tokens, LANES), jnp.float32)
        att_t, dq_t = [], []
        for h in range(per_group):
            mine = (lane >= h * HD) & (lane < (h + 1) * HD)
            mask = jnp.where(mine, 1.0, 0.0).astype(jnp.bfloat16)
            qm = q * mask
            dam = da * mask
            s = mm(k, qm, NT)
            e = jnp.exp2(s - jnp.max(s, axis=0, keepdims=True))
            p = e * (1.0 / jnp.sum(e, axis=0, keepdims=True))
            p_low = p.astype(jnp.bfloat16)
            dp = mm(v, dam, NT)
            mine_t = slice(h * HD, (h + 1) * HD)
            att_t.append(mm(v_t[mine_t], p_low))
            delta = jnp.sum(att_t[-1] * da_t[mine_t], axis=0, keepdims=True)
            ds = (p * (dp - delta)).astype(jnp.bfloat16)
            dv += mm(p_low, dam)
            dk += mm(ds, qm)
            dq_t.append(mm(k_t[mine_t], ds))
        att_s[:, pl.ds(base, LANES)] = jnp.concatenate(att_t, axis=0).T.astype(jnp.bfloat16)
        dqkv_s[:, pl.ds(base, LANES)] = (
            jnp.concatenate(dq_t, axis=0).T * scaling
        ).astype(jnp.bfloat16)
        dqkv_s[:, pl.ds(width + base, LANES)] = (dk * (1.0 / LOG2E)).astype(jnp.bfloat16)
        dqkv_s[:, pl.ds(2 * width + base, LANES)] = dv.astype(jnp.bfloat16)
        return carry

    lax.fori_loop(0, width // LANES, group, 0)
    att = att_s[...]
    d_qkv = dqkv_s[...]
    d_hidden = mm(d_qkv, w_ref[:, : 3 * width], NT)
    xhat = xhat_s[...]
    term_gain = jnp.sum(d_hidden * xhat, axis=0, keepdims=True)
    d_normed = d_hidden * gain
    y = x_s[...] + mm(att, w_ref[:, 3 * width:])
    dx = g_s[...] + inv * (
        d_normed
        - jnp.mean(d_normed, axis=1, keepdims=True)
        - xhat * jnp.mean(d_normed * xhat, axis=1, keepdims=True)
    )
    for at, (row, col) in enumerate(places):
        y_ref[row, col] = y[at * WZ:(at + 1) * WZ].astype(jnp.bfloat16)
        dx_ref[row, col] = dx[at * WZ:(at + 1) * WZ].astype(jnp.bfloat16)
    here = pl.ds(pl.multiple_of(step * tokens, tokens), tokens)
    hid_all[here, :] = hidden
    att_all[here, :] = att
    gs_all[here, :] = gs
    dqkv_all[here, :] = d_qkv

    @pl.when(step == 0)
    def _():
        gain_s[...] = jnp.zeros_like(gain_s)

    gain_s[...] += term_gain

    @pl.when(step == steps - 1)
    def _():
        for f, ref in enumerate((y_ref, dx_ref)):
            strip_ref[f] = ref[:rim_rows]
            rim_ref[f] = ref[:, :rim_cols]
        g_qkv = mm(hid_all[...], dqkv_all[...], TN).astype(jnp.bfloat16)
        g_out = mm(att_all[...], gs_all[...], TN).astype(jnp.bfloat16)
        gg_ref[...] = gain_s[...]
        if len(gw_ref.shape) == 2:
            gw_ref[:, : 3 * width] = g_qkv
            gw_ref[:, 3 * width:] = g_out
        else:
            cores, n_rad, n_z, part, _ = gw_ref.shape
            extra = jnp.concatenate(
                [gain_s[:, n * LANES:(n + 1) * LANES] for n in range(width // LANES)]
                + [jnp.zeros((part - width // LANES, LANES), jnp.float32)],
                axis=0,
            ).astype(jnp.bfloat16)
            for n in range(cores * n_rad * n_z):
                z, core, i = n // n_rad // cores, n // n_rad % cores, n % n_rad
                here = gw_ref.at[core, i, z]
                here[:, : 3 * width] = g_qkv[n * part:(n + 1) * part]
                here[:, 3 * width: 4 * width] = g_out[n * part:(n + 1) * part]
                here[:, 4 * width:] = extra


def block_pass(info, x, g, side, main, following, gain, mine, other, term_shape):
    rows, cols, depth, width = x.shape
    tokens = WR * WA * WZ
    number = rows * cols * depth

    def whole(shape):
        return pl.BlockSpec(shape, lambda i, info: (0,) * len(shape))

    bf, f32 = jnp.bfloat16, jnp.float32
    strip_shape = (2, WR - 1, cols, depth, width)
    rim_shape = (2, rows, WA - 1, depth, width)
    ins = (x, g, side, main, following, gain, mine, other)
    outs = [
        (x.shape, bf), (x.shape, bf), (strip_shape, bf), (rim_shape, bf),
        (term_shape, bf), ((1, width), f32),
    ]
    return pl.pallas_call(
        block_kernel,
        grid_spec=pltpu.PrefetchScalarGridSpec(
            num_scalar_prefetch=1,
            grid=(number // tokens,),
            in_specs=[whole(array.shape) for array in ins],
            out_specs=[whole(shape) for shape, _ in outs],
            scratch_shapes=[
                pltpu.VMEM((2,) + x.shape, bf),
                pltpu.VMEM((width, 4 * width), bf),
                pltpu.VMEM((tokens, width), f32),
                pltpu.VMEM((tokens, width), f32),
                pltpu.VMEM((tokens, width), f32),
                pltpu.VMEM((tokens, 3 * width), bf),
                pltpu.VMEM((tokens, width), bf),
                pltpu.VMEM((tokens, width), bf),
                pltpu.VMEM((tokens, 3 * width), bf),
                pltpu.VMEM((number, width), bf),
                pltpu.VMEM((number, width), bf),
                pltpu.VMEM((number, width), bf),
                pltpu.VMEM((number, 3 * width), bf),
                pltpu.VMEM((1, width), f32),
            ],
        ),
        out_shape=[jax.ShapeDtypeStruct(shape, kind) for shape, kind in outs],
        compiler_params=pltpu.CompilerParams(vmem_limit_bytes=56 * 1024 * 1024),
        cost_estimate=pl.CostEstimate(
            flops=number * width * width * 24, bytes_accessed=16 * 2 ** 20, transcendentals=0
        ),
        name="block_pass",
    )(info, *ins)


BOTH = ("rad", "azi")


def route(pairs, array, back):
    n_azi = lax.axis_size("azi")
    flat = [(a[0] * n_azi + a[1], b[0] * n_azi + b[1]) for a, b in pairs]
    return lax.ppermute(array, BOTH, [(t, s) if back else (s, t) for s, t in flat])


def strip_routes(hops, back):
    n_rad, n_azi = lax.axis_size("rad"), lax.axis_size("azi")
    azi = range(n_azi)
    near = [((i + 1, j), (i, j)) for i in range(n_rad - 1) for j in azi]
    wrap = [((0, (j + hops) % n_azi), (n_rad - 1, j)) for j in azi]
    return near, wrap


def beside(array, back):
    n_rad, n_azi = lax.axis_size("rad"), lax.axis_size("azi")
    pairs = [((i, (j + 1) % n_azi), (i, j)) for i in range(n_rad) for j in range(n_azi)]
    return route(pairs, array, back)


def over_switch(body, arrays, shift_rad, hops):
    n_azi = lax.axis_size("azi")
    sizes = range(1, WR) if n_azi <= 16 else [WR - 1]
    branches = [body(rows, n) for rows in sizes for n in range(n_azi)]
    index = (shift_rad - 1) * n_azi + hops if len(sizes) > 1 else hops
    return lax.switch(index, branches, *arrays)


def full_rows(array):
    missing = WR - 1 - array.shape[1]
    return jnp.pad(array, ((0, 0), (0, missing), (0, 0), (0, 0), (0, 0)))


def radial_strip(strip, shift_rad, hops, back):
    def body(rows, hops):
        def send(strip):
            near, wrap = strip_routes(hops, back)
            return full_rows(route(near + wrap, strip[:, :rows], back))

        return send

    return over_switch(body, (strip,), shift_rad, hops)


def permuted(array, axis, target):
    count = lax.axis_size(axis)
    return lax.ppermute(array, axis, [(n, target(n)) for n in range(count)])


def scatter_sum(pieces, index, send, hold=lambda arrays: arrays):
    count = pieces.shape[0]
    if count > 4 and count % 2 == 0:
        half = count // 2
        halves = pieces.reshape((2, half) + pieces.shape[1:])
        upper = index // half
        kept = lax.dynamic_index_in_dim(halves, upper, 0, keepdims=False)
        given = lax.dynamic_index_in_dim(halves, 1 - upper, 0, keepdims=False)
        got = send(given, lambda n: (n + half) % count)
        kept = (kept.astype(jnp.float32) + got.astype(jnp.float32)).astype(pieces.dtype)
        return scatter_sum(
            kept,
            index % half,
            lambda array, to: send(array, lambda n: n // half * half + to(n % half)),
            hold,
        )
    total = lax.dynamic_index_in_dim(pieces, index, 0, keepdims=False).astype(jnp.float32)
    arrived = []
    for d in range(1, count):
        given = lax.dynamic_index_in_dim(pieces, (index + d) % count, 0, keepdims=False)
        arrived.append(send(given, lambda n: (n + d) % count))
    for got in hold(arrived):
        total = total + got.astype(jnp.float32)
    return total.astype(pieces.dtype)


def over_core(cores):
    return lambda array, to: permuted(
        array, "azi", lambda n: n // cores * cores + to(n % cores)
    )


def over_z(cores):
    return lambda array, to: permuted(
        array, "azi", lambda n: to(n // cores) * cores + n % cores
    )


def over_rad(array, to):
    return permuted(array, "rad", to)


def fetch_all(strip, side, shard, shift_rad, hops, cores):
    n_z = lax.axis_size("azi") // cores
    inside = n_z <= 4

    def swap(mine):
        return over_core(cores)(mine, lambda n: (n + 1) % cores)

    def body(rows, hops):
        def send(strip, side, shard):
            near, wrap = strip_routes(hops, False)
            main = route(near + wrap, strip[:, :rows], False)
            got_side = beside(side, False)
            following = beside(main, False)
            halos = full_rows(main), full_rows(following), got_side
            if not inside:
                return halos
            mine = jnp.stack(
                [shard] + [over_z(cores)(shard, lambda n: (n - d) % n_z) for d in range(1, n_z)]
            )
            return halos + (mine, swap(mine))

        return send

    got = over_switch(body, (strip, side, shard), shift_rad, hops)
    if inside:
        return got + (lax.axis_index("azi") // cores,)
    groups = [list(range(core, n_z * cores, cores)) for core in range(cores)]
    mine = lax.all_gather(shard, "azi", axis=0, axis_index_groups=groups)
    return tuple(got) + (mine, swap(mine), 0)


def on_device(tokens, cotangent, ln_gain, qkv_weight, out_weight, shear_offset, window_shift):
    rows_dev, cols_dev, depth, width = tokens.shape
    assert depth == WZ
    number = rows_dev * cols_dev * depth
    n_rad = lax.axis_size("rad")
    n_azi = lax.axis_size("azi")
    at_rad = lax.axis_index("rad")
    total_cols = cols_dev * n_azi
    rim_rows, rim_cols = WR - 1, WA - 1
    shift_rad = window_shift[0]
    shift_azi = window_shift[1]
    offset = shear_offset[0]
    amount = (offset + shift_azi) % total_cols
    hops = amount // cols_dev
    cores = 2
    assert n_azi % cores == 0
    shard = jnp.concatenate([qkv_weight, out_weight], axis=1)
    side = jnp.stack([tokens[:, :rim_cols], cotangent[:, :rim_cols]])
    strip = jnp.stack([tokens[:rim_rows], cotangent[:rim_rows]])
    main, following, side, mine, other, first_z = fetch_all(
        strip, side, shard, shift_rad, hops, cores
    )
    last = at_rad == n_rad - 1
    wrap_col = jnp.where(last, amount % cols_dev, shift_azi)
    at_core = lax.axis_index("azi") % cores
    info = jnp.stack([shift_rad, shift_azi, wrap_col, first_z, at_core]).astype(jnp.int32)
    part_rows = width // n_azi // n_rad
    placed = part_rows % 16 == 0
    pieces_shape = (cores, n_rad, n_azi // cores, part_rows, 4 * width + LANES)
    y, dx, strip, side, term, gain = block_pass(
        info, tokens, cotangent, side, main, following, ln_gain.reshape(1, width), mine, other,
        pieces_shape if placed else (width, 4 * width),
    )
    following = beside(strip, True)
    side = beside(side, True)
    col = jnp.arange(cols_dev, dtype=jnp.int32).reshape(1, 1, cols_dev, 1, 1)
    strip = jnp.where(col < wrap_col, following, strip)
    if placed:
        at_azi = lax.axis_index("azi")
        term = scatter_sum(term, at_azi % cores, over_core(cores))
        strip_back = []

        def beside_strip(arrays):
            arrays, back = lax.optimization_barrier(
                (arrays, radial_strip(strip, shift_rad, hops, True))
            )
            strip_back.append(back)
            return arrays

        term = scatter_sum(term, at_rad, over_rad, beside_strip)
        strip = strip_back[0]
    else:
        strip = radial_strip(strip, shift_rad, hops, True)
    if placed:
        mine = scatter_sum(term, at_azi // cores, over_z(cores))
        others = [over_rad(mine, lambda n: (n - d) % n_rad) for d in range(1, n_rad)]
        share = jnp.roll(jnp.stack([mine] + others), at_rad, axis=0)
    col = jnp.arange(rim_cols, dtype=jnp.int32).reshape(1, rim_cols, 1, 1)
    row = jnp.arange(rim_rows, dtype=jnp.int32).reshape(rim_rows, 1, 1, 1)

    def finish(array, strip, side):
        edge = jnp.where(col < shift_azi, side, array[:, :rim_cols])
        array = lax.dynamic_update_slice(array, edge, (0, 0, 0, 0))
        edge = jnp.where(row < shift_rad, strip, array[:rim_rows])
        return lax.dynamic_update_slice(array, edge, (0, 0, 0, 0))

    block_out = finish(y, strip[0], side[0])
    grad_tokens = finish(dx, strip[1], side[1])
    if placed:
        gain = share[0, :, 4 * width:].reshape(-1)[:width].astype(jnp.float32)
        share = share[:, :, : 4 * width].reshape(n_rad * part_rows, 4 * width)
    else:
        gain = lax.psum(gain[0], BOTH)
        share = lax.psum_scatter(term, "azi", scatter_dimension=0, tiled=True)
        share = lax.psum(share, "rad")
    share = share.astype(jnp.float32)
    factor = float(number * n_rad * n_azi) ** (-0.5)
    grad_qkv = share[:, : 3 * width] * factor
    grad_out = share[:, 3 * width :] * factor
    return (block_out, grad_tokens, grad_qkv, grad_out, gain * factor)


def solution(mesh):
    in_specs = (
        P("rad", "azi", None, None),
        P("rad", "azi", None, None),
        P(),
        P("azi", None),
        P("azi", None),
        P(),
        P(),
    )
    out_specs = (
        P("rad", "azi", None, None),
        P("rad", "azi", None, None),
        P("azi", None),
        P("azi", None),
        P(),
    )
    return jax.shard_map(
        on_device, mesh=mesh, in_specs=in_specs, out_specs=out_specs, check_vma=False
    )
```

```python
import jax
import jax.numpy as jnp
from jax import lax
from jax.experimental import pallas as pl
from jax.experimental.pallas import tpu as pltpu
from jax.sharding import PartitionSpec as P

HEADS = 16
HD = 32
WR = 4
WA = 8
WZ = 8
LANES = 128
LOG2E = 1.4426950408889634

EPS = 1e-05
NT = (((1,), (1,)), ((), ()))
TN = (((0,), (0,)), ((), ()))


def mm(a, b, dims=(((1,), (0,)), ((), ()))):
    return lax.dot_general(a, b, dims, preferred_element_type=jnp.float32)


def block_kernel(
    info_ref, x_ref, g_ref, side_ref, main_ref, next_ref, gain_ref, mine_ref, other_ref,
    y_ref, dx_ref, strip_ref, rim_ref, gw_ref, gg_ref,
    f_s, w_ref,
    x_s, g_s, xhat_s, qkv_s, da_s, att_s, dqkv_s, hid_all, att_all, gs_all, dqkv_all, gain_s,
):
    step = pl.program_id(0)
    steps = pl.num_programs(0)
    rows, cols, depth, width = x_ref.shape
    rim_rows, rim_cols = strip_ref.shape[1], rim_ref.shape[2]
    grid_a = cols // WA
    tokens = WR * WA * WZ
    first_row, first_col, wrap_col = info_ref[0], info_ref[1], info_ref[2]

    @pl.when(step == 0)
    def _():
        f_s[0] = x_ref[...]
        f_s[1] = g_ref[...]

        def put_strip(n, carry):
            row, col = n // cols, lax.rem(n, cols)
            for f in range(2):
                f_s[f, row, col] = jnp.where(
                    col < wrap_col, next_ref[f, row, col], main_ref[f, row, col]
                )
            return carry

        def put_side(col, carry):
            def put(row, carry):
                for f in range(2):
                    f_s[f, row, col] = side_ref[f, row, col]
                return carry

            return lax.fori_loop(first_row, rows, put, carry)

        lax.fori_loop(0, first_row * cols, put_strip, 0)
        lax.fori_loop(0, first_col, put_side, 0)
        n_z, shard, _ = mine_ref.shape
        for d in range(n_z):
            z = lax.rem(info_ref[3] + d, n_z)
            for ref, core in ((mine_ref, info_ref[4]), (other_ref, 1 - info_ref[4])):
                at = pl.multiple_of((z * 2 + core) * shard, shard)
                w_ref[pl.ds(at, shard), :] = ref[d]

    places = []
    for k in range(WR):
        row = lax.rem(first_row + (step // grid_a) * WR + k, rows)
        start = jnp.where(row < first_row, wrap_col, first_col) + (step % grid_a) * WA
        for m in range(WA):
            places.append((row, lax.rem(start + m, cols)))
    for at, (row, col) in enumerate(places):
        x_s[at * WZ:(at + 1) * WZ, :] = f_s[0, row, col].astype(jnp.float32)
        g_s[at * WZ:(at + 1) * WZ, :] = f_s[1, row, col].astype(jnp.float32)
    x = x_s[...]
    gs = g_s[...].astype(jnp.bfloat16)
    gain = gain_ref[...]
    centred = x - jnp.mean(x, axis=1, keepdims=True)
    inv = lax.rsqrt(jnp.mean(centred * centred, axis=1, keepdims=True) + EPS)
    xhat = centred * inv
    xhat_s[...] = xhat
    hidden = (xhat * gain).astype(jnp.bfloat16)
    scaling = HD ** (-0.5)
    q_scaled = mm(hidden, w_ref[:, :width]) * (scaling * LOG2E)
    qkv_s[:, :width] = q_scaled.astype(jnp.bfloat16)
    qkv_s[:, width:] = mm(hidden, w_ref[:, width: 3 * width]).astype(jnp.bfloat16)
    da_s[...] = mm(gs, w_ref[:, 3 * width:], NT).astype(jnp.bfloat16)
    lane = lax.broadcasted_iota(jnp.int32, (1, LANES), 1)
    per_group = LANES // HD

    def group(g, carry):
        base = pl.multiple_of(g * LANES, LANES)
        q = qkv_s[:, pl.ds(base, LANES)]
        k = qkv_s[:, pl.ds(width + base, LANES)]
        v = qkv_s[:, pl.ds(2 * width + base, LANES)]
        da = da_s[:, pl.ds(base, LANES)]
        k_t = k.astype(jnp.float32).T.astype(jnp.bfloat16)
        v_t = v.astype(jnp.float32).T.astype(jnp.bfloat16)
        da_t = da.astype(jnp.float32).T
        dv = jnp.zeros((tokens, LANES), jnp.float32)
        dk = jnp.zeros((tokens, LANES), jnp.float32)
        att_t, dq_t = [], []

        def products(h):
            mine = (lane >= h * HD) & (lane < (h + 1) * HD)
            mask = jnp.where(mine, 1.0, 0.0).astype(jnp.bfloat16)
            qm = q * mask
            dam = da * mask
            return qm, dam, mm(k, qm, NT), mm(v, dam, NT)

        ready = products(0)
        for h in range(per_group):
            qm, dam, s, dp = ready
            if h + 1 < per_group:
                ready = products(h + 1)
            mine_t = slice(h * HD, (h + 1) * HD)
            e = jnp.exp2(s - jnp.max(s, axis=0, keepdims=True))
            p = e * (1.0 / jnp.sum(e, axis=0, keepdims=True))
            p_low = p.astype(jnp.bfloat16)
            att_t.append(mm(v_t[mine_t], p_low))
            dv += mm(p_low, dam)
            delta = jnp.sum(att_t[-1] * da_t[mine_t], axis=0, keepdims=True)
            ds = (p * (dp - delta)).astype(jnp.bfloat16)
            dk += mm(ds, qm)
            dq_t.append(mm(k_t[mine_t], ds))
        att_s[:, pl.ds(base, LANES)] = jnp.concatenate(att_t, axis=0).T.astype(jnp.bfloat16)
        dqkv_s[:, pl.ds(base, LANES)] = (
            jnp.concatenate(dq_t, axis=0).T * scaling
        ).astype(jnp.bfloat16)
        dqkv_s[:, pl.ds(width + base, LANES)] = (dk * (1.0 / LOG2E)).astype(jnp.bfloat16)
        dqkv_s[:, pl.ds(2 * width + base, LANES)] = dv.astype(jnp.bfloat16)
        return carry

    lax.fori_loop(0, width // LANES, group, 0)
    att = att_s[...]
    d_qkv = dqkv_s[...]
    d_hidden = mm(d_qkv, w_ref[:, : 3 * width], NT)
    xhat = xhat_s[...]
    term_gain = jnp.sum(d_hidden * xhat, axis=0, keepdims=True)
    d_normed = d_hidden * gain
    y = x_s[...] + mm(att, w_ref[:, 3 * width:])
    dx = g_s[...] + inv * (
        d_normed
        - jnp.mean(d_normed, axis=1, keepdims=True)
        - xhat * jnp.mean(d_normed * xhat, axis=1, keepdims=True)
    )
    for at, (row, col) in enumerate(places):
        y_ref[row, col] = y[at * WZ:(at + 1) * WZ].astype(jnp.bfloat16)
        dx_ref[row, col] = dx[at * WZ:(at + 1) * WZ].astype(jnp.bfloat16)
    here = pl.ds(pl.multiple_of(step * tokens, tokens), tokens)
    hid_all[here, :] = hidden
    att_all[here, :] = att
    gs_all[here, :] = gs
    dqkv_all[here, :] = d_qkv

    @pl.when(step == 0)
    def _():
        gain_s[...] = jnp.zeros_like(gain_s)

    gain_s[...] += term_gain

    @pl.when(step == steps - 1)
    def _():
        for f, ref in enumerate((y_ref, dx_ref)):
            strip_ref[f] = ref[:rim_rows]
            rim_ref[f] = ref[:, :rim_cols]
        g_qkv = mm(hid_all[...], dqkv_all[...], TN).astype(jnp.bfloat16)
        g_out = mm(att_all[...], gs_all[...], TN).astype(jnp.bfloat16)
        gg_ref[...] = gain_s[...]
        if len(gw_ref.shape) == 2:
            gw_ref[:, : 3 * width] = g_qkv
            gw_ref[:, 3 * width:] = g_out
        else:
            cores, n_rad, n_z, part, _ = gw_ref.shape
            extra = jnp.concatenate(
                [gain_s[:, n * LANES:(n + 1) * LANES] for n in range(width // LANES)]
                + [jnp.zeros((part - width // LANES, LANES), jnp.float32)],
                axis=0,
            ).astype(jnp.bfloat16)
            for n in range(cores * n_rad * n_z):
                z, core, i = n // n_rad // cores, n // n_rad % cores, n % n_rad
                here = gw_ref.at[core, i, z]
                here[:, : 3 * width] = g_qkv[n * part:(n + 1) * part]
                here[:, 3 * width: 4 * width] = g_out[n * part:(n + 1) * part]
                here[:, 4 * width:] = extra


def block_pass(info, x, g, side, main, following, gain, mine, other, term_shape):
    rows, cols, depth, width = x.shape
    tokens = WR * WA * WZ
    number = rows * cols * depth

    def whole(shape):
        return pl.BlockSpec(shape, lambda i, info: (0,) * len(shape))

    bf, f32 = jnp.bfloat16, jnp.float32
    strip_shape = (2, WR - 1, cols, depth, width)
    rim_shape = (2, rows, WA - 1, depth, width)
    ins = (x, g, side, main, following, gain, mine, other)
    outs = [
        (x.shape, bf), (x.shape, bf), (strip_shape, bf), (rim_shape, bf),
        (term_shape, bf), ((1, width), f32),
    ]
    return pl.pallas_call(
        block_kernel,
        grid_spec=pltpu.PrefetchScalarGridSpec(
            num_scalar_prefetch=1,
            grid=(number // tokens,),
            in_specs=[whole(array.shape) for array in ins],
            out_specs=[whole(shape) for shape, _ in outs],
            scratch_shapes=[
                pltpu.VMEM((2,) + x.shape, bf),
                pltpu.VMEM((width, 4 * width), bf),
                pltpu.VMEM((tokens, width), f32),
                pltpu.VMEM((tokens, width), f32),
                pltpu.VMEM((tokens, width), f32),
                pltpu.VMEM((tokens, 3 * width), bf),
                pltpu.VMEM((tokens, width), bf),
                pltpu.VMEM((tokens, width), bf),
                pltpu.VMEM((tokens, 3 * width), bf),
                pltpu.VMEM((number, width), bf),
                pltpu.VMEM((number, width), bf),
                pltpu.VMEM((number, width), bf),
                pltpu.VMEM((number, 3 * width), bf),
                pltpu.VMEM((1, width), f32),
            ],
        ),
        out_shape=[jax.ShapeDtypeStruct(shape, kind) for shape, kind in outs],
        compiler_params=pltpu.CompilerParams(vmem_limit_bytes=56 * 1024 * 1024),
        cost_estimate=pl.CostEstimate(
            flops=number * width * width * 24, bytes_accessed=16 * 2 ** 20, transcendentals=0
        ),
        name="block_pass",
    )(info, *ins)


BOTH = ("rad", "azi")


def route(pairs, array, back):
    n_azi = lax.axis_size("azi")
    flat = [(a[0] * n_azi + a[1], b[0] * n_azi + b[1]) for a, b in pairs]
    return lax.ppermute(array, BOTH, [(t, s) if back else (s, t) for s, t in flat])


def strip_routes(hops, back):
    n_rad, n_azi = lax.axis_size("rad"), lax.axis_size("azi")
    azi = range(n_azi)
    near = [((i + 1, j), (i, j)) for i in range(n_rad - 1) for j in azi]
    wrap = [((0, (j + hops) % n_azi), (n_rad - 1, j)) for j in azi]
    return near, wrap


def beside(array, back):
    n_rad, n_azi = lax.axis_size("rad"), lax.axis_size("azi")
    pairs = [((i, (j + 1) % n_azi), (i, j)) for i in range(n_rad) for j in range(n_azi)]
    return route(pairs, array, back)


def over_switch(body, arrays, shift_rad, hops):
    n_azi = lax.axis_size("azi")
    sizes = range(1, WR) if n_azi <= 16 else [WR - 1]
    branches = [body(rows, n) for rows in sizes for n in range(n_azi)]
    index = (shift_rad - 1) * n_azi + hops if len(sizes) > 1 else hops
    return lax.switch(index, branches, *arrays)


def full_rows(array):
    missing = WR - 1 - array.shape[1]
    return jnp.pad(array, ((0, 0), (0, missing), (0, 0), (0, 0), (0, 0)))


def radial_strip(strip, shift_rad, hops, back):
    def body(rows, hops):
        def send(strip):
            near, wrap = strip_routes(hops, back)
            return full_rows(route(near + wrap, strip[:, :rows], back))

        return send

    return over_switch(body, (strip,), shift_rad, hops)


def permuted(array, axis, target):
    count = lax.axis_size(axis)
    return lax.ppermute(array, axis, [(n, target(n)) for n in range(count)])


def scatter_sum(pieces, index, send, hold=lambda arrays: arrays):
    count = pieces.shape[0]
    if count > 4 and count % 2 == 0:
        half = count // 2
        halves = pieces.reshape((2, half) + pieces.shape[1:])
        upper = index // half
        kept = lax.dynamic_index_in_dim(halves, upper, 0, keepdims=False)
        given = lax.dynamic_index_in_dim(halves, 1 - upper, 0, keepdims=False)
        got = send(given, lambda n: (n + half) % count)
        kept = (kept.astype(jnp.float32) + got.astype(jnp.float32)).astype(pieces.dtype)
        return scatter_sum(
            kept,
            index % half,
            lambda array, to: send(array, lambda n: n // half * half + to(n % half)),
            hold,
        )
    total = lax.dynamic_index_in_dim(pieces, index, 0, keepdims=False).astype(jnp.float32)
    arrived = []
    for d in range(1, count):
        given = lax.dynamic_index_in_dim(pieces, (index + d) % count, 0, keepdims=False)
        arrived.append(send(given, lambda n: (n + d) % count))
    for got in hold(arrived):
        total = total + got.astype(jnp.float32)
    return total.astype(pieces.dtype)


def over_core(cores):
    return lambda array, to: permuted(
        array, "azi", lambda n: n // cores * cores + to(n % cores)
    )


def over_z(cores):
    return lambda array, to: permuted(
        array, "azi", lambda n: to(n // cores) * cores + n % cores
    )


def over_rad(array, to):
    return permuted(array, "rad", to)


def fetch_all(strip, side, shard, shift_rad, hops, cores):
    n_z = lax.axis_size("azi") // cores
    first_z = 0
    if n_z <= 4:
        first_z = lax.axis_index("azi") // cores
        mine = [over_z(cores)(shard, lambda n: (n - d) % n_z) for d in range(1, n_z)]
        mine = [shard] + mine
    else:
        groups = [list(range(core, n_z * cores, cores)) for core in range(cores)]
        mine = [lax.all_gather(shard, "azi", axis=0, axis_index_groups=groups)]
    side = beside(side, False)
    main = radial_strip(strip, shift_rad, hops, False)
    main, side, mine = lax.optimization_barrier((main, side, mine))
    mine = jnp.stack(mine) if len(mine) > 1 else mine[0]
    other = over_core(cores)(mine, lambda n: (n + 1) % cores)
    following = beside(main, False)
    return main, following, side, mine, other, first_z


def on_device(tokens, cotangent, ln_gain, qkv_weight, out_weight, shear_offset, window_shift):
    rows_dev, cols_dev, depth, width = tokens.shape
    assert depth == WZ
    number = rows_dev * cols_dev * depth
    n_rad = lax.axis_size("rad")
    n_azi = lax.axis_size("azi")
    at_rad = lax.axis_index("rad")
    total_cols = cols_dev * n_azi
    rim_rows, rim_cols = WR - 1, WA - 1
    shift_rad = window_shift[0]
    shift_azi = window_shift[1]
    offset = shear_offset[0]
    amount = (offset + shift_azi) % total_cols
    hops = amount // cols_dev
    cores = 2
    assert n_azi % cores == 0
    shard = jnp.concatenate([qkv_weight, out_weight], axis=1)
    side = jnp.stack([tokens[:, :rim_cols], cotangent[:, :rim_cols]])
    strip = jnp.stack([tokens[:rim_rows], cotangent[:rim_rows]])
    main, following, side, mine, other, first_z = fetch_all(
        strip, side, shard, shift_rad, hops, cores
    )
    last = at_rad == n_rad - 1
    wrap_col = jnp.where(last, amount % cols_dev, shift_azi)
    at_core = lax.axis_index("azi") % cores
    info = jnp.stack([shift_rad, shift_azi, wrap_col, first_z, at_core]).astype(jnp.int32)
    part_rows = width // n_azi // n_rad
    placed = part_rows % 16 == 0
    pieces_shape = (cores, n_rad, n_azi // cores, part_rows, 4 * width + LANES)
    y, dx, strip, side, term, gain = block_pass(
        info, tokens, cotangent, side, main, following, ln_gain.reshape(1, width), mine, other,
        pieces_shape if placed else (width, 4 * width),
    )
    following = beside(strip, True)
    side = beside(side, True)
    col = jnp.arange(cols_dev, dtype=jnp.int32).reshape(1, 1, cols_dev, 1, 1)
    strip = jnp.where(col < wrap_col, following, strip)
    if placed:
        at_azi = lax.axis_index("azi")
        term = scatter_sum(term, at_azi % cores, over_core(cores))
        strip_back = []

        def beside_strip(arrays):
            arrays, back = lax.optimization_barrier(
                (arrays, radial_strip(strip, shift_rad, hops, True))
            )
            strip_back.append(back)
            return arrays

        term = scatter_sum(term, at_rad, over_rad, beside_strip)
        strip = strip_back[0]
    else:
        strip = radial_strip(strip, shift_rad, hops, True)
    if placed:
        mine = scatter_sum(term, at_azi // cores, over_z(cores))
        others = [over_rad(mine, lambda n: (n - d) % n_rad) for d in range(1, n_rad)]
        share = jnp.roll(jnp.stack([mine] + others), at_rad, axis=0)
    col = jnp.arange(rim_cols, dtype=jnp.int32).reshape(1, rim_cols, 1, 1)
    row = jnp.arange(rim_rows, dtype=jnp.int32).reshape(rim_rows, 1, 1, 1)

    def finish(array, strip, side):
        edge = jnp.where(col < shift_azi, side, array[:, :rim_cols])
        array = lax.dynamic_update_slice(array, edge, (0, 0, 0, 0))
        edge = jnp.where(row < shift_rad, strip, array[:rim_rows])
        return lax.dynamic_update_slice(array, edge, (0, 0, 0, 0))

    block_out = finish(y, strip[0], side[0])
    grad_tokens = finish(dx, strip[1], side[1])
    if placed:
        gain = share[0, :, 4 * width:].reshape(-1)[:width].astype(jnp.float32)
        share = share[:, :, : 4 * width].reshape(n_rad * part_rows, 4 * width)
    else:
        gain = lax.psum(gain[0], BOTH)
        share = lax.psum_scatter(term, "azi", scatter_dimension=0, tiled=True)
        share = lax.psum(share, "rad")
    share = share.astype(jnp.float32)
    factor = float(number * n_rad * n_azi) ** (-0.5)
    grad_qkv = share[:, : 3 * width] * factor
    grad_out = share[:, 3 * width :] * factor
    return (block_out, grad_tokens, grad_qkv, grad_out, gain * factor)


def solution(mesh):
    in_specs = (
        P("rad", "azi", None, None),
        P("rad", "azi", None, None),
        P(),
        P("azi", None),
        P("azi", None),
        P(),
        P(),
    )
    out_specs = (
        P("rad", "azi", None, None),
        P("rad", "azi", None, None),
        P("azi", None),
        P("azi", None),
        P(),
    )
    return jax.shard_map(
        on_device, mesh=mesh, in_specs=in_specs, out_specs=out_specs, check_vma=False
    )
```

```python
import jax
import jax.numpy as jnp
from jax import lax
from jax.experimental import pallas as pl
from jax.experimental.pallas import tpu as pltpu
from jax.sharding import PartitionSpec as P

HEADS = 16
HD = 32
WR = 4
WA = 8
WZ = 8
LANES = 128
LOG2E = 1.4426950408889634

EPS = 1e-05
NT = (((1,), (1,)), ((), ()))
TN = (((0,), (0,)), ((), ()))


def mm(a, b, dims=(((1,), (0,)), ((), ()))):
    return lax.dot_general(a, b, dims, preferred_element_type=jnp.float32)


def block_kernel(
    info_ref, x_ref, g_ref, side_ref, main_ref, next_ref, gain_ref, mine_ref, other_ref,
    y_ref, dx_ref, strip_ref, rim_ref, gw_ref, gg_ref,
    f_s, w_ref,
    x_s, g_s, xhat_s, qkv_s, da_s, att_s, dqkv_s, hid_all, att_all, gs_all, dqkv_all, gain_s,
):
    step = pl.program_id(0)
    steps = pl.num_programs(0)
    rows, cols, depth, width = x_ref.shape
    rim_rows, rim_cols = strip_ref.shape[1], rim_ref.shape[2]
    grid_a = cols // WA
    tokens = WR * WA * WZ
    first_row, first_col, wrap_col = info_ref[0], info_ref[1], info_ref[2]

    @pl.when(step == 0)
    def _():
        f_s[0] = x_ref[...]
        f_s[1] = g_ref[...]

        def put_strip(n, carry):
            row, col = n // cols, lax.rem(n, cols)
            for f in range(2):
                f_s[f, row, col] = jnp.where(
                    col < wrap_col, next_ref[f, row, col], main_ref[f, row, col]
                )
            return carry

        def put_side(col, carry):
            def put(row, carry):
                for f in range(2):
                    f_s[f, row, col] = side_ref[f, row, col]
                return carry

            return lax.fori_loop(first_row, rows, put, carry)

        lax.fori_loop(0, first_row * cols, put_strip, 0)
        lax.fori_loop(0, first_col, put_side, 0)
        splits, n_z, share, _ = mine_ref.shape
        for n in range(splits):
            part = lax.rem(info_ref[5] + n, splits)
            for d in range(n_z):
                z = lax.rem(info_ref[3] + d, n_z)
                for ref, core in ((mine_ref, info_ref[4]), (other_ref, 1 - info_ref[4])):
                    at = ((z * 2 + core) * splits + part) * share
                    w_ref[pl.ds(pl.multiple_of(at, share), share), :] = ref[n, d]

    places = []
    for k in range(WR):
        row = lax.rem(first_row + (step // grid_a) * WR + k, rows)
        start = jnp.where(row < first_row, wrap_col, first_col) + (step % grid_a) * WA
        for m in range(WA):
            places.append((row, lax.rem(start + m, cols)))
    for at, (row, col) in enumerate(places):
        x_s[at * WZ:(at + 1) * WZ, :] = f_s[0, row, col].astype(jnp.float32)
        g_s[at * WZ:(at + 1) * WZ, :] = f_s[1, row, col].astype(jnp.float32)
    x = x_s[...]
    gs = g_s[...].astype(jnp.bfloat16)
    gain = gain_ref[...]
    centred = x - jnp.mean(x, axis=1, keepdims=True)
    inv = lax.rsqrt(jnp.mean(centred * centred, axis=1, keepdims=True) + EPS)
    xhat = centred * inv
    xhat_s[...] = xhat
    hidden = (xhat * gain).astype(jnp.bfloat16)
    scaling = HD ** (-0.5)
    q_scaled = mm(hidden, w_ref[:, :width]) * (scaling * LOG2E)
    qkv_s[:, :width] = q_scaled.astype(jnp.bfloat16)
    qkv_s[:, width:] = mm(hidden, w_ref[:, width: 3 * width]).astype(jnp.bfloat16)
    da_s[...] = mm(gs, w_ref[:, 3 * width:], NT).astype(jnp.bfloat16)
    lane = lax.broadcasted_iota(jnp.int32, (1, LANES), 1)
    per_group = LANES // HD

    at_once = 2 if width // LANES % 2 == 0 else 1
    heads = at_once * per_group

    def some_groups(step, carry):
        loaded, taken = {}, {}

        def load(g):
            base = pl.multiple_of((step * at_once + g) * LANES, LANES)
            q = qkv_s[:, pl.ds(base, LANES)]
            k = qkv_s[:, pl.ds(width + base, LANES)]
            v = qkv_s[:, pl.ds(2 * width + base, LANES)]
            da = da_s[:, pl.ds(base, LANES)]
            loaded[g] = q, k, v, da
            k_t = k.astype(jnp.float32).T.astype(jnp.bfloat16)
            v_t = v.astype(jnp.float32).T.astype(jnp.bfloat16)
            taken[g] = k_t, v_t, da.astype(jnp.float32).T

        zeros = jnp.zeros((tokens, LANES), jnp.float32)
        dv, dk = [zeros] * at_once, [zeros] * at_once
        att_t, dq_t = [[] for _ in range(at_once)], [[] for _ in range(at_once)]

        def products(n):
            g, h = n // per_group, n % per_group
            if g not in loaded:
                load(g)
            q, k, v, da = loaded[g]
            mine = (lane >= h * HD) & (lane < (h + 1) * HD)
            mask = jnp.where(mine, 1.0, 0.0).astype(jnp.bfloat16)
            qm = q * mask
            dam = da * mask
            return qm, dam, mm(k, qm, NT), mm(v, dam, NT)

        def forward(n, ready):
            g, h = n // per_group, n % per_group
            qm, dam, s, dp = ready
            _, v_t, da_t = taken[g]
            mine_t = slice(h * HD, (h + 1) * HD)
            e = jnp.exp2(s - jnp.max(s, axis=0, keepdims=True))
            p = e * (1.0 / jnp.sum(e, axis=0, keepdims=True))
            p_low = p.astype(jnp.bfloat16)
            att = mm(v_t[mine_t], p_low)
            att_t[g].append(att)
            dv[g] += mm(p_low, dam)
            return p, dp, jnp.sum(att * da_t[mine_t], axis=0, keepdims=True), qm

        def backward(n, softened):
            g, h = n // per_group, n % per_group
            p, dp, delta, qm = softened
            ds = (p * (dp - delta)).astype(jnp.bfloat16)
            dk[g] += mm(ds, qm)
            dq_t[g].append(mm(taken[g][0][h * HD:(h + 1) * HD], ds))

        ready, softened = products(0), None
        for n in range(heads):
            now = ready
            if n + 1 < heads:
                ready = products(n + 1)
            before, softened = softened, forward(n, now)
            if before is not None:
                backward(n - 1, before)
        backward(heads - 1, softened)
        for g in range(at_once):
            base = pl.multiple_of((step * at_once + g) * LANES, LANES)
            att_s[:, pl.ds(base, LANES)] = (
                jnp.concatenate(att_t[g], axis=0).T.astype(jnp.bfloat16)
            )
            dqkv_s[:, pl.ds(base, LANES)] = (
                jnp.concatenate(dq_t[g], axis=0).T * scaling
            ).astype(jnp.bfloat16)
            dqkv_s[:, pl.ds(width + base, LANES)] = (dk[g] * (1.0 / LOG2E)).astype(jnp.bfloat16)
            dqkv_s[:, pl.ds(2 * width + base, LANES)] = dv[g].astype(jnp.bfloat16)
        return carry

    lax.fori_loop(0, width // LANES // at_once, some_groups, 0)
    att = att_s[...]
    d_qkv = dqkv_s[...]
    d_hidden = mm(d_qkv, w_ref[:, : 3 * width], NT)
    xhat = xhat_s[...]
    term_gain = jnp.sum(d_hidden * xhat, axis=0, keepdims=True)
    d_normed = d_hidden * gain
    y = x_s[...] + mm(att, w_ref[:, 3 * width:])
    dx = g_s[...] + inv * (
        d_normed
        - jnp.mean(d_normed, axis=1, keepdims=True)
        - xhat * jnp.mean(d_normed * xhat, axis=1, keepdims=True)
    )
    for at, (row, col) in enumerate(places):
        y_ref[row, col] = y[at * WZ:(at + 1) * WZ].astype(jnp.bfloat16)
        dx_ref[row, col] = dx[at * WZ:(at + 1) * WZ].astype(jnp.bfloat16)
    here = pl.ds(pl.multiple_of(step * tokens, tokens), tokens)
    hid_all[here, :] = hidden
    att_all[here, :] = att
    gs_all[here, :] = gs
    dqkv_all[here, :] = d_qkv

    @pl.when(step == 0)
    def _():
        gain_s[...] = jnp.zeros_like(gain_s)

    gain_s[...] += term_gain

    @pl.when(step == steps - 1)
    def _():
        for f, ref in enumerate((y_ref, dx_ref)):
            strip_ref[f] = ref[:rim_rows]
            rim_ref[f] = ref[:, :rim_cols]
        g_qkv = mm(hid_all[...], dqkv_all[...], TN).astype(jnp.bfloat16)
        g_out = mm(att_all[...], gs_all[...], TN).astype(jnp.bfloat16)
        gg_ref[...] = gain_s[...]
        if len(gw_ref.shape) == 2:
            gw_ref[:, : 3 * width] = g_qkv
            gw_ref[:, 3 * width:] = g_out
        else:
            cores, n_rad, n_z, part, _ = gw_ref.shape
            extra = jnp.concatenate(
                [gain_s[:, n * LANES:(n + 1) * LANES] for n in range(width // LANES)]
                + [jnp.zeros((part - width // LANES, LANES), jnp.float32)],
                axis=0,
            ).astype(jnp.bfloat16)
            for n in range(cores * n_rad * n_z):
                z, core, i = n // n_rad // cores, n // n_rad % cores, n % n_rad
                here = gw_ref.at[core, i, z]
                here[:, : 3 * width] = g_qkv[n * part:(n + 1) * part]
                here[:, 3 * width: 4 * width] = g_out[n * part:(n + 1) * part]
                here[:, 4 * width:] = extra


def block_pass(info, x, g, side, main, following, gain, mine, other, term_shape):
    rows, cols, depth, width = x.shape
    tokens = WR * WA * WZ
    number = rows * cols * depth

    def whole(shape):
        return pl.BlockSpec(shape, lambda i, info: (0,) * len(shape))

    bf, f32 = jnp.bfloat16, jnp.float32
    strip_shape = (2, WR - 1, cols, depth, width)
    rim_shape = (2, rows, WA - 1, depth, width)
    ins = (x, g, side, main, following, gain, mine, other)
    outs = [
        (x.shape, bf), (x.shape, bf), (strip_shape, bf), (rim_shape, bf),
        (term_shape, bf), ((1, width), f32),
    ]
    return pl.pallas_call(
        block_kernel,
        grid_spec=pltpu.PrefetchScalarGridSpec(
            num_scalar_prefetch=1,
            grid=(number // tokens,),
            in_specs=[whole(array.shape) for array in ins],
            out_specs=[whole(shape) for shape, _ in outs],
            scratch_shapes=[
                pltpu.VMEM((2,) + x.shape, bf),
                pltpu.VMEM((width, 4 * width), bf),
                pltpu.VMEM((tokens, width), f32),
                pltpu.VMEM((tokens, width), f32),
                pltpu.VMEM((tokens, width), f32),
                pltpu.VMEM((tokens, 3 * width), bf),
                pltpu.VMEM((tokens, width), bf),
                pltpu.VMEM((tokens, width), bf),
                pltpu.VMEM((tokens, 3 * width), bf),
                pltpu.VMEM((number, width), bf),
                pltpu.VMEM((number, width), bf),
                pltpu.VMEM((number, width), bf),
                pltpu.VMEM((number, 3 * width), bf),
                pltpu.VMEM((1, width), f32),
            ],
        ),
        out_shape=[jax.ShapeDtypeStruct(shape, kind) for shape, kind in outs],
        compiler_params=pltpu.CompilerParams(vmem_limit_bytes=56 * 1024 * 1024),
        cost_estimate=pl.CostEstimate(
            flops=number * width * width * 24, bytes_accessed=16 * 2 ** 20, transcendentals=0
        ),
        name="block_pass",
    )(info, *ins)


BOTH = ("rad", "azi")


def route(pairs, array, back):
    n_azi = lax.axis_size("azi")
    flat = [(a[0] * n_azi + a[1], b[0] * n_azi + b[1]) for a, b in pairs]
    return lax.ppermute(array, BOTH, [(t, s) if back else (s, t) for s, t in flat])


def strip_routes(hops, back):
    n_rad, n_azi = lax.axis_size("rad"), lax.axis_size("azi")
    azi = range(n_azi)
    near = [((i + 1, j), (i, j)) for i in range(n_rad - 1) for j in azi]
    wrap = [((0, (j + hops) % n_azi), (n_rad - 1, j)) for j in azi]
    return near, wrap


def beside(array, back):
    n_rad, n_azi = lax.axis_size("rad"), lax.axis_size("azi")
    pairs = [((i, (j + 1) % n_azi), (i, j)) for i in range(n_rad) for j in range(n_azi)]
    return route(pairs, array, back)


def over_switch(body, arrays, shift_rad, hops):
    n_azi = lax.axis_size("azi")
    sizes = range(1, WR) if n_azi <= 16 else [WR - 1]
    branches = [body(rows, n) for rows in sizes for n in range(n_azi)]
    index = (shift_rad - 1) * n_azi + hops if len(sizes) > 1 else hops
    return lax.switch(index, branches, *arrays)


def full_rows(array):
    missing = WR - 1 - array.shape[1]
    return jnp.pad(array, ((0, 0), (0, missing), (0, 0), (0, 0), (0, 0)))


def radial_strip(strip, shift_rad, hops, back):
    def body(rows, hops):
        def send(strip):
            near, wrap = strip_routes(hops, back)
            return full_rows(route(near + wrap, strip[:, :rows], back))

        return send

    return over_switch(body, (strip,), shift_rad, hops)


def permuted(array, axis, target):
    count = lax.axis_size(axis)
    return lax.ppermute(array, axis, [(n, target(n)) for n in range(count)])


def scatter_sum(pieces, index, send, hold=lambda arrays: arrays):
    count = pieces.shape[0]
    if count > 4 and count % 2 == 0:
        half = count // 2
        halves = pieces.reshape((2, half) + pieces.shape[1:])
        upper = index // half
        kept = lax.dynamic_index_in_dim(halves, upper, 0, keepdims=False)
        given = lax.dynamic_index_in_dim(halves, 1 - upper, 0, keepdims=False)
        got = send(given, lambda n: (n + half) % count)
        kept = (kept.astype(jnp.float32) + got.astype(jnp.float32)).astype(pieces.dtype)
        return scatter_sum(
            kept,
            index % half,
            lambda array, to: send(array, lambda n: n // half * half + to(n % half)),
            hold,
        )
    total = lax.dynamic_index_in_dim(pieces, index, 0, keepdims=False).astype(jnp.float32)
    arrived = []
    for d in range(1, count):
        given = lax.dynamic_index_in_dim(pieces, (index + d) % count, 0, keepdims=False)
        arrived.append(send(given, lambda n: (n + d) % count))
    for got in hold(arrived):
        total = total + got.astype(jnp.float32)
    return total.astype(pieces.dtype)


def over_core(cores):
    return lambda array, to: permuted(
        array, "azi", lambda n: n // cores * cores + to(n % cores)
    )


def over_z(cores):
    return lambda array, to: permuted(
        array, "azi", lambda n: to(n // cores) * cores + n % cores
    )


def over_rad(array, to):
    return permuted(array, "rad", to)


def fetch_all(strip, side, shard, shift_rad, hops, cores):
    n_rad, n_z = lax.axis_size("rad"), lax.axis_size("azi") // cores
    first_z = first_part = 0
    if n_z <= 4 and n_rad % 2 == 0:
        first_z = lax.axis_index("azi") // cores
        first_part = lax.axis_index("rad") % 2
        share = shard.shape[0] // 2
        half = lax.dynamic_slice_in_dim(shard, first_part * share, share, 0)
        mine = [over_z(cores)(half, lambda n: (n - d) % n_z) for d in range(1, n_z)]
        side = beside(side, False)
        strip, mine = lax.optimization_barrier((strip, [half] + mine))
        mine = jnp.stack(mine)
        partner = over_rad(mine, lambda n: n // 2 * 2 + (n + 1) % 2)
        main = radial_strip(strip, shift_rad, hops, False)
        main, side, mine, partner = lax.optimization_barrier((main, side, mine, partner))
        mine = jnp.stack([mine, partner])
    else:
        groups = [list(range(core, n_z * cores, cores)) for core in range(cores)]
        mine = lax.all_gather(shard, "azi", axis=0, axis_index_groups=groups)[None]
        side = beside(side, False)
        main = radial_strip(strip, shift_rad, hops, False)
    other = over_core(cores)(mine, lambda n: (n + 1) % cores)
    following = beside(main, False)
    return main, following, side, mine, other, first_z, first_part


def on_device(tokens, cotangent, ln_gain, qkv_weight, out_weight, shear_offset, window_shift):
    rows_dev, cols_dev, depth, width = tokens.shape
    assert depth == WZ
    number = rows_dev * cols_dev * depth
    n_rad = lax.axis_size("rad")
    n_azi = lax.axis_size("azi")
    at_rad = lax.axis_index("rad")
    total_cols = cols_dev * n_azi
    rim_rows, rim_cols = WR - 1, WA - 1
    shift_rad = window_shift[0]
    shift_azi = window_shift[1]
    offset = shear_offset[0]
    amount = (offset + shift_azi) % total_cols
    hops = amount // cols_dev
    cores = 2
    assert n_azi % cores == 0
    shard = jnp.concatenate([qkv_weight, out_weight], axis=1)
    side = jnp.stack([tokens[:, :rim_cols], cotangent[:, :rim_cols]])
    strip = jnp.stack([tokens[:rim_rows], cotangent[:rim_rows]])
    main, following, side, mine, other, first_z, first_part = fetch_all(
        strip, side, shard, shift_rad, hops, cores
    )
    last = at_rad == n_rad - 1
    wrap_col = jnp.where(last, amount % cols_dev, shift_azi)
    at_core = lax.axis_index("azi") % cores
    info = [shift_rad, shift_azi, wrap_col, first_z, at_core, first_part]
    info = jnp.stack([jnp.asarray(value, jnp.int32) for value in info])
    part_rows = width // n_azi // n_rad
    placed = part_rows % 16 == 0
    pieces_shape = (cores, n_rad, n_azi // cores, part_rows, 4 * width + LANES)
    y, dx, strip, side, term, gain = block_pass(
        info, tokens, cotangent, side, main, following, ln_gain.reshape(1, width), mine, other,
        pieces_shape if placed else (width, 4 * width),
    )
    following = beside(strip, True)
    following, side = lax.optimization_barrier((following, side))
    side = beside(side, True)
    col = jnp.arange(cols_dev, dtype=jnp.int32).reshape(1, 1, cols_dev, 1, 1)
    strip = jnp.where(col < wrap_col, following, strip)
    if placed:
        at_azi = lax.axis_index("azi")
        term = scatter_sum(term, at_azi % cores, over_core(cores))
        strip_back = []

        def beside_strip(arrays):
            arrays, back, beside_it = lax.optimization_barrier(
                (arrays, radial_strip(strip, shift_rad, hops, True), side)
            )
            strip_back.extend((back, beside_it))
            return arrays

        term = scatter_sum(term, at_rad, over_rad, beside_strip)
        strip, side = strip_back
    else:
        strip = radial_strip(strip, shift_rad, hops, True)
    if placed:
        mine = scatter_sum(term, at_azi // cores, over_z(cores))
        others = [over_rad(mine, lambda n: (n - d) % n_rad) for d in range(1, n_rad)]
        share = jnp.roll(jnp.stack([mine] + others), at_rad, axis=0)
    col = jnp.arange(rim_cols, dtype=jnp.int32).reshape(1, rim_cols, 1, 1)
    row = jnp.arange(rim_rows, dtype=jnp.int32).reshape(rim_rows, 1, 1, 1)

    def finish(array, strip, side):
        edge = jnp.where(col < shift_azi, side, array[:, :rim_cols])
        array = lax.dynamic_update_slice(array, edge, (0, 0, 0, 0))
        edge = jnp.where(row < shift_rad, strip, array[:rim_rows])
        return lax.dynamic_update_slice(array, edge, (0, 0, 0, 0))

    block_out = finish(y, strip[0], side[0])
    grad_tokens = finish(dx, strip[1], side[1])
    if placed:
        gain = share[0, :, 4 * width:].reshape(-1)[:width].astype(jnp.float32)
        share = share[:, :, : 4 * width].reshape(n_rad * part_rows, 4 * width)
    else:
        gain = lax.psum(gain[0], BOTH)
        share = lax.psum_scatter(term, "azi", scatter_dimension=0, tiled=True)
        share = lax.psum(share, "rad")
    share = share.astype(jnp.float32)
    factor = float(number * n_rad * n_azi) ** (-0.5)
    grad_qkv = share[:, : 3 * width] * factor
    grad_out = share[:, 3 * width :] * factor
    return (block_out, grad_tokens, grad_qkv, grad_out, gain * factor)


def solution(mesh):
    in_specs = (
        P("rad", "azi", None, None),
        P("rad", "azi", None, None),
        P(),
        P("azi", None),
        P("azi", None),
        P(),
        P(),
    )
    out_specs = (
        P("rad", "azi", None, None),
        P("rad", "azi", None, None),
        P("azi", None),
        P("azi", None),
        P(),
    )
    return jax.shard_map(
        on_device, mesh=mesh, in_specs=in_specs, out_specs=out_specs, check_vma=False
    )
```

```python
import jax
import jax.numpy as jnp
from jax import lax
from jax.experimental import pallas as pl
from jax.experimental.pallas import tpu as pltpu
from jax.sharding import PartitionSpec as P

HEADS = 16
HD = 32
WR = 4
WA = 8
WZ = 8
LANES = 128
LOG2E = 1.4426950408889634

EPS = 1e-05
NT = (((1,), (1,)), ((), ()))
TN = (((0,), (0,)), ((), ()))


def mm(a, b, dims=(((1,), (0,)), ((), ()))):
    return lax.dot_general(a, b, dims, preferred_element_type=jnp.float32)


def block_kernel(
    info_ref, x_ref, g_ref, side_ref, main_ref, next_ref, gain_ref, mine_ref, other_ref,
    y_ref, dx_ref, strip_ref, rim_ref, gw_ref, gg_ref,
    f_s, w_ref,
    x_s, g_s, xhat_s, qkv_s, da_s, att_s, dqkv_s, hid_all, att_all, gs_all, dqkv_all, gain_s,
):
    step = pl.program_id(0)
    steps = pl.num_programs(0)
    rows, cols, depth, width = x_ref.shape
    rim_rows, rim_cols = strip_ref.shape[1], rim_ref.shape[2]
    grid_a = cols // WA
    tokens = WR * WA * WZ
    first_row, first_col, wrap_col = info_ref[0], info_ref[1], info_ref[2]

    @pl.when(step == 0)
    def _():
        f_s[0] = x_ref[...]
        f_s[1] = g_ref[...]

        def put_strip(n, carry):
            row, col = n // cols, lax.rem(n, cols)
            for f in range(2):
                f_s[f, row, col] = jnp.where(
                    col < wrap_col, next_ref[f, row, col], main_ref[f, row, col]
                )
            return carry

        def put_side(col, carry):
            def put(row, carry):
                for f in range(2):
                    f_s[f, row, col] = side_ref[f, row, col]
                return carry

            return lax.fori_loop(first_row, rows, put, carry)

        lax.fori_loop(0, first_row * cols, put_strip, 0)
        lax.fori_loop(0, first_col, put_side, 0)
        n_z, share, _ = mine_ref.shape
        for d in range(n_z):
            z = lax.rem(info_ref[3] + d, n_z)
            for ref, core in ((mine_ref, info_ref[4]), (other_ref, 1 - info_ref[4])):
                at = pl.multiple_of((z * 2 + core) * share, share)
                w_ref[pl.ds(at, share), :] = ref[d]

    places = []
    for k in range(WR):
        row = lax.rem(first_row + (step // grid_a) * WR + k, rows)
        start = jnp.where(row < first_row, wrap_col, first_col) + (step % grid_a) * WA
        for m in range(WA):
            places.append((row, lax.rem(start + m, cols)))
    for at, (row, col) in enumerate(places):
        x_s[at * WZ:(at + 1) * WZ, :] = f_s[0, row, col].astype(jnp.float32)
        g_s[at * WZ:(at + 1) * WZ, :] = f_s[1, row, col].astype(jnp.float32)
    x = x_s[...]
    gs = g_s[...].astype(jnp.bfloat16)
    gain = gain_ref[...]
    centred = x - jnp.mean(x, axis=1, keepdims=True)
    inv = lax.rsqrt(jnp.mean(centred * centred, axis=1, keepdims=True) + EPS)
    xhat = centred * inv
    xhat_s[...] = xhat
    hidden = (xhat * gain).astype(jnp.bfloat16)
    scaling = HD ** (-0.5)
    q_scaled = mm(hidden, w_ref[:, :width]) * (scaling * LOG2E)
    qkv_s[:, :width] = q_scaled.astype(jnp.bfloat16)
    qkv_s[:, width:] = mm(hidden, w_ref[:, width: 3 * width]).astype(jnp.bfloat16)
    da_s[...] = mm(gs, w_ref[:, 3 * width:], NT).astype(jnp.bfloat16)
    lane = lax.broadcasted_iota(jnp.int32, (1, LANES), 1)
    per_group = LANES // HD

    at_once = width // LANES
    heads = at_once * per_group

    def some_groups(step, carry):
        loaded, taken = {}, {}

        def load(g):
            base = pl.multiple_of((step * at_once + g) * LANES, LANES)
            q = qkv_s[:, pl.ds(base, LANES)]
            k = qkv_s[:, pl.ds(width + base, LANES)]
            v = qkv_s[:, pl.ds(2 * width + base, LANES)]
            da = da_s[:, pl.ds(base, LANES)]
            loaded[g] = q, k, v, da
            k_t = k.astype(jnp.float32).T.astype(jnp.bfloat16)
            v_t = v.astype(jnp.float32).T.astype(jnp.bfloat16)
            taken[g] = k_t, v_t, da.astype(jnp.float32).T

        zeros = jnp.zeros((tokens, LANES), jnp.float32)
        dv, dk = [zeros] * at_once, [zeros] * at_once
        att_t, dq_t = [[] for _ in range(at_once)], [[] for _ in range(at_once)]

        def products(n):
            g, h = n // per_group, n % per_group
            if g not in loaded:
                load(g)
            q, k, v, da = loaded[g]
            mine = (lane >= h * HD) & (lane < (h + 1) * HD)
            mask = jnp.where(mine, 1.0, 0.0).astype(jnp.bfloat16)
            qm = q * mask
            dam = da * mask
            return qm, dam, mm(k, qm, NT), mm(v, dam, NT)

        def forward(n, ready):
            g, h = n // per_group, n % per_group
            qm, dam, s, dp = ready
            _, v_t, da_t = taken[g]
            mine_t = slice(h * HD, (h + 1) * HD)
            e = jnp.exp2(s - jnp.max(s, axis=0, keepdims=True))
            p = e * (1.0 / jnp.sum(e, axis=0, keepdims=True))
            p_low = p.astype(jnp.bfloat16)
            att = mm(v_t[mine_t], p_low)
            att_t[g].append(att)
            dv[g] += mm(p_low, dam)
            return p, dp, jnp.sum(att * da_t[mine_t], axis=0, keepdims=True), qm

        def backward(n, softened):
            g, h = n // per_group, n % per_group
            p, dp, delta, qm = softened
            ds = (p * (dp - delta)).astype(jnp.bfloat16)
            dk[g] += mm(ds, qm)
            dq_t[g].append(mm(taken[g][0][h * HD:(h + 1) * HD], ds))

        ready, softened = products(0), None
        for n in range(heads):
            now = ready
            if n + 1 < heads:
                ready = products(n + 1)
            before, softened = softened, forward(n, now)
            if before is not None:
                backward(n - 1, before)
        backward(heads - 1, softened)
        for g in range(at_once):
            base = pl.multiple_of((step * at_once + g) * LANES, LANES)
            att_s[:, pl.ds(base, LANES)] = (
                jnp.concatenate(att_t[g], axis=0).T.astype(jnp.bfloat16)
            )
            dqkv_s[:, pl.ds(base, LANES)] = (
                jnp.concatenate(dq_t[g], axis=0).T * scaling
            ).astype(jnp.bfloat16)
            dqkv_s[:, pl.ds(width + base, LANES)] = (dk[g] * (1.0 / LOG2E)).astype(jnp.bfloat16)
            dqkv_s[:, pl.ds(2 * width + base, LANES)] = dv[g].astype(jnp.bfloat16)
        return carry

    lax.fori_loop(0, width // LANES // at_once, some_groups, 0)
    att = att_s[...]
    d_qkv = dqkv_s[...]
    d_hidden = mm(d_qkv, w_ref[:, : 3 * width], NT)
    xhat = xhat_s[...]
    term_gain = jnp.sum(d_hidden * xhat, axis=0, keepdims=True)
    d_normed = d_hidden * gain
    y = x_s[...] + mm(att, w_ref[:, 3 * width:])
    dx = g_s[...] + inv * (
        d_normed
        - jnp.mean(d_normed, axis=1, keepdims=True)
        - xhat * jnp.mean(d_normed * xhat, axis=1, keepdims=True)
    )
    for at, (row, col) in enumerate(places):
        y_ref[row, col] = y[at * WZ:(at + 1) * WZ].astype(jnp.bfloat16)
        dx_ref[row, col] = dx[at * WZ:(at + 1) * WZ].astype(jnp.bfloat16)
    here = pl.ds(pl.multiple_of(step * tokens, tokens), tokens)
    hid_all[here, :] = hidden
    att_all[here, :] = att
    gs_all[here, :] = gs
    dqkv_all[here, :] = d_qkv

    @pl.when(step == 0)
    def _():
        gain_s[...] = jnp.zeros_like(gain_s)

    gain_s[...] += term_gain

    @pl.when(step == steps - 1)
    def _():
        for f, ref in enumerate((y_ref, dx_ref)):
            strip_ref[f] = ref[:rim_rows]
            rim_ref[f] = ref[:, :rim_cols]
        g_qkv = mm(hid_all[...], dqkv_all[...], TN).astype(jnp.bfloat16)
        g_out = mm(att_all[...], gs_all[...], TN).astype(jnp.bfloat16)
        gg_ref[...] = gain_s[...]
        if len(gw_ref.shape) == 2:
            gw_ref[:, : 3 * width] = g_qkv
            gw_ref[:, 3 * width:] = g_out
        else:
            cores, n_rad, n_z, part, _ = gw_ref.shape
            extra = jnp.concatenate(
                [gain_s[:, n * LANES:(n + 1) * LANES] for n in range(width // LANES)]
                + [jnp.zeros((part - width // LANES, LANES), jnp.float32)],
                axis=0,
            ).astype(jnp.bfloat16)
            for n in range(cores * n_rad * n_z):
                z, core, i = n // n_rad // cores, n // n_rad % cores, n % n_rad
                here = gw_ref.at[core, i, z]
                here[:, : 3 * width] = g_qkv[n * part:(n + 1) * part]
                here[:, 3 * width: 4 * width] = g_out[n * part:(n + 1) * part]
                here[:, 4 * width:] = extra


def block_pass(info, x, g, side, main, following, gain, mine, other, term_shape):
    rows, cols, depth, width = x.shape
    tokens = WR * WA * WZ
    number = rows * cols * depth

    def whole(shape):
        return pl.BlockSpec(shape, lambda i, info: (0,) * len(shape))

    bf, f32 = jnp.bfloat16, jnp.float32
    strip_shape = (2, WR - 1, cols, depth, width)
    rim_shape = (2, rows, WA - 1, depth, width)
    ins = (x, g, side, main, following, gain, mine, other)
    outs = [
        (x.shape, bf), (x.shape, bf), (strip_shape, bf), (rim_shape, bf),
        (term_shape, bf), ((1, width), f32),
    ]
    return pl.pallas_call(
        block_kernel,
        grid_spec=pltpu.PrefetchScalarGridSpec(
            num_scalar_prefetch=1,
            grid=(number // tokens,),
            in_specs=[whole(array.shape) for array in ins],
            out_specs=[whole(shape) for shape, _ in outs],
            scratch_shapes=[
                pltpu.VMEM((2,) + x.shape, bf),
                pltpu.VMEM((width, 4 * width), bf),
                pltpu.VMEM((tokens, width), f32),
                pltpu.VMEM((tokens, width), f32),
                pltpu.VMEM((tokens, width), f32),
                pltpu.VMEM((tokens, 3 * width), bf),
                pltpu.VMEM((tokens, width), bf),
                pltpu.VMEM((tokens, width), bf),
                pltpu.VMEM((tokens, 3 * width), bf),
                pltpu.VMEM((number, width), bf),
                pltpu.VMEM((number, width), bf),
                pltpu.VMEM((number, width), bf),
                pltpu.VMEM((number, 3 * width), bf),
                pltpu.VMEM((1, width), f32),
            ],
        ),
        out_shape=[jax.ShapeDtypeStruct(shape, kind) for shape, kind in outs],
        compiler_params=pltpu.CompilerParams(vmem_limit_bytes=56 * 1024 * 1024),
        cost_estimate=pl.CostEstimate(
            flops=number * width * width * 24, bytes_accessed=16 * 2 ** 20, transcendentals=0
        ),
        name="block_pass",
    )(info, *ins)


BOTH = ("rad", "azi")


def route(pairs, array, back):
    n_azi = lax.axis_size("azi")
    flat = [(a[0] * n_azi + a[1], b[0] * n_azi + b[1]) for a, b in pairs]
    return lax.ppermute(array, BOTH, [(t, s) if back else (s, t) for s, t in flat])


def strip_routes(hops, back):
    n_rad, n_azi = lax.axis_size("rad"), lax.axis_size("azi")
    azi = range(n_azi)
    near = [((i + 1, j), (i, j)) for i in range(n_rad - 1) for j in azi]
    wrap = [((0, (j + hops) % n_azi), (n_rad - 1, j)) for j in azi]
    return near, wrap


def beside(array, back):
    n_rad, n_azi = lax.axis_size("rad"), lax.axis_size("azi")
    pairs = [((i, (j + 1) % n_azi), (i, j)) for i in range(n_rad) for j in range(n_azi)]
    return route(pairs, array, back)


def over_switch(body, arrays, shift_rad, hops):
    n_azi = lax.axis_size("azi")
    sizes = range(1, WR) if n_azi <= 16 else [WR - 1]
    branches = [body(rows, n) for rows in sizes for n in range(n_azi)]
    index = (shift_rad - 1) * n_azi + hops if len(sizes) > 1 else hops
    return lax.switch(index, branches, *arrays)


def full_rows(array):
    missing = WR - 1 - array.shape[1]
    return jnp.pad(array, ((0, 0), (0, missing), (0, 0), (0, 0), (0, 0)))


def radial_strip(strip, shift_rad, hops, back):
    def body(rows, hops):
        def send(strip):
            near, wrap = strip_routes(hops, back)
            return full_rows(route(near + wrap, strip[:, :rows], back))

        return send

    return over_switch(body, (strip,), shift_rad, hops)


def permuted(array, axis, target):
    count = lax.axis_size(axis)
    return lax.ppermute(array, axis, [(n, target(n)) for n in range(count)])


def scatter_sum(pieces, index, send, hold=lambda arrays: arrays):
    count = pieces.shape[0]
    if count > 4 and count % 2 == 0:
        half = count // 2
        halves = pieces.reshape((2, half) + pieces.shape[1:])
        upper = index // half
        kept = lax.dynamic_index_in_dim(halves, upper, 0, keepdims=False)
        given = lax.dynamic_index_in_dim(halves, 1 - upper, 0, keepdims=False)
        got = send(given, lambda n: (n + half) % count)
        kept = (kept.astype(jnp.float32) + got.astype(jnp.float32)).astype(pieces.dtype)
        return scatter_sum(
            kept,
            index % half,
            lambda array, to: send(array, lambda n: n // half * half + to(n % half)),
            hold,
        )
    total = lax.dynamic_index_in_dim(pieces, index, 0, keepdims=False).astype(jnp.float32)
    arrived = []
    for d in range(1, count):
        given = lax.dynamic_index_in_dim(pieces, (index + d) % count, 0, keepdims=False)
        arrived.append(send(given, lambda n: (n + d) % count))
    for got in hold(arrived):
        total = total + got.astype(jnp.float32)
    return total.astype(pieces.dtype)


def over_core(cores):
    return lambda array, to: permuted(
        array, "azi", lambda n: n // cores * cores + to(n % cores)
    )


def over_z(cores):
    return lambda array, to: permuted(
        array, "azi", lambda n: to(n // cores) * cores + n % cores
    )


def over_rad(array, to):
    return permuted(array, "rad", to)


def fetch_all(strip, side, shard, shift_rad, hops, cores):
    n_z = lax.axis_size("azi") // cores
    first_z = 0
    if n_z <= 4:
        first_z = lax.axis_index("azi") // cores
        mine = [over_z(cores)(shard, lambda n: (n - d) % n_z) for d in range(1, n_z)]
        mine = [shard] + mine
    else:
        groups = [list(range(core, n_z * cores, cores)) for core in range(cores)]
        mine = [lax.all_gather(shard, "azi", axis=0, axis_index_groups=groups)]
    side = beside(side, False)
    main = radial_strip(strip, shift_rad, hops, False)
    main, side, mine = lax.optimization_barrier((main, side, mine))
    mine = jnp.stack(mine) if len(mine) > 1 else mine[0]
    other = over_core(cores)(mine, lambda n: (n + 1) % cores)
    following = beside(main, False)
    return main, following, side, mine, other, first_z


def on_device(tokens, cotangent, ln_gain, qkv_weight, out_weight, shear_offset, window_shift):
    rows_dev, cols_dev, depth, width = tokens.shape
    assert depth == WZ
    number = rows_dev * cols_dev * depth
    n_rad = lax.axis_size("rad")
    n_azi = lax.axis_size("azi")
    at_rad = lax.axis_index("rad")
    total_cols = cols_dev * n_azi
    rim_rows, rim_cols = WR - 1, WA - 1
    shift_rad = window_shift[0]
    shift_azi = window_shift[1]
    offset = shear_offset[0]
    amount = (offset + shift_azi) % total_cols
    hops = amount // cols_dev
    cores = 2
    assert n_azi % cores == 0
    shard = jnp.concatenate([qkv_weight, out_weight], axis=1)
    side = jnp.stack([tokens[:, :rim_cols], cotangent[:, :rim_cols]])
    strip = jnp.stack([tokens[:rim_rows], cotangent[:rim_rows]])
    main, following, side, mine, other, first_z = fetch_all(
        strip, side, shard, shift_rad, hops, cores
    )
    last = at_rad == n_rad - 1
    wrap_col = jnp.where(last, amount % cols_dev, shift_azi)
    at_core = lax.axis_index("azi") % cores
    info = [shift_rad, shift_azi, wrap_col, first_z, at_core]
    info = jnp.stack([jnp.asarray(value, jnp.int32) for value in info])
    part_rows = width // n_azi // n_rad
    placed = part_rows % 16 == 0
    pieces_shape = (cores, n_rad, n_azi // cores, part_rows, 4 * width + LANES)
    y, dx, strip, side, term, gain = block_pass(
        info, tokens, cotangent, side, main, following, ln_gain.reshape(1, width), mine, other,
        pieces_shape if placed else (width, 4 * width),
    )
    following = beside(strip, True)
    following, side = lax.optimization_barrier((following, side))
    side = beside(side, True)
    col = jnp.arange(cols_dev, dtype=jnp.int32).reshape(1, 1, cols_dev, 1, 1)
    if placed:
        at_azi = lax.axis_index("azi")
        term = scatter_sum(term, at_azi % cores, over_core(cores))
        strip_back = []

        def beside_strip(arrays):
            arrays, back, beside_it = lax.optimization_barrier(
                (arrays, radial_strip(strip, shift_rad, hops, True), side)
            )
            strip_back.extend((back, beside_it))
            return arrays

        term = scatter_sum(term, at_rad, over_rad)
        following, term = lax.optimization_barrier((following, term))
        strip = jnp.where(col < wrap_col, following, strip)
        mine = scatter_sum(term, at_azi // cores, over_z(cores), beside_strip)
        strip, side = strip_back
    else:
        strip = jnp.where(col < wrap_col, following, strip)
        strip = radial_strip(strip, shift_rad, hops, True)
    if placed:
        others = [over_rad(mine, lambda n: (n - d) % n_rad) for d in range(1, n_rad)]
        share = jnp.roll(jnp.stack([mine] + others), at_rad, axis=0)
    col = jnp.arange(rim_cols, dtype=jnp.int32).reshape(1, rim_cols, 1, 1)
    row = jnp.arange(rim_rows, dtype=jnp.int32).reshape(rim_rows, 1, 1, 1)

    def finish(array, strip, side):
        edge = jnp.where(col < shift_azi, side, array[:, :rim_cols])
        array = lax.dynamic_update_slice(array, edge, (0, 0, 0, 0))
        edge = jnp.where(row < shift_rad, strip, array[:rim_rows])
        return lax.dynamic_update_slice(array, edge, (0, 0, 0, 0))

    block_out = finish(y, strip[0], side[0])
    grad_tokens = finish(dx, strip[1], side[1])
    if placed:
        gain = share[0, :, 4 * width:].reshape(-1)[:width].astype(jnp.float32)
        share = share[:, :, : 4 * width].reshape(n_rad * part_rows, 4 * width)
    else:
        gain = lax.psum(gain[0], BOTH)
        share = lax.psum_scatter(term, "azi", scatter_dimension=0, tiled=True)
        share = lax.psum(share, "rad")
    share = share.astype(jnp.float32)
    factor = float(number * n_rad * n_azi) ** (-0.5)
    grad_qkv = share[:, : 3 * width] * factor
    grad_out = share[:, 3 * width :] * factor
    return (block_out, grad_tokens, grad_qkv, grad_out, gain * factor)


def solution(mesh):
    in_specs = (
        P("rad", "azi", None, None),
        P("rad", "azi", None, None),
        P(),
        P("azi", None),
        P("azi", None),
        P(),
        P(),
    )
    out_specs = (
        P("rad", "azi", None, None),
        P("rad", "azi", None, None),
        P("azi", None),
        P("azi", None),
        P(),
    )
    return jax.shard_map(
        on_device, mesh=mesh, in_specs=in_specs, out_specs=out_specs, check_vma=False
    )
```

```python
import jax
import jax.numpy as jnp
from jax import lax
from jax.experimental import pallas as pl
from jax.experimental.pallas import tpu as pltpu
from jax.sharding import PartitionSpec as P

HEADS = 16
HD = 32
WR = 4
WA = 8
WZ = 8
LANES = 128
LOG2E = 1.4426950408889634

EPS = 1e-05
NT = (((1,), (1,)), ((), ()))
TN = (((0,), (0,)), ((), ()))


def mm(a, b, dims=(((1,), (0,)), ((), ()))):
    return lax.dot_general(a, b, dims, preferred_element_type=jnp.float32)


def block_kernel(info_ref, *refs):
    x_ref, g_ref, side_ref, main_ref, next_ref, gain_ref = refs[:6]
    weight_refs, refs = refs[6:-20], refs[-20:]
    y_ref, dx_ref, strip_ref, rim_ref, gw_ref, gg_ref, f_s, w_ref = refs[:8]
    x_s, g_s, xhat_s, qkv_s, da_s, att_s, dqkv_s = refs[8:15]
    hid_all, att_all, gs_all, dqkv_all, gain_s = refs[15:20]
    step = pl.program_id(0)
    steps = pl.num_programs(0)
    rows, cols, depth, width = x_ref.shape
    rim_rows, rim_cols = strip_ref.shape[1], rim_ref.shape[2]
    grid_a = cols // WA
    tokens = WR * WA * WZ
    first_row, first_col, wrap_col = info_ref[0], info_ref[1], info_ref[2]

    @pl.when(step == 0)
    def _():
        f_s[0] = x_ref[...]
        f_s[1] = g_ref[...]

        def put_strip(n, carry):
            row, col = n // cols, lax.rem(n, cols)
            for f in range(2):
                f_s[f, row, col] = jnp.where(
                    col < wrap_col, next_ref[f, row, col], main_ref[f, row, col]
                )
            return carry

        def put_side(col, carry):
            def put(row, carry):
                for f in range(2):
                    f_s[f, row, col] = side_ref[f, row, col]
                return carry

            return lax.fori_loop(first_row, rows, put, carry)

        lax.fori_loop(0, first_row * cols, put_strip, 0)
        lax.fori_loop(0, first_col, put_side, 0)
        splits = len(weight_refs) // 2
        n_z, share, _ = weight_refs[0].shape
        for n, ref in enumerate(weight_refs):
            core = info_ref[4] if n < splits else 1 - info_ref[4]
            part = lax.rem(info_ref[5] + n % splits, splits)
            for d in range(n_z):
                z = lax.rem(info_ref[3] + d, n_z)
                at = ((z * 2 + core) * splits + part) * share
                w_ref[pl.ds(pl.multiple_of(at, share), share), :] = ref[d]

    places = []
    for k in range(WR):
        row = lax.rem(first_row + (step // grid_a) * WR + k, rows)
        start = jnp.where(row < first_row, wrap_col, first_col) + (step % grid_a) * WA
        for m in range(WA):
            places.append((row, lax.rem(start + m, cols)))
    for at, (row, col) in enumerate(places):
        x_s[at * WZ:(at + 1) * WZ, :] = f_s[0, row, col].astype(jnp.float32)
        g_s[at * WZ:(at + 1) * WZ, :] = f_s[1, row, col].astype(jnp.float32)
    x = x_s[...]
    gs = g_s[...].astype(jnp.bfloat16)
    gain = gain_ref[...]
    centred = x - jnp.mean(x, axis=1, keepdims=True)
    inv = lax.rsqrt(jnp.mean(centred * centred, axis=1, keepdims=True) + EPS)
    xhat = centred * inv
    xhat_s[...] = xhat
    hidden = (xhat * gain).astype(jnp.bfloat16)
    scaling = HD ** (-0.5)
    q_scaled = mm(hidden, w_ref[:, :width]) * (scaling * LOG2E)
    qkv_s[:, :width] = q_scaled.astype(jnp.bfloat16)
    qkv_s[:, width:] = mm(hidden, w_ref[:, width: 3 * width]).astype(jnp.bfloat16)
    da_s[...] = mm(gs, w_ref[:, 3 * width:], NT).astype(jnp.bfloat16)
    lane = lax.broadcasted_iota(jnp.int32, (1, LANES), 1)
    per_group = LANES // HD

    at_once = width // LANES
    heads = at_once * per_group

    def some_groups(step, carry):
        loaded, taken = {}, {}

        def load(g):
            base = pl.multiple_of((step * at_once + g) * LANES, LANES)
            q = qkv_s[:, pl.ds(base, LANES)]
            k = qkv_s[:, pl.ds(width + base, LANES)]
            v = qkv_s[:, pl.ds(2 * width + base, LANES)]
            da = da_s[:, pl.ds(base, LANES)]
            loaded[g] = q, k, v, da
            k_t = k.astype(jnp.float32).T.astype(jnp.bfloat16)
            v_t = v.astype(jnp.float32).T.astype(jnp.bfloat16)
            taken[g] = k_t, v_t, da.astype(jnp.float32).T

        zeros = jnp.zeros((tokens, LANES), jnp.float32)
        dv, dk = [zeros] * at_once, [zeros] * at_once
        att_t, dq_t = [[] for _ in range(at_once)], [[] for _ in range(at_once)]

        def products(n):
            g, h = n // per_group, n % per_group
            if g not in loaded:
                load(g)
            q, k, v, da = loaded[g]
            mine = (lane >= h * HD) & (lane < (h + 1) * HD)
            mask = jnp.where(mine, 1.0, 0.0).astype(jnp.bfloat16)
            qm = q * mask
            dam = da * mask
            return qm, dam, mm(k, qm, NT), mm(v, dam, NT)

        def forward(n, ready):
            g, h = n // per_group, n % per_group
            qm, dam, s, dp = ready
            _, v_t, da_t = taken[g]
            mine_t = slice(h * HD, (h + 1) * HD)
            e = jnp.exp2(s - jnp.max(s, axis=0, keepdims=True))
            p = e * (1.0 / jnp.sum(e, axis=0, keepdims=True))
            p_low = p.astype(jnp.bfloat16)
            att = mm(v_t[mine_t], p_low)
            att_t[g].append(att)
            dv[g] += mm(p_low, dam)
            return p, dp, jnp.sum(att * da_t[mine_t], axis=0, keepdims=True), qm

        def backward(n, softened):
            g, h = n // per_group, n % per_group
            p, dp, delta, qm = softened
            ds = (p * (dp - delta)).astype(jnp.bfloat16)
            dk[g] += mm(ds, qm)
            dq_t[g].append(mm(taken[g][0][h * HD:(h + 1) * HD], ds))

        ready, softened = products(0), None
        for n in range(heads):
            now = ready
            if n + 1 < heads:
                ready = products(n + 1)
            before, softened = softened, forward(n, now)
            if before is not None:
                backward(n - 1, before)
        backward(heads - 1, softened)
        for g in range(at_once):
            base = pl.multiple_of((step * at_once + g) * LANES, LANES)
            att_s[:, pl.ds(base, LANES)] = (
                jnp.concatenate(att_t[g], axis=0).T.astype(jnp.bfloat16)
            )
            dqkv_s[:, pl.ds(base, LANES)] = (
                jnp.concatenate(dq_t[g], axis=0).T * scaling
            ).astype(jnp.bfloat16)
            dqkv_s[:, pl.ds(width + base, LANES)] = (dk[g] * (1.0 / LOG2E)).astype(jnp.bfloat16)
            dqkv_s[:, pl.ds(2 * width + base, LANES)] = dv[g].astype(jnp.bfloat16)
        return carry

    lax.fori_loop(0, width // LANES // at_once, some_groups, 0)
    att = att_s[...]
    d_qkv = dqkv_s[...]
    d_hidden = mm(d_qkv, w_ref[:, : 3 * width], NT)
    xhat = xhat_s[...]
    term_gain = jnp.sum(d_hidden * xhat, axis=0, keepdims=True)
    d_normed = d_hidden * gain
    y = x_s[...] + mm(att, w_ref[:, 3 * width:])
    dx = g_s[...] + inv * (
        d_normed
        - jnp.mean(d_normed, axis=1, keepdims=True)
        - xhat * jnp.mean(d_normed * xhat, axis=1, keepdims=True)
    )
    for at, (row, col) in enumerate(places):
        y_ref[row, col] = y[at * WZ:(at + 1) * WZ].astype(jnp.bfloat16)
        dx_ref[row, col] = dx[at * WZ:(at + 1) * WZ].astype(jnp.bfloat16)
    here = pl.ds(pl.multiple_of(step * tokens, tokens), tokens)
    hid_all[here, :] = hidden
    att_all[here, :] = att
    gs_all[here, :] = gs
    dqkv_all[here, :] = d_qkv

    @pl.when(step == 0)
    def _():
        gain_s[...] = jnp.zeros_like(gain_s)

    gain_s[...] += term_gain

    @pl.when(step == steps - 1)
    def _():
        for f, ref in enumerate((y_ref, dx_ref)):
            strip_ref[f] = ref[:rim_rows]
            rim_ref[f] = ref[:, :rim_cols]
        g_qkv = mm(hid_all[...], dqkv_all[...], TN).astype(jnp.bfloat16)
        g_out = mm(att_all[...], gs_all[...], TN).astype(jnp.bfloat16)
        gg_ref[...] = gain_s[...]
        if len(gw_ref.shape) == 2:
            gw_ref[:, : 3 * width] = g_qkv
            gw_ref[:, 3 * width:] = g_out
        else:
            cores, n_rad, n_z, part, _ = gw_ref.shape
            extra = jnp.concatenate(
                [gain_s[:, n * LANES:(n + 1) * LANES] for n in range(width // LANES)]
                + [jnp.zeros((part - width // LANES, LANES), jnp.float32)],
                axis=0,
            ).astype(jnp.bfloat16)
            for n in range(cores * n_rad * n_z):
                z, core, i = n // n_rad // cores, n // n_rad % cores, n % n_rad
                here = gw_ref.at[core, i, z]
                here[:, : 3 * width] = g_qkv[n * part:(n + 1) * part]
                here[:, 3 * width: 4 * width] = g_out[n * part:(n + 1) * part]
                here[:, 4 * width:] = extra


def block_pass(info, x, g, side, main, following, gain, weights, term_shape):
    rows, cols, depth, width = x.shape
    tokens = WR * WA * WZ
    number = rows * cols * depth

    def whole(shape):
        return pl.BlockSpec(shape, lambda i, info: (0,) * len(shape))

    bf, f32 = jnp.bfloat16, jnp.float32
    strip_shape = (2, WR - 1, cols, depth, width)
    rim_shape = (2, rows, WA - 1, depth, width)
    ins = (x, g, side, main, following, gain) + tuple(weights)
    outs = [
        (x.shape, bf), (x.shape, bf), (strip_shape, bf), (rim_shape, bf),
        (term_shape, bf), ((1, width), f32),
    ]
    return pl.pallas_call(
        block_kernel,
        grid_spec=pltpu.PrefetchScalarGridSpec(
            num_scalar_prefetch=1,
            grid=(number // tokens,),
            in_specs=[whole(array.shape) for array in ins],
            out_specs=[whole(shape) for shape, _ in outs],
            scratch_shapes=[
                pltpu.VMEM((2,) + x.shape, bf),
                pltpu.VMEM((width, 4 * width), bf),
                pltpu.VMEM((tokens, width), f32),
                pltpu.VMEM((tokens, width), f32),
                pltpu.VMEM((tokens, width), f32),
                pltpu.VMEM((tokens, 3 * width), bf),
                pltpu.VMEM((tokens, width), bf),
                pltpu.VMEM((tokens, width), bf),
                pltpu.VMEM((tokens, 3 * width), bf),
                pltpu.VMEM((number, width), bf),
                pltpu.VMEM((number, width), bf),
                pltpu.VMEM((number, width), bf),
                pltpu.VMEM((number, 3 * width), bf),
                pltpu.VMEM((1, width), f32),
            ],
        ),
        out_shape=[jax.ShapeDtypeStruct(shape, kind) for shape, kind in outs],
        compiler_params=pltpu.CompilerParams(vmem_limit_bytes=56 * 1024 * 1024),
        cost_estimate=pl.CostEstimate(
            flops=number * width * width * 24, bytes_accessed=16 * 2 ** 20, transcendentals=0
        ),
        name="block_pass",
    )(info, *ins)


BOTH = ("rad", "azi")


def route(pairs, array, back):
    n_azi = lax.axis_size("azi")
    flat = [(a[0] * n_azi + a[1], b[0] * n_azi + b[1]) for a, b in pairs]
    return lax.ppermute(array, BOTH, [(t, s) if back else (s, t) for s, t in flat])


def strip_routes(hops, back):
    n_rad, n_azi = lax.axis_size("rad"), lax.axis_size("azi")
    azi = range(n_azi)
    near = [((i + 1, j), (i, j)) for i in range(n_rad - 1) for j in azi]
    wrap = [((0, (j + hops) % n_azi), (n_rad - 1, j)) for j in azi]
    return near, wrap


def beside(array, back):
    n_rad, n_azi = lax.axis_size("rad"), lax.axis_size("azi")
    pairs = [((i, (j + 1) % n_azi), (i, j)) for i in range(n_rad) for j in range(n_azi)]
    return route(pairs, array, back)


def over_switch(body, arrays, shift_rad, hops):
    n_azi = lax.axis_size("azi")
    sizes = range(1, WR) if n_azi <= 16 else [WR - 1]
    branches = [body(rows, n) for rows in sizes for n in range(n_azi)]
    index = (shift_rad - 1) * n_azi + hops if len(sizes) > 1 else hops
    return lax.switch(index, branches, *arrays)


def full_rows(array):
    missing = WR - 1 - array.shape[1]
    return jnp.pad(array, ((0, 0), (0, missing), (0, 0), (0, 0), (0, 0)))


def radial_strip(strip, shift_rad, hops, back):
    def body(rows, hops):
        def send(strip):
            near, wrap = strip_routes(hops, back)
            return full_rows(route(near + wrap, strip[:, :rows], back))

        return send

    return over_switch(body, (strip,), shift_rad, hops)


def permuted(array, axis, target):
    count = lax.axis_size(axis)
    return lax.ppermute(array, axis, [(n, target(n)) for n in range(count)])


def scatter_sum(pieces, index, send, hold=lambda arrays: arrays):
    count = pieces.shape[0]
    if count > 4 and count % 2 == 0:
        half = count // 2
        halves = pieces.reshape((2, half) + pieces.shape[1:])
        upper = index // half
        kept = lax.dynamic_index_in_dim(halves, upper, 0, keepdims=False)
        given = lax.dynamic_index_in_dim(halves, 1 - upper, 0, keepdims=False)
        got = send(given, lambda n: (n + half) % count)
        kept = (kept.astype(jnp.float32) + got.astype(jnp.float32)).astype(pieces.dtype)
        return scatter_sum(
            kept,
            index % half,
            lambda array, to: send(array, lambda n: n // half * half + to(n % half)),
            hold,
        )
    total = lax.dynamic_index_in_dim(pieces, index, 0, keepdims=False).astype(jnp.float32)
    arrived = []
    for d in range(1, count):
        given = lax.dynamic_index_in_dim(pieces, (index + d) % count, 0, keepdims=False)
        arrived.append(send(given, lambda n: (n + d) % count))
    for got in hold(arrived):
        total = total + got.astype(jnp.float32)
    return total.astype(pieces.dtype)


def over_core(cores):
    return lambda array, to: permuted(
        array, "azi", lambda n: n // cores * cores + to(n % cores)
    )


def over_z(cores):
    return lambda array, to: permuted(
        array, "azi", lambda n: to(n // cores) * cores + n % cores
    )


def over_rad(array, to):
    return permuted(array, "rad", to)


def fetch_all(strip, side, shard, shift_rad, hops, cores):
    n_rad, n_z = lax.axis_size("rad"), lax.axis_size("azi") // cores
    first_z = first_part = 0
    split = n_z <= 4 and n_rad % 2 == 0
    if split:
        first_z = lax.axis_index("azi") // cores
        first_part = lax.axis_index("rad") % 2
        share = shard.shape[0] // 2
        half = lax.dynamic_slice_in_dim(shard, first_part * share, share, 0)
        mine = [half] + [over_z(cores)(half, lambda n: (n - d) % n_z) for d in range(1, n_z)]
    else:
        groups = [list(range(core, n_z * cores, cores)) for core in range(cores)]
        mine = [lax.all_gather(shard, "azi", axis=0, axis_index_groups=groups)]
    side = beside(side, False)
    main = radial_strip(strip, shift_rad, hops, False)
    main, side, mine = lax.optimization_barrier((main, side, mine))
    following = beside(main, False)
    if split:
        mine = jnp.stack(mine)
        mine = [mine, over_rad(mine, lambda n: n // 2 * 2 + (n + 1) % 2)]
    weights = mine + [over_core(cores)(part, lambda n: (n + 1) % cores) for part in mine]
    return main, following, side, weights, first_z, first_part


def on_device(tokens, cotangent, ln_gain, qkv_weight, out_weight, shear_offset, window_shift):
    rows_dev, cols_dev, depth, width = tokens.shape
    assert depth == WZ
    number = rows_dev * cols_dev * depth
    n_rad = lax.axis_size("rad")
    n_azi = lax.axis_size("azi")
    at_rad = lax.axis_index("rad")
    total_cols = cols_dev * n_azi
    rim_rows, rim_cols = WR - 1, WA - 1
    shift_rad = window_shift[0]
    shift_azi = window_shift[1]
    offset = shear_offset[0]
    amount = (offset + shift_azi) % total_cols
    hops = amount // cols_dev
    cores = 2
    assert n_azi % cores == 0
    shard = jnp.concatenate([qkv_weight, out_weight], axis=1)
    side = jnp.stack([tokens[:, :rim_cols], cotangent[:, :rim_cols]])
    strip = jnp.stack([tokens[:rim_rows], cotangent[:rim_rows]])
    main, following, side, weights, first_z, first_part = fetch_all(
        strip, side, shard, shift_rad, hops, cores
    )
    last = at_rad == n_rad - 1
    wrap_col = jnp.where(last, amount % cols_dev, shift_azi)
    at_core = lax.axis_index("azi") % cores
    info = [shift_rad, shift_azi, wrap_col, first_z, at_core, first_part]
    info = jnp.stack([jnp.asarray(value, jnp.int32) for value in info])
    part_rows = width // n_azi // n_rad
    placed = part_rows % 16 == 0
    pieces_shape = (cores, n_rad, n_azi // cores, part_rows, 4 * width + LANES)
    y, dx, strip, side, term, gain = block_pass(
        info, tokens, cotangent, side, main, following, ln_gain.reshape(1, width), weights,
        pieces_shape if placed else (width, 4 * width),
    )
    following = beside(strip, True)
    following, side = lax.optimization_barrier((following, side))
    side = beside(side, True)
    col = jnp.arange(cols_dev, dtype=jnp.int32).reshape(1, 1, cols_dev, 1, 1)
    if placed:
        at_azi = lax.axis_index("azi")
        term = scatter_sum(term, at_azi % cores, over_core(cores))
        strip_back = []

        def beside_strip(arrays):
            arrays, back, beside_it = lax.optimization_barrier(
                (arrays, radial_strip(strip, shift_rad, hops, True), side)
            )
            strip_back.extend((back, beside_it))
            return arrays

        term = scatter_sum(term, at_rad, over_rad)
        following, term = lax.optimization_barrier((following, term))
        strip = jnp.where(col < wrap_col, following, strip)
        mine = scatter_sum(term, at_azi // cores, over_z(cores), beside_strip)
        strip, side = strip_back
    else:
        strip = jnp.where(col < wrap_col, following, strip)
        strip = radial_strip(strip, shift_rad, hops, True)
    if placed:
        others = [over_rad(mine, lambda n: (n - d) % n_rad) for d in range(1, n_rad)]
        share = jnp.roll(jnp.stack([mine] + others), at_rad, axis=0)
    col = jnp.arange(rim_cols, dtype=jnp.int32).reshape(1, rim_cols, 1, 1)
    row = jnp.arange(rim_rows, dtype=jnp.int32).reshape(rim_rows, 1, 1, 1)

    def finish(array, strip, side):
        edge = jnp.where(col < shift_azi, side, array[:, :rim_cols])
        array = lax.dynamic_update_slice(array, edge, (0, 0, 0, 0))
        edge = jnp.where(row < shift_rad, strip, array[:rim_rows])
        return lax.dynamic_update_slice(array, edge, (0, 0, 0, 0))

    block_out = finish(y, strip[0], side[0])
    grad_tokens = finish(dx, strip[1], side[1])
    if placed:
        gain = share[0, :, 4 * width:].reshape(-1)[:width].astype(jnp.float32)
        share = share[:, :, : 4 * width].reshape(n_rad * part_rows, 4 * width)
    else:
        gain = lax.psum(gain[0], BOTH)
        share = lax.psum_scatter(term, "azi", scatter_dimension=0, tiled=True)
        share = lax.psum(share, "rad")
    share = share.astype(jnp.float32)
    factor = float(number * n_rad * n_azi) ** (-0.5)
    grad_qkv = share[:, : 3 * width] * factor
    grad_out = share[:, 3 * width :] * factor
    return (block_out, grad_tokens, grad_qkv, grad_out, gain * factor)


def solution(mesh):
    in_specs = (
        P("rad", "azi", None, None),
        P("rad", "azi", None, None),
        P(),
        P("azi", None),
        P("azi", None),
        P(),
        P(),
    )
    out_specs = (
        P("rad", "azi", None, None),
        P("rad", "azi", None, None),
        P("azi", None),
        P("azi", None),
        P(),
    )
    return jax.shard_map(
        on_device, mesh=mesh, in_specs=in_specs, out_specs=out_specs, check_vma=False
    )
```

```python
import jax
import jax.numpy as jnp
from jax import lax
from jax.experimental import pallas as pl
from jax.experimental.pallas import tpu as pltpu
from jax.sharding import PartitionSpec as P

HEADS = 16
HD = 32
WR = 4
WA = 8
WZ = 8
LANES = 128
LOG2E = 1.4426950408889634

EPS = 1e-05
NT = (((1,), (1,)), ((), ()))
TN = (((0,), (0,)), ((), ()))


def mm(a, b, dims=(((1,), (0,)), ((), ()))):
    return lax.dot_general(a, b, dims, preferred_element_type=jnp.float32)


def block_kernel(info_ref, *refs):
    x_ref, g_ref, side_ref, main_ref, next_ref, gain_ref = refs[:6]
    weight_refs, refs = refs[6:-20], refs[-20:]
    y_ref, dx_ref, strip_ref, rim_ref, gw_ref, gg_ref, f_s, w_ref = refs[:8]
    x_s, g_s, xhat_s, qkv_s, da_s, att_s, dqkv_s = refs[8:15]
    hid_all, att_all, gs_all, dqkv_all, gain_s = refs[15:20]
    step = pl.program_id(0)
    steps = pl.num_programs(0)
    rows, cols, depth, width = x_ref.shape
    rim_rows, rim_cols = strip_ref.shape[1], rim_ref.shape[2]
    grid_a = cols // WA
    tokens = WR * WA * WZ
    first_row, first_col, wrap_col = info_ref[0], info_ref[1], info_ref[2]

    @pl.when(step == 0)
    def _():
        f_s[0] = x_ref[...]
        f_s[1] = g_ref[...]

        def put_strip(n, carry):
            row, col = n // cols, lax.rem(n, cols)
            for f in range(2):
                f_s[f, row, col] = jnp.where(
                    col < wrap_col, next_ref[f, row, col], main_ref[f, row, col]
                )
            return carry

        def put_side(col, carry):
            def put(row, carry):
                for f in range(2):
                    f_s[f, row, col] = side_ref[f, row, col]
                return carry

            return lax.fori_loop(first_row, rows, put, carry)

        lax.fori_loop(0, first_row * cols, put_strip, 0)
        lax.fori_loop(0, first_col, put_side, 0)
        splits = len(weight_refs) // 2
        n_z, share, _ = weight_refs[0].shape
        for n, ref in enumerate(weight_refs):
            core = info_ref[4] if n < splits else 1 - info_ref[4]
            part = lax.rem(info_ref[5] + n % splits, splits)
            for d in range(n_z):
                z = lax.rem(info_ref[3] + d, n_z)
                at = ((z * 2 + core) * splits + part) * share
                w_ref[pl.ds(pl.multiple_of(at, share), share), :] = ref[d]

    places = []
    for k in range(WR):
        row = lax.rem(first_row + (step // grid_a) * WR + k, rows)
        start = jnp.where(row < first_row, wrap_col, first_col) + (step % grid_a) * WA
        for m in range(WA):
            places.append((row, lax.rem(start + m, cols)))
    for at, (row, col) in enumerate(places):
        x_s[at * WZ:(at + 1) * WZ, :] = f_s[0, row, col].astype(jnp.float32)
        g_s[at * WZ:(at + 1) * WZ, :] = f_s[1, row, col].astype(jnp.float32)
    x = x_s[...]
    gs = g_s[...].astype(jnp.bfloat16)
    gain = gain_ref[...]
    centred = x - jnp.mean(x, axis=1, keepdims=True)
    inv = lax.rsqrt(jnp.mean(centred * centred, axis=1, keepdims=True) + EPS)
    xhat = centred * inv
    xhat_s[...] = xhat
    hidden = (xhat * gain).astype(jnp.bfloat16)
    scaling = HD ** (-0.5)
    q_scaled = mm(hidden, w_ref[:, :width]) * (scaling * LOG2E)
    qkv_s[:, :width] = q_scaled.astype(jnp.bfloat16)
    qkv_s[:, width:] = mm(hidden, w_ref[:, width: 3 * width]).astype(jnp.bfloat16)
    da_s[...] = mm(gs, w_ref[:, 3 * width:], NT).astype(jnp.bfloat16)
    lane = lax.broadcasted_iota(jnp.int32, (1, LANES), 1)
    per_group = LANES // HD

    at_once = width // LANES
    heads = at_once * per_group

    def some_groups(step, carry):
        loaded, taken = {}, {}

        def load(g):
            base = pl.multiple_of((step * at_once + g) * LANES, LANES)
            q = qkv_s[:, pl.ds(base, LANES)]
            k = qkv_s[:, pl.ds(width + base, LANES)]
            v = qkv_s[:, pl.ds(2 * width + base, LANES)]
            da = da_s[:, pl.ds(base, LANES)]
            loaded[g] = q, k, v, da
            k_t = k.astype(jnp.float32).T.astype(jnp.bfloat16)
            v_t = v.astype(jnp.float32).T.astype(jnp.bfloat16)
            taken[g] = k_t, v_t, da.astype(jnp.float32).T

        zeros = jnp.zeros((tokens, LANES), jnp.float32)
        dv, dk = [zeros] * at_once, [zeros] * at_once
        att_t, dq_t = [[] for _ in range(at_once)], [[] for _ in range(at_once)]

        def products(n):
            g, h = n // per_group, n % per_group
            if g not in loaded:
                load(g)
            q, k, v, da = loaded[g]
            mine = (lane >= h * HD) & (lane < (h + 1) * HD)
            mask = jnp.where(mine, 1.0, 0.0).astype(jnp.bfloat16)
            qm = q * mask
            dam = da * mask
            return qm, dam, mm(k, qm, NT), mm(v, dam, NT)

        def forward(n, ready):
            g, h = n // per_group, n % per_group
            qm, dam, s, dp = ready
            _, v_t, da_t = taken[g]
            mine_t = slice(h * HD, (h + 1) * HD)
            e = jnp.exp2(s - jnp.max(s, axis=0, keepdims=True))
            p = e * (1.0 / jnp.sum(e, axis=0, keepdims=True))
            p_low = p.astype(jnp.bfloat16)
            att = mm(v_t[mine_t], p_low)
            att_t[g].append(att)
            dv[g] += mm(p_low, dam)
            return p, dp, jnp.sum(att * da_t[mine_t], axis=0, keepdims=True), qm

        def backward(n, softened):
            g, h = n // per_group, n % per_group
            p, dp, delta, qm = softened
            ds = (p * (dp - delta)).astype(jnp.bfloat16)
            dk[g] += mm(ds, qm)
            dq_t[g].append(mm(taken[g][0][h * HD:(h + 1) * HD], ds))

        ready, softened = products(0), None
        for n in range(heads):
            now = ready
            if n + 1 < heads:
                ready = products(n + 1)
            if softened is not None:
                backward(n - 1, softened)
            softened = forward(n, now)
        backward(heads - 1, softened)
        for g in range(at_once):
            base = pl.multiple_of((step * at_once + g) * LANES, LANES)
            att_s[:, pl.ds(base, LANES)] = (
                jnp.concatenate(att_t[g], axis=0).T.astype(jnp.bfloat16)
            )
            dqkv_s[:, pl.ds(base, LANES)] = (
                jnp.concatenate(dq_t[g], axis=0).T * scaling
            ).astype(jnp.bfloat16)
            dqkv_s[:, pl.ds(width + base, LANES)] = (dk[g] * (1.0 / LOG2E)).astype(jnp.bfloat16)
            dqkv_s[:, pl.ds(2 * width + base, LANES)] = dv[g].astype(jnp.bfloat16)
        return carry

    lax.fori_loop(0, width // LANES // at_once, some_groups, 0)
    att = att_s[...]
    d_qkv = dqkv_s[...]
    d_hidden = mm(d_qkv, w_ref[:, : 3 * width], NT)
    xhat = xhat_s[...]
    term_gain = jnp.sum(d_hidden * xhat, axis=0, keepdims=True)
    d_normed = d_hidden * gain
    y = x_s[...] + mm(att, w_ref[:, 3 * width:])
    dx = g_s[...] + inv * (
        d_normed
        - jnp.mean(d_normed, axis=1, keepdims=True)
        - xhat * jnp.mean(d_normed * xhat, axis=1, keepdims=True)
    )
    for at, (row, col) in enumerate(places):
        y_ref[row, col] = y[at * WZ:(at + 1) * WZ].astype(jnp.bfloat16)
        dx_ref[row, col] = dx[at * WZ:(at + 1) * WZ].astype(jnp.bfloat16)
    here = pl.ds(pl.multiple_of(step * tokens, tokens), tokens)
    hid_all[here, :] = hidden
    att_all[here, :] = att
    gs_all[here, :] = gs
    dqkv_all[here, :] = d_qkv

    @pl.when(step == 0)
    def _():
        gain_s[...] = jnp.zeros_like(gain_s)

    gain_s[...] += term_gain

    @pl.when(step == steps - 1)
    def _():
        for f, ref in enumerate((y_ref, dx_ref)):
            strip_ref[f] = ref[:rim_rows]
            rim_ref[f] = ref[:, :rim_cols]
        g_qkv = mm(hid_all[...], dqkv_all[...], TN).astype(jnp.bfloat16)
        g_out = mm(att_all[...], gs_all[...], TN).astype(jnp.bfloat16)
        gg_ref[...] = gain_s[...]
        if len(gw_ref.shape) == 2:
            gw_ref[:, : 3 * width] = g_qkv
            gw_ref[:, 3 * width:] = g_out
        else:
            cores, n_rad, n_z, part, _ = gw_ref.shape
            extra = jnp.concatenate(
                [gain_s[:, n * LANES:(n + 1) * LANES] for n in range(width // LANES)]
                + [jnp.zeros((part - width // LANES, LANES), jnp.float32)],
                axis=0,
            ).astype(jnp.bfloat16)
            for n in range(cores * n_rad * n_z):
                z, core, i = n // n_rad // cores, n // n_rad % cores, n % n_rad
                here = gw_ref.at[core, i, z]
                here[:, : 3 * width] = g_qkv[n * part:(n + 1) * part]
                here[:, 3 * width: 4 * width] = g_out[n * part:(n + 1) * part]
                here[:, 4 * width:] = extra


def block_pass(info, x, g, side, main, following, gain, weights, term_shape):
    rows, cols, depth, width = x.shape
    tokens = WR * WA * WZ
    number = rows * cols * depth

    def whole(shape):
        return pl.BlockSpec(shape, lambda i, info: (0,) * len(shape))

    bf, f32 = jnp.bfloat16, jnp.float32
    strip_shape = (2, WR - 1, cols, depth, width)
    rim_shape = (2, rows, WA - 1, depth, width)
    ins = (x, g, side, main, following, gain) + tuple(weights)
    outs = [
        (x.shape, bf), (x.shape, bf), (strip_shape, bf), (rim_shape, bf),
        (term_shape, bf), ((1, width), f32),
    ]
    return pl.pallas_call(
        block_kernel,
        grid_spec=pltpu.PrefetchScalarGridSpec(
            num_scalar_prefetch=1,
            grid=(number // tokens,),
            in_specs=[whole(array.shape) for array in ins],
            out_specs=[whole(shape) for shape, _ in outs],
            scratch_shapes=[
                pltpu.VMEM((2,) + x.shape, bf),
                pltpu.VMEM((width, 4 * width), bf),
                pltpu.VMEM((tokens, width), f32),
                pltpu.VMEM((tokens, width), f32),
                pltpu.VMEM((tokens, width), f32),
                pltpu.VMEM((tokens, 3 * width), bf),
                pltpu.VMEM((tokens, width), bf),
                pltpu.VMEM((tokens, width), bf),
                pltpu.VMEM((tokens, 3 * width), bf),
                pltpu.VMEM((number, width), bf),
                pltpu.VMEM((number, width), bf),
                pltpu.VMEM((number, width), bf),
                pltpu.VMEM((number, 3 * width), bf),
                pltpu.VMEM((1, width), f32),
            ],
        ),
        out_shape=[jax.ShapeDtypeStruct(shape, kind) for shape, kind in outs],
        compiler_params=pltpu.CompilerParams(vmem_limit_bytes=56 * 1024 * 1024),
        cost_estimate=pl.CostEstimate(
            flops=number * width * width * 24, bytes_accessed=16 * 2 ** 20, transcendentals=0
        ),
        name="block_pass",
    )(info, *ins)


BOTH = ("rad", "azi")


def route(pairs, array, back):
    n_azi = lax.axis_size("azi")
    flat = [(a[0] * n_azi + a[1], b[0] * n_azi + b[1]) for a, b in pairs]
    return lax.ppermute(array, BOTH, [(t, s) if back else (s, t) for s, t in flat])


def strip_routes(hops, back):
    n_rad, n_azi = lax.axis_size("rad"), lax.axis_size("azi")
    azi = range(n_azi)
    near = [((i + 1, j), (i, j)) for i in range(n_rad - 1) for j in azi]
    wrap = [((0, (j + hops) % n_azi), (n_rad - 1, j)) for j in azi]
    return near, wrap


def beside(array, back):
    n_rad, n_azi = lax.axis_size("rad"), lax.axis_size("azi")
    pairs = [((i, (j + 1) % n_azi), (i, j)) for i in range(n_rad) for j in range(n_azi)]
    return route(pairs, array, back)


def over_switch(body, arrays, shift_rad, hops):
    n_azi = lax.axis_size("azi")
    sizes = range(1, WR) if n_azi <= 16 else [WR - 1]
    branches = [body(rows, n) for rows in sizes for n in range(n_azi)]
    index = (shift_rad - 1) * n_azi + hops if len(sizes) > 1 else hops
    return lax.switch(index, branches, *arrays)


def full_rows(array):
    missing = WR - 1 - array.shape[1]
    return jnp.pad(array, ((0, 0), (0, missing), (0, 0), (0, 0), (0, 0)))


def radial_strip(strip, shift_rad, hops, back):
    def body(rows, hops):
        def send(strip):
            near, wrap = strip_routes(hops, back)
            return full_rows(route(near + wrap, strip[:, :rows], back))

        return send

    return over_switch(body, (strip,), shift_rad, hops)


def permuted(array, axis, target):
    count = lax.axis_size(axis)
    return lax.ppermute(array, axis, [(n, target(n)) for n in range(count)])


def scatter_sum(pieces, index, send, hold=lambda arrays: arrays):
    count = pieces.shape[0]
    if count > 4 and count % 2 == 0:
        half = count // 2
        halves = pieces.reshape((2, half) + pieces.shape[1:])
        upper = index // half
        kept = lax.dynamic_index_in_dim(halves, upper, 0, keepdims=False)
        given = lax.dynamic_index_in_dim(halves, 1 - upper, 0, keepdims=False)
        got = send(given, lambda n: (n + half) % count)
        kept = (kept.astype(jnp.float32) + got.astype(jnp.float32)).astype(pieces.dtype)
        return scatter_sum(
            kept,
            index % half,
            lambda array, to: send(array, lambda n: n // half * half + to(n % half)),
            hold,
        )
    total = lax.dynamic_index_in_dim(pieces, index, 0, keepdims=False).astype(jnp.float32)
    arrived = []
    for d in range(1, count):
        given = lax.dynamic_index_in_dim(pieces, (index + d) % count, 0, keepdims=False)
        arrived.append(send(given, lambda n: (n + d) % count))
    for got in hold(arrived):
        total = total + got.astype(jnp.float32)
    return total.astype(pieces.dtype)


def over_core(cores):
    return lambda array, to: permuted(
        array, "azi", lambda n: n // cores * cores + to(n % cores)
    )


def over_z(cores):
    return lambda array, to: permuted(
        array, "azi", lambda n: to(n // cores) * cores + n % cores
    )


def over_rad(array, to):
    return permuted(array, "rad", to)


def fetch_all(strip, side, shard, shift_rad, hops, cores):
    n_rad, n_z = lax.axis_size("rad"), lax.axis_size("azi") // cores
    first_z = first_part = 0
    split = n_z <= 4 and n_rad % 2 == 0
    if split:
        first_z = lax.axis_index("azi") // cores
        first_part = lax.axis_index("rad") % 2
        share = shard.shape[0] // 2
        half = lax.dynamic_slice_in_dim(shard, first_part * share, share, 0)
        mine = [half] + [over_z(cores)(half, lambda n: (n - d) % n_z) for d in range(1, n_z)]
    else:
        groups = [list(range(core, n_z * cores, cores)) for core in range(cores)]
        mine = [lax.all_gather(shard, "azi", axis=0, axis_index_groups=groups)]
    main = radial_strip(strip, shift_rad, hops, False)
    main, mine, side = lax.optimization_barrier((main, mine, side))
    following = beside(main, False)
    side = beside(side, False)
    if split:
        mine = jnp.stack(mine)
        mine = [mine, over_rad(mine, lambda n: n // 2 * 2 + (n + 1) % 2)]
    weights = mine + [over_core(cores)(part, lambda n: (n + 1) % cores) for part in mine]
    return main, following, side, weights, first_z, first_part


def on_device(tokens, cotangent, ln_gain, qkv_weight, out_weight, shear_offset, window_shift):
    rows_dev, cols_dev, depth, width = tokens.shape
    assert depth == WZ
    number = rows_dev * cols_dev * depth
    n_rad = lax.axis_size("rad")
    n_azi = lax.axis_size("azi")
    at_rad = lax.axis_index("rad")
    total_cols = cols_dev * n_azi
    rim_rows, rim_cols = WR - 1, WA - 1
    shift_rad = window_shift[0]
    shift_azi = window_shift[1]
    offset = shear_offset[0]
    amount = (offset + shift_azi) % total_cols
    hops = amount // cols_dev
    cores = 2
    assert n_azi % cores == 0
    shard = jnp.concatenate([qkv_weight, out_weight], axis=1)
    side = jnp.stack([tokens[:, :rim_cols], cotangent[:, :rim_cols]])
    strip = jnp.stack([tokens[:rim_rows], cotangent[:rim_rows]])
    main, following, side, weights, first_z, first_part = fetch_all(
        strip, side, shard, shift_rad, hops, cores
    )
    last = at_rad == n_rad - 1
    wrap_col = jnp.where(last, amount % cols_dev, shift_azi)
    at_core = lax.axis_index("azi") % cores
    info = [shift_rad, shift_azi, wrap_col, first_z, at_core, first_part]
    info = jnp.stack([jnp.asarray(value, jnp.int32) for value in info])
    part_rows = width // n_azi // n_rad
    placed = part_rows % 16 == 0
    pieces_shape = (cores, n_rad, n_azi // cores, part_rows, 4 * width + LANES)
    y, dx, strip, side, term, gain = block_pass(
        info, tokens, cotangent, side, main, following, ln_gain.reshape(1, width), weights,
        pieces_shape if placed else (width, 4 * width),
    )
    following = beside(strip, True)
    following, side = lax.optimization_barrier((following, side))
    side = beside(side, True)
    col = jnp.arange(cols_dev, dtype=jnp.int32).reshape(1, 1, cols_dev, 1, 1)
    if placed:
        at_azi = lax.axis_index("azi")
        term = scatter_sum(term, at_azi % cores, over_core(cores))
        strip_back = []

        def beside_strip(arrays):
            arrays, back, beside_it = lax.optimization_barrier(
                (arrays, radial_strip(strip, shift_rad, hops, True), side)
            )
            strip_back.extend((back, beside_it))
            return arrays

        term = scatter_sum(term, at_rad, over_rad)
        following, term = lax.optimization_barrier((following, term))
        strip = jnp.where(col < wrap_col, following, strip)
        mine = scatter_sum(term, at_azi // cores, over_z(cores), beside_strip)
        strip, side = strip_back
    else:
        strip = jnp.where(col < wrap_col, following, strip)
        strip = radial_strip(strip, shift_rad, hops, True)
    if placed:
        others = [over_rad(mine, lambda n: (n - d) % n_rad) for d in range(1, n_rad)]
        share = jnp.roll(jnp.stack([mine] + others), at_rad, axis=0)
    col = jnp.arange(rim_cols, dtype=jnp.int32).reshape(1, rim_cols, 1, 1)
    row = jnp.arange(rim_rows, dtype=jnp.int32).reshape(rim_rows, 1, 1, 1)

    def finish(array, strip, side):
        edge = jnp.where(col < shift_azi, side, array[:, :rim_cols])
        array = lax.dynamic_update_slice(array, edge, (0, 0, 0, 0))
        edge = jnp.where(row < shift_rad, strip, array[:rim_rows])
        return lax.dynamic_update_slice(array, edge, (0, 0, 0, 0))

    block_out = finish(y, strip[0], side[0])
    grad_tokens = finish(dx, strip[1], side[1])
    if placed:
        gain = share[0, :, 4 * width:].reshape(-1)[:width].astype(jnp.float32)
        share = share[:, :, : 4 * width].reshape(n_rad * part_rows, 4 * width)
    else:
        gain = lax.psum(gain[0], BOTH)
        share = lax.psum_scatter(term, "azi", scatter_dimension=0, tiled=True)
        share = lax.psum(share, "rad")
    share = share.astype(jnp.float32)
    factor = float(number * n_rad * n_azi) ** (-0.5)
    grad_qkv = share[:, : 3 * width] * factor
    grad_out = share[:, 3 * width :] * factor
    return (block_out, grad_tokens, grad_qkv, grad_out, gain * factor)


def solution(mesh):
    in_specs = (
        P("rad", "azi", None, None),
        P("rad", "azi", None, None),
        P(),
        P("azi", None),
        P("azi", None),
        P(),
        P(),
    )
    out_specs = (
        P("rad", "azi", None, None),
        P("rad", "azi", None, None),
        P("azi", None),
        P("azi", None),
        P(),
    )
    return jax.shard_map(
        on_device, mesh=mesh, in_specs=in_specs, out_specs=out_specs, check_vma=False
    )
```

```python
import jax
import jax.numpy as jnp
from jax import lax
from jax.experimental import pallas as pl
from jax.experimental.pallas import tpu as pltpu
from jax.sharding import PartitionSpec as P

HEADS = 16
HD = 32
WR = 4
WA = 8
WZ = 8
LANES = 128
LOG2E = 1.4426950408889634

EPS = 1e-05
NT = (((1,), (1,)), ((), ()))
TN = (((0,), (0,)), ((), ()))


def mm(a, b, dims=(((1,), (0,)), ((), ()))):
    return lax.dot_general(a, b, dims, preferred_element_type=jnp.float32)


def block_kernel(info_ref, *refs):
    x_ref, g_ref, side_ref, main_ref, next_ref, gain_ref = refs[:6]
    weight_refs, refs = refs[6:-20], refs[-20:]
    y_ref, dx_ref, strip_ref, rim_ref, gw_ref, gg_ref, f_s, w_ref = refs[:8]
    x_s, g_s, xhat_s, qkv_s, da_s, att_s, dqkv_s = refs[8:15]
    hid_all, att_all, gs_all, dqkv_all, gain_s = refs[15:20]
    step = pl.program_id(0)
    steps = pl.num_programs(0)
    rows, cols, depth, width = x_ref.shape
    rim_rows, rim_cols = strip_ref.shape[1], rim_ref.shape[2]
    grid_a = cols // WA
    tokens = WR * WA * WZ
    first_row, first_col, wrap_col = info_ref[0], info_ref[1], info_ref[2]

    @pl.when(step == 0)
    def _():
        f_s[0] = x_ref[...]
        f_s[1] = g_ref[...]

        def put_strip(n, carry):
            row, col = n // cols, lax.rem(n, cols)
            for f in range(2):
                f_s[f, row, col] = jnp.where(
                    col < wrap_col, next_ref[f, row, col], main_ref[f, row, col]
                )
            return carry

        def put_side(col, carry):
            def put(row, carry):
                for f in range(2):
                    f_s[f, row, col] = side_ref[f, row, col]
                return carry

            return lax.fori_loop(first_row, rows, put, carry)

        lax.fori_loop(0, first_row * cols, put_strip, 0)
        lax.fori_loop(0, first_col, put_side, 0)
        splits = len(weight_refs) // 2
        n_z, share, _ = weight_refs[0].shape
        for n, ref in enumerate(weight_refs):
            core = info_ref[4] if n < splits else 1 - info_ref[4]
            part = lax.rem(info_ref[5] + n % splits, splits)
            for d in range(n_z):
                z = lax.rem(info_ref[3] + d, n_z)
                at = ((z * 2 + core) * splits + part) * share
                w_ref[pl.ds(pl.multiple_of(at, share), share), :] = ref[d]

    places = []
    for k in range(WR):
        row = lax.rem(first_row + (step // grid_a) * WR + k, rows)
        start = jnp.where(row < first_row, wrap_col, first_col) + (step % grid_a) * WA
        for m in range(WA):
            places.append((row, lax.rem(start + m, cols)))
    for at, (row, col) in enumerate(places):
        x_s[at * WZ:(at + 1) * WZ, :] = f_s[0, row, col].astype(jnp.float32)
        g_s[at * WZ:(at + 1) * WZ, :] = f_s[1, row, col].astype(jnp.float32)
    x = x_s[...]
    gs = g_s[...].astype(jnp.bfloat16)
    gain = gain_ref[...]
    centred = x - jnp.mean(x, axis=1, keepdims=True)
    inv = lax.rsqrt(jnp.mean(centred * centred, axis=1, keepdims=True) + EPS)
    xhat = centred * inv
    xhat_s[...] = xhat
    hidden = (xhat * gain).astype(jnp.bfloat16)
    scaling = HD ** (-0.5)
    q_scaled = mm(hidden, w_ref[:, :width]) * (scaling * LOG2E)
    qkv_s[:, :width] = q_scaled.astype(jnp.bfloat16)
    qkv_s[:, width:] = mm(hidden, w_ref[:, width: 3 * width]).astype(jnp.bfloat16)
    da_s[...] = mm(gs, w_ref[:, 3 * width:], NT).astype(jnp.bfloat16)
    lane = lax.broadcasted_iota(jnp.int32, (1, LANES), 1)
    per_group = LANES // HD

    at_once = width // LANES
    heads = at_once * per_group

    def some_groups(step, carry):
        loaded, taken = {}, {}

        def load(g):
            base = pl.multiple_of((step * at_once + g) * LANES, LANES)
            q = qkv_s[:, pl.ds(base, LANES)]
            k = qkv_s[:, pl.ds(width + base, LANES)]
            v = qkv_s[:, pl.ds(2 * width + base, LANES)]
            da = da_s[:, pl.ds(base, LANES)]
            loaded[g] = q, k, v, da
            k_t = k.astype(jnp.float32).T.astype(jnp.bfloat16)
            v_t = v.astype(jnp.float32).T.astype(jnp.bfloat16)
            taken[g] = k_t, v_t, da.astype(jnp.float32).T

        dv, dk = [None] * at_once, [None] * at_once
        for_v, for_k = [[] for _ in range(at_once)], [[] for _ in range(at_once)]

        def stacked(pairs):
            left = jnp.concatenate([pair[0] for pair in pairs], axis=1)
            return mm(left, jnp.concatenate([pair[1] for pair in pairs], axis=0))

        att_t, dq_t = [[] for _ in range(at_once)], [[] for _ in range(at_once)]

        def products(n):
            g, h = n // per_group, n % per_group
            if g not in loaded:
                load(g)
            q, k, v, da = loaded[g]
            mine = (lane >= h * HD) & (lane < (h + 1) * HD)
            mask = jnp.where(mine, 1.0, 0.0).astype(jnp.bfloat16)
            qm = q * mask
            dam = da * mask
            return qm, dam, mm(k, qm, NT), mm(v, dam, NT)

        def forward(n, ready):
            g, h = n // per_group, n % per_group
            qm, dam, s, dp = ready
            _, v_t, da_t = taken[g]
            mine_t = slice(h * HD, (h + 1) * HD)
            e = jnp.exp2(s - jnp.max(s, axis=0, keepdims=True))
            p = e * (1.0 / jnp.sum(e, axis=0, keepdims=True))
            p_low = p.astype(jnp.bfloat16)
            att = mm(v_t[mine_t], p_low)
            att_t[g].append(att)
            for_v[g].append((p_low, dam))
            if h == per_group - 1:
                dv[g] = stacked(for_v[g])
            return p, dp, jnp.sum(att * da_t[mine_t], axis=0, keepdims=True), qm

        def backward(n, softened):
            g, h = n // per_group, n % per_group
            p, dp, delta, qm = softened
            ds = (p * (dp - delta)).astype(jnp.bfloat16)
            for_k[g].append((ds, qm))
            if h == per_group - 1:
                dk[g] = stacked(for_k[g])
            dq_t[g].append(mm(taken[g][0][h * HD:(h + 1) * HD], ds))

        ready, softened = products(0), None
        for n in range(heads):
            now = ready
            if n + 1 < heads:
                ready = products(n + 1)
            before, softened = softened, forward(n, now)
            if before is not None:
                backward(n - 1, before)
        backward(heads - 1, softened)
        for g in range(at_once):
            base = pl.multiple_of((step * at_once + g) * LANES, LANES)
            att_s[:, pl.ds(base, LANES)] = (
                jnp.concatenate(att_t[g], axis=0).T.astype(jnp.bfloat16)
            )
            dqkv_s[:, pl.ds(base, LANES)] = (
                jnp.concatenate(dq_t[g], axis=0).T * scaling
            ).astype(jnp.bfloat16)
            dqkv_s[:, pl.ds(width + base, LANES)] = (dk[g] * (1.0 / LOG2E)).astype(jnp.bfloat16)
            dqkv_s[:, pl.ds(2 * width + base, LANES)] = dv[g].astype(jnp.bfloat16)
        return carry

    lax.fori_loop(0, width // LANES // at_once, some_groups, 0)
    att = att_s[...]
    d_qkv = dqkv_s[...]
    d_hidden = mm(d_qkv, w_ref[:, : 3 * width], NT)
    xhat = xhat_s[...]
    term_gain = jnp.sum(d_hidden * xhat, axis=0, keepdims=True)
    d_normed = d_hidden * gain
    y = x_s[...] + mm(att, w_ref[:, 3 * width:])
    dx = g_s[...] + inv * (
        d_normed
        - jnp.mean(d_normed, axis=1, keepdims=True)
        - xhat * jnp.mean(d_normed * xhat, axis=1, keepdims=True)
    )
    for at, (row, col) in enumerate(places):
        y_ref[row, col] = y[at * WZ:(at + 1) * WZ].astype(jnp.bfloat16)
        dx_ref[row, col] = dx[at * WZ:(at + 1) * WZ].astype(jnp.bfloat16)
    here = pl.ds(pl.multiple_of(step * tokens, tokens), tokens)
    hid_all[here, :] = hidden
    att_all[here, :] = att
    gs_all[here, :] = gs
    dqkv_all[here, :] = d_qkv

    @pl.when(step == 0)
    def _():
        gain_s[...] = jnp.zeros_like(gain_s)

    gain_s[...] += term_gain

    @pl.when(step == steps - 1)
    def _():
        for f, ref in enumerate((y_ref, dx_ref)):
            strip_ref[f] = ref[:rim_rows]
            rim_ref[f] = ref[:, :rim_cols]
        g_qkv = mm(hid_all[...], dqkv_all[...], TN).astype(jnp.bfloat16)
        g_out = mm(att_all[...], gs_all[...], TN).astype(jnp.bfloat16)
        gg_ref[...] = gain_s[...]
        if len(gw_ref.shape) == 2:
            gw_ref[:, : 3 * width] = g_qkv
            gw_ref[:, 3 * width:] = g_out
        else:
            cores, n_rad, n_z, part, _ = gw_ref.shape
            extra = jnp.concatenate(
                [gain_s[:, n * LANES:(n + 1) * LANES] for n in range(width // LANES)]
                + [jnp.zeros((part - width // LANES, LANES), jnp.float32)],
                axis=0,
            ).astype(jnp.bfloat16)
            for n in range(cores * n_rad * n_z):
                z, core, i = n // n_rad // cores, n // n_rad % cores, n % n_rad
                here = gw_ref.at[core, i, z]
                here[:, : 3 * width] = g_qkv[n * part:(n + 1) * part]
                here[:, 3 * width: 4 * width] = g_out[n * part:(n + 1) * part]
                here[:, 4 * width:] = extra


def block_pass(info, x, g, side, main, following, gain, weights, term_shape):
    rows, cols, depth, width = x.shape
    tokens = WR * WA * WZ
    number = rows * cols * depth

    def whole(shape):
        return pl.BlockSpec(shape, lambda i, info: (0,) * len(shape))

    bf, f32 = jnp.bfloat16, jnp.float32
    strip_shape = (2, WR - 1, cols, depth, width)
    rim_shape = (2, rows, WA - 1, depth, width)
    ins = (x, g, side, main, following, gain) + tuple(weights)
    outs = [
        (x.shape, bf), (x.shape, bf), (strip_shape, bf), (rim_shape, bf),
        (term_shape, bf), ((1, width), f32),
    ]
    return pl.pallas_call(
        block_kernel,
        grid_spec=pltpu.PrefetchScalarGridSpec(
            num_scalar_prefetch=1,
            grid=(number // tokens,),
            in_specs=[whole(array.shape) for array in ins],
            out_specs=[whole(shape) for shape, _ in outs],
            scratch_shapes=[
                pltpu.VMEM((2,) + x.shape, bf),
                pltpu.VMEM((width, 4 * width), bf),
                pltpu.VMEM((tokens, width), f32),
                pltpu.VMEM((tokens, width), f32),
                pltpu.VMEM((tokens, width), f32),
                pltpu.VMEM((tokens, 3 * width), bf),
                pltpu.VMEM((tokens, width), bf),
                pltpu.VMEM((tokens, width), bf),
                pltpu.VMEM((tokens, 3 * width), bf),
                pltpu.VMEM((number, width), bf),
                pltpu.VMEM((number, width), bf),
                pltpu.VMEM((number, width), bf),
                pltpu.VMEM((number, 3 * width), bf),
                pltpu.VMEM((1, width), f32),
            ],
        ),
        out_shape=[jax.ShapeDtypeStruct(shape, kind) for shape, kind in outs],
        compiler_params=pltpu.CompilerParams(vmem_limit_bytes=56 * 1024 * 1024),
        cost_estimate=pl.CostEstimate(
            flops=number * width * width * 24, bytes_accessed=16 * 2 ** 20, transcendentals=0
        ),
        name="block_pass",
    )(info, *ins)


BOTH = ("rad", "azi")


def route(pairs, array, back):
    n_azi = lax.axis_size("azi")
    flat = [(a[0] * n_azi + a[1], b[0] * n_azi + b[1]) for a, b in pairs]
    return lax.ppermute(array, BOTH, [(t, s) if back else (s, t) for s, t in flat])


def strip_routes(hops, back):
    n_rad, n_azi = lax.axis_size("rad"), lax.axis_size("azi")
    azi = range(n_azi)
    near = [((i + 1, j), (i, j)) for i in range(n_rad - 1) for j in azi]
    wrap = [((0, (j + hops) % n_azi), (n_rad - 1, j)) for j in azi]
    return near, wrap


def beside(array, back):
    n_rad, n_azi = lax.axis_size("rad"), lax.axis_size("azi")
    pairs = [((i, (j + 1) % n_azi), (i, j)) for i in range(n_rad) for j in range(n_azi)]
    return route(pairs, array, back)


def over_switch(body, arrays, shift_rad, hops):
    n_azi = lax.axis_size("azi")
    sizes = range(1, WR) if n_azi <= 16 else [WR - 1]
    branches = [body(rows, n) for rows in sizes for n in range(n_azi)]
    index = (shift_rad - 1) * n_azi + hops if len(sizes) > 1 else hops
    return lax.switch(index, branches, *arrays)


def full_rows(array):
    missing = WR - 1 - array.shape[1]
    return jnp.pad(array, ((0, 0), (0, missing), (0, 0), (0, 0), (0, 0)))


def radial_strip(strip, shift_rad, hops, back):
    def body(rows, hops):
        def send(strip):
            near, wrap = strip_routes(hops, back)
            return full_rows(route(near + wrap, strip[:, :rows], back))

        return send

    return over_switch(body, (strip,), shift_rad, hops)


def permuted(array, axis, target):
    count = lax.axis_size(axis)
    return lax.ppermute(array, axis, [(n, target(n)) for n in range(count)])


def scatter_sum(pieces, index, send, hold=lambda arrays: arrays):
    count = pieces.shape[0]
    if count > 4 and count % 2 == 0:
        half = count // 2
        halves = pieces.reshape((2, half) + pieces.shape[1:])
        upper = index // half
        kept = lax.dynamic_index_in_dim(halves, upper, 0, keepdims=False)
        given = lax.dynamic_index_in_dim(halves, 1 - upper, 0, keepdims=False)
        got = send(given, lambda n: (n + half) % count)
        kept = (kept.astype(jnp.float32) + got.astype(jnp.float32)).astype(pieces.dtype)
        return scatter_sum(
            kept,
            index % half,
            lambda array, to: send(array, lambda n: n // half * half + to(n % half)),
            hold,
        )
    total = lax.dynamic_index_in_dim(pieces, index, 0, keepdims=False).astype(jnp.float32)
    arrived = []
    for d in range(1, count):
        given = lax.dynamic_index_in_dim(pieces, (index + d) % count, 0, keepdims=False)
        arrived.append(send(given, lambda n: (n + d) % count))
    for got in hold(arrived):
        total = total + got.astype(jnp.float32)
    return total.astype(pieces.dtype)


def over_core(cores):
    return lambda array, to: permuted(
        array, "azi", lambda n: n // cores * cores + to(n % cores)
    )


def over_z(cores):
    return lambda array, to: permuted(
        array, "azi", lambda n: to(n // cores) * cores + n % cores
    )


def over_rad(array, to):
    return permuted(array, "rad", to)


def fetch_all(strip, side, shard, shift_rad, hops, cores):
    n_rad, n_z = lax.axis_size("rad"), lax.axis_size("azi") // cores
    first_z = first_part = 0
    split = n_z <= 4 and n_rad % 2 == 0
    if split:
        first_z = lax.axis_index("azi") // cores
        first_part = lax.axis_index("rad") % 2
        share = shard.shape[0] // 2
        half = lax.dynamic_slice_in_dim(shard, first_part * share, share, 0)
        mine = [half] + [over_z(cores)(half, lambda n: (n - d) % n_z) for d in range(1, n_z)]
    else:
        groups = [list(range(core, n_z * cores, cores)) for core in range(cores)]
        mine = [lax.all_gather(shard, "azi", axis=0, axis_index_groups=groups)]
    side = beside(side, False)
    main = radial_strip(strip, shift_rad, hops, False)
    main, side, mine = lax.optimization_barrier((main, side, mine))
    following = beside(main, False)
    if split:
        mine = jnp.stack(mine)
        mine = [mine, over_rad(mine, lambda n: n // 2 * 2 + (n + 1) % 2)]
    weights = mine + [over_core(cores)(part, lambda n: (n + 1) % cores) for part in mine]
    return main, following, side, weights, first_z, first_part


def on_device(tokens, cotangent, ln_gain, qkv_weight, out_weight, shear_offset, window_shift):
    rows_dev, cols_dev, depth, width = tokens.shape
    assert depth == WZ
    number = rows_dev * cols_dev * depth
    n_rad = lax.axis_size("rad")
    n_azi = lax.axis_size("azi")
    at_rad = lax.axis_index("rad")
    total_cols = cols_dev * n_azi
    rim_rows, rim_cols = WR - 1, WA - 1
    shift_rad = window_shift[0]
    shift_azi = window_shift[1]
    offset = shear_offset[0]
    amount = (offset + shift_azi) % total_cols
    hops = amount // cols_dev
    cores = 2
    assert n_azi % cores == 0
    shard = jnp.concatenate([qkv_weight, out_weight], axis=1)
    side = jnp.stack([tokens[:, :rim_cols], cotangent[:, :rim_cols]])
    strip = jnp.stack([tokens[:rim_rows], cotangent[:rim_rows]])
    main, following, side, weights, first_z, first_part = fetch_all(
        strip, side, shard, shift_rad, hops, cores
    )
    last = at_rad == n_rad - 1
    wrap_col = jnp.where(last, amount % cols_dev, shift_azi)
    at_core = lax.axis_index("azi") % cores
    info = [shift_rad, shift_azi, wrap_col, first_z, at_core, first_part]
    info = jnp.stack([jnp.asarray(value, jnp.int32) for value in info])
    part_rows = width // n_azi // n_rad
    placed = part_rows % 16 == 0
    pieces_shape = (cores, n_rad, n_azi // cores, part_rows, 4 * width + LANES)
    y, dx, strip, side, term, gain = block_pass(
        info, tokens, cotangent, side, main, following, ln_gain.reshape(1, width), weights,
        pieces_shape if placed else (width, 4 * width),
    )
    following = beside(strip, True)
    following, side = lax.optimization_barrier((following, side))
    side = beside(side, True)
    col = jnp.arange(cols_dev, dtype=jnp.int32).reshape(1, 1, cols_dev, 1, 1)
    if placed:
        at_azi = lax.axis_index("azi")
        term = scatter_sum(term, at_azi % cores, over_core(cores))
        strip_back = []

        def beside_strip(arrays):
            arrays, back, beside_it = lax.optimization_barrier(
                (arrays, radial_strip(strip, shift_rad, hops, True), side)
            )
            strip_back.extend((back, beside_it))
            return arrays

        term = scatter_sum(term, at_rad, over_rad)
        following, term = lax.optimization_barrier((following, term))
        strip = jnp.where(col < wrap_col, following, strip)
        mine = scatter_sum(term, at_azi // cores, over_z(cores), beside_strip)
        strip, side = strip_back
    else:
        strip = jnp.where(col < wrap_col, following, strip)
        strip = radial_strip(strip, shift_rad, hops, True)
    if placed:
        others = [over_rad(mine, lambda n: (n - d) % n_rad) for d in range(1, n_rad)]
        share = jnp.roll(jnp.stack([mine] + others), at_rad, axis=0)
    col = jnp.arange(rim_cols, dtype=jnp.int32).reshape(1, rim_cols, 1, 1)
    row = jnp.arange(rim_rows, dtype=jnp.int32).reshape(rim_rows, 1, 1, 1)

    def finish(array, strip, side):
        edge = jnp.where(col < shift_azi, side, array[:, :rim_cols])
        array = lax.dynamic_update_slice(array, edge, (0, 0, 0, 0))
        edge = jnp.where(row < shift_rad, strip, array[:rim_rows])
        return lax.dynamic_update_slice(array, edge, (0, 0, 0, 0))

    block_out = finish(y, strip[0], side[0])
    grad_tokens = finish(dx, strip[1], side[1])
    if placed:
        gain = share[0, :, 4 * width:].reshape(-1)[:width].astype(jnp.float32)
        share = share[:, :, : 4 * width].reshape(n_rad * part_rows, 4 * width)
    else:
        gain = lax.psum(gain[0], BOTH)
        share = lax.psum_scatter(term, "azi", scatter_dimension=0, tiled=True)
        share = lax.psum(share, "rad")
    share = share.astype(jnp.float32)
    factor = float(number * n_rad * n_azi) ** (-0.5)
    grad_qkv = share[:, : 3 * width] * factor
    grad_out = share[:, 3 * width :] * factor
    return (block_out, grad_tokens, grad_qkv, grad_out, gain * factor)


def solution(mesh):
    in_specs = (
        P("rad", "azi", None, None),
        P("rad", "azi", None, None),
        P(),
        P("azi", None),
        P("azi", None),
        P(),
        P(),
    )
    out_specs = (
        P("rad", "azi", None, None),
        P("rad", "azi", None, None),
        P("azi", None),
        P("azi", None),
        P(),
    )
    return jax.shard_map(
        on_device, mesh=mesh, in_specs=in_specs, out_specs=out_specs, check_vma=False
    )
```

```python
import functools

import jax
import jax.numpy as jnp
from jax import lax
from jax.experimental import pallas as pl
from jax.experimental.pallas import tpu as pltpu
from jax.sharding import PartitionSpec as P

HEADS = 16
HD = 32
WR = 4
WA = 8
WZ = 8
LANES = 128
LOG2E = 1.4426950408889634

EPS = 1e-05
NT = (((1,), (1,)), ((), ()))
TN = (((0,), (0,)), ((), ()))


def mm(a, b, dims=(((1,), (0,)), ((), ()))):
    return lax.dot_general(a, b, dims, preferred_element_type=jnp.float32)


def block_kernel(info_ref, *refs):
    x_ref, g_ref, side_ref, main_ref, next_ref, gain_ref = refs[:6]
    weight_refs, refs = refs[6:-21], refs[-21:]
    y_ref, dx_ref, strip_ref, rim_ref, gw_ref, given_ref, gg_ref, f_s, w_ref = refs[:9]
    x_s, g_s, xhat_s, qkv_s, da_s, att_s, dqkv_s = refs[9:16]
    hid_all, att_all, gs_all, dqkv_all, gain_s = refs[16:21]
    step = pl.program_id(0)
    steps = pl.num_programs(0)
    rows, cols, depth, width = x_ref.shape
    rim_rows, rim_cols = strip_ref.shape[1], rim_ref.shape[2]
    grid_a = cols // WA
    tokens = WR * WA * WZ
    first_row, first_col, wrap_col = info_ref[0], info_ref[1], info_ref[2]

    @pl.when(step == 0)
    def _():
        f_s[0] = x_ref[...]
        f_s[1] = g_ref[...]

        def put_strip(n, carry):
            row, col = n // cols, lax.rem(n, cols)
            for f in range(2):
                f_s[f, row, col] = jnp.where(
                    col < wrap_col, next_ref[f, row, col], main_ref[f, row, col]
                )
            return carry

        def put_side(col, carry):
            def put(row, carry):
                for f in range(2):
                    f_s[f, row, col] = side_ref[f, row, col]
                return carry

            return lax.fori_loop(first_row, rows, put, carry)

        lax.fori_loop(0, first_row * cols, put_strip, 0)
        lax.fori_loop(0, first_col, put_side, 0)
        splits = len(weight_refs) // 2
        n_z, share, _ = weight_refs[0].shape
        for n, ref in enumerate(weight_refs):
            core = info_ref[4] if n < splits else 1 - info_ref[4]
            part = lax.rem(info_ref[5] + n % splits, splits)
            for d in range(n_z):
                z = lax.rem(info_ref[3] + d, n_z)
                at = ((z * 2 + core) * splits + part) * share
                w_ref[pl.ds(pl.multiple_of(at, share), share), :] = ref[d]

    places = []
    for k in range(WR):
        row = lax.rem(first_row + (step // grid_a) * WR + k, rows)
        start = jnp.where(row < first_row, wrap_col, first_col) + (step % grid_a) * WA
        for m in range(WA):
            places.append((row, lax.rem(start + m, cols)))
    for at, (row, col) in enumerate(places):
        x_s[at * WZ:(at + 1) * WZ, :] = f_s[0, row, col].astype(jnp.float32)
        g_s[at * WZ:(at + 1) * WZ, :] = f_s[1, row, col].astype(jnp.float32)
    x = x_s[...]
    gs = g_s[...].astype(jnp.bfloat16)
    gain = gain_ref[...]
    centred = x - jnp.mean(x, axis=1, keepdims=True)
    inv = lax.rsqrt(jnp.mean(centred * centred, axis=1, keepdims=True) + EPS)
    xhat = centred * inv
    xhat_s[...] = xhat
    hidden = (xhat * gain).astype(jnp.bfloat16)
    scaling = HD ** (-0.5)
    q_scaled = mm(hidden, w_ref[:, :width]) * (scaling * LOG2E)
    qkv_s[:, :width] = q_scaled.astype(jnp.bfloat16)
    qkv_s[:, width:] = mm(hidden, w_ref[:, width: 3 * width]).astype(jnp.bfloat16)
    da_s[...] = mm(gs, w_ref[:, 3 * width:], NT).astype(jnp.bfloat16)
    lane = lax.broadcasted_iota(jnp.int32, (1, LANES), 1)
    per_group = LANES // HD

    at_once = width // LANES
    heads = at_once * per_group

    def some_groups(step, carry):
        loaded, taken = {}, {}

        def load(g):
            base = pl.multiple_of((step * at_once + g) * LANES, LANES)
            q = qkv_s[:, pl.ds(base, LANES)]
            k = qkv_s[:, pl.ds(width + base, LANES)]
            v = qkv_s[:, pl.ds(2 * width + base, LANES)]
            da = da_s[:, pl.ds(base, LANES)]
            loaded[g] = q, k, v, da
            k_t = k.astype(jnp.float32).T.astype(jnp.bfloat16)
            v_t = v.astype(jnp.float32).T.astype(jnp.bfloat16)
            taken[g] = k_t, v_t, da.astype(jnp.float32).T

        zeros = jnp.zeros((tokens, LANES), jnp.float32)
        dv, dk = [zeros] * at_once, [zeros] * at_once
        att_t, dq_t = [[] for _ in range(at_once)], [[] for _ in range(at_once)]

        def products(n):
            g, h = n // per_group, n % per_group
            if g not in loaded:
                load(g)
            q, k, v, da = loaded[g]
            mine = (lane >= h * HD) & (lane < (h + 1) * HD)
            mask = jnp.where(mine, 1.0, 0.0).astype(jnp.bfloat16)
            qm = q * mask
            dam = da * mask
            return qm, dam, mm(k, qm, NT), mm(v, dam, NT)

        def forward(n, ready):
            g, h = n // per_group, n % per_group
            qm, dam, s, dp = ready
            _, v_t, da_t = taken[g]
            mine_t = slice(h * HD, (h + 1) * HD)
            e = jnp.exp2(s - jnp.max(s, axis=0, keepdims=True))
            p = e * (1.0 / jnp.sum(e, axis=0, keepdims=True))
            p_low = p.astype(jnp.bfloat16)
            att = mm(v_t[mine_t], p_low)
            att_t[g].append(att)
            dv[g] += mm(p_low, dam)
            return p, dp, jnp.sum(att * da_t[mine_t], axis=0, keepdims=True), qm

        def backward(n, softened):
            g, h = n // per_group, n % per_group
            p, dp, delta, qm = softened
            ds = (p * (dp - delta)).astype(jnp.bfloat16)
            dk[g] += mm(ds, qm)
            dq_t[g].append(mm(taken[g][0][h * HD:(h + 1) * HD], ds))

        ready, softened = products(0), None
        for n in range(heads):
            now = ready
            if n + 1 < heads:
                ready = products(n + 1)
            before, softened = softened, forward(n, now)
            if before is not None:
                backward(n - 1, before)
        backward(heads - 1, softened)
        for g in range(at_once):
            base = pl.multiple_of((step * at_once + g) * LANES, LANES)
            att_s[:, pl.ds(base, LANES)] = (
                jnp.concatenate(att_t[g], axis=0).T.astype(jnp.bfloat16)
            )
            dqkv_s[:, pl.ds(base, LANES)] = (
                jnp.concatenate(dq_t[g], axis=0).T * scaling
            ).astype(jnp.bfloat16)
            dqkv_s[:, pl.ds(width + base, LANES)] = (dk[g] * (1.0 / LOG2E)).astype(jnp.bfloat16)
            dqkv_s[:, pl.ds(2 * width + base, LANES)] = dv[g].astype(jnp.bfloat16)
        return carry

    lax.fori_loop(0, width // LANES // at_once, some_groups, 0)
    att = att_s[...]
    d_qkv = dqkv_s[...]
    d_hidden = mm(d_qkv, w_ref[:, : 3 * width], NT)
    xhat = xhat_s[...]
    term_gain = jnp.sum(d_hidden * xhat, axis=0, keepdims=True)
    d_normed = d_hidden * gain
    y = x_s[...] + mm(att, w_ref[:, 3 * width:])
    dx = g_s[...] + inv * (
        d_normed
        - jnp.mean(d_normed, axis=1, keepdims=True)
        - xhat * jnp.mean(d_normed * xhat, axis=1, keepdims=True)
    )
    for at, (row, col) in enumerate(places):
        y_ref[row, col] = y[at * WZ:(at + 1) * WZ].astype(jnp.bfloat16)
        dx_ref[row, col] = dx[at * WZ:(at + 1) * WZ].astype(jnp.bfloat16)
    here = pl.ds(pl.multiple_of(step * tokens, tokens), tokens)
    hid_all[here, :] = hidden
    att_all[here, :] = att
    gs_all[here, :] = gs
    dqkv_all[here, :] = d_qkv

    @pl.when(step == 0)
    def _():
        gain_s[...] = jnp.zeros_like(gain_s)

    gain_s[...] += term_gain

    @pl.when(step == steps - 1)
    def _():
        for f, ref in enumerate((y_ref, dx_ref)):
            strip_ref[f] = ref[:rim_rows]
            rim_ref[f] = ref[:, :rim_cols]
        g_qkv = mm(hid_all[...], dqkv_all[...], TN).astype(jnp.bfloat16)
        g_out = mm(att_all[...], gs_all[...], TN).astype(jnp.bfloat16)
        gg_ref[...] = gain_s[...]
        if len(gw_ref.shape) == 2:
            gw_ref[:, : 3 * width] = g_qkv
            gw_ref[:, 3 * width:] = g_out
        else:
            n_rad, n_z, part, _ = gw_ref.shape
            extra = jnp.concatenate(
                [gain_s[:, n * LANES:(n + 1) * LANES] for n in range(width // LANES)]
                + [jnp.zeros((part - width // LANES, LANES), jnp.float32)],
                axis=0,
            ).astype(jnp.bfloat16)

            def place(kept_core):
                for n in range(2 * n_rad * n_z):
                    z, core, i = n // n_rad // 2, n // n_rad % 2, n % n_rad
                    rad_ahead = lax.rem(i + n_rad - info_ref[6], n_rad)
                    z_ahead = lax.rem(z + n_z - info_ref[7], n_z)
                    ref = gw_ref if core == kept_core else given_ref
                    here = ref.at[rad_ahead, z_ahead]
                    here[:, : 3 * width] = g_qkv[n * part:(n + 1) * part]
                    here[:, 3 * width: 4 * width] = g_out[n * part:(n + 1) * part]
                    here[:, 4 * width:] = extra

            for kept_core in range(2):
                pl.when(info_ref[4] == kept_core)(functools.partial(place, kept_core))


def block_pass(info, x, g, side, main, following, gain, weights, term_shape):
    rows, cols, depth, width = x.shape
    tokens = WR * WA * WZ
    number = rows * cols * depth

    def whole(shape):
        return pl.BlockSpec(shape, lambda i, info: (0,) * len(shape))

    bf, f32 = jnp.bfloat16, jnp.float32
    strip_shape = (2, WR - 1, cols, depth, width)
    rim_shape = (2, rows, WA - 1, depth, width)
    ins = (x, g, side, main, following, gain) + tuple(weights)
    outs = [
        (x.shape, bf), (x.shape, bf), (strip_shape, bf), (rim_shape, bf),
        (term_shape, bf), (term_shape, bf), ((1, width), f32),
    ]
    return pl.pallas_call(
        block_kernel,
        grid_spec=pltpu.PrefetchScalarGridSpec(
            num_scalar_prefetch=1,
            grid=(number // tokens,),
            in_specs=[whole(array.shape) for array in ins],
            out_specs=[whole(shape) for shape, _ in outs],
            scratch_shapes=[
                pltpu.VMEM((2,) + x.shape, bf),
                pltpu.VMEM((width, 4 * width), bf),
                pltpu.VMEM((tokens, width), f32),
                pltpu.VMEM((tokens, width), f32),
                pltpu.VMEM((tokens, width), f32),
                pltpu.VMEM((tokens, 3 * width), bf),
                pltpu.VMEM((tokens, width), bf),
                pltpu.VMEM((tokens, width), bf),
                pltpu.VMEM((tokens, 3 * width), bf),
                pltpu.VMEM((number, width), bf),
                pltpu.VMEM((number, width), bf),
                pltpu.VMEM((number, width), bf),
                pltpu.VMEM((number, 3 * width), bf),
                pltpu.VMEM((1, width), f32),
            ],
        ),
        out_shape=[jax.ShapeDtypeStruct(shape, kind) for shape, kind in outs],
        compiler_params=pltpu.CompilerParams(vmem_limit_bytes=56 * 1024 * 1024),
        cost_estimate=pl.CostEstimate(
            flops=number * width * width * 24, bytes_accessed=16 * 2 ** 20, transcendentals=0
        ),
        name="block_pass",
    )(info, *ins)


BOTH = ("rad", "azi")


def route(pairs, array, back):
    n_azi = lax.axis_size("azi")
    flat = [(a[0] * n_azi + a[1], b[0] * n_azi + b[1]) for a, b in pairs]
    return lax.ppermute(array, BOTH, [(t, s) if back else (s, t) for s, t in flat])


def strip_routes(hops, back):
    n_rad, n_azi = lax.axis_size("rad"), lax.axis_size("azi")
    azi = range(n_azi)
    near = [((i + 1, j), (i, j)) for i in range(n_rad - 1) for j in azi]
    wrap = [((0, (j + hops) % n_azi), (n_rad - 1, j)) for j in azi]
    return near, wrap


def beside(array, back):
    n_rad, n_azi = lax.axis_size("rad"), lax.axis_size("azi")
    pairs = [((i, (j + 1) % n_azi), (i, j)) for i in range(n_rad) for j in range(n_azi)]
    return route(pairs, array, back)


def over_switch(body, arrays, shift_rad, hops):
    n_azi = lax.axis_size("azi")
    sizes = range(1, WR) if n_azi <= 16 else [WR - 1]
    branches = [body(rows, n) for rows in sizes for n in range(n_azi)]
    index = (shift_rad - 1) * n_azi + hops if len(sizes) > 1 else hops
    return lax.switch(index, branches, *arrays)


def full_rows(array):
    missing = WR - 1 - array.shape[1]
    return jnp.pad(array, ((0, 0), (0, missing), (0, 0), (0, 0), (0, 0)))


def radial_strip(strip, shift_rad, hops, back):
    def body(rows, hops):
        def send(strip):
            near, wrap = strip_routes(hops, back)
            return full_rows(route(near + wrap, strip[:, :rows], back))

        return send

    return over_switch(body, (strip,), shift_rad, hops)


def permuted(array, axis, target):
    count = lax.axis_size(axis)
    return lax.ppermute(array, axis, [(n, target(n)) for n in range(count)])


def scatter_sum(pieces, send, hold=lambda arrays: arrays):
    count = pieces.shape[0]
    arrived = [send(pieces[d], lambda n: (n + d) % count) for d in range(1, count)]
    total = pieces[0].astype(jnp.float32)
    for got in hold(arrived):
        total = total + got.astype(jnp.float32)
    return total.astype(pieces.dtype)


def over_core(cores):
    return lambda array, to: permuted(
        array, "azi", lambda n: n // cores * cores + to(n % cores)
    )


def over_z(cores):
    return lambda array, to: permuted(
        array, "azi", lambda n: to(n // cores) * cores + n % cores
    )


def over_rad(array, to):
    return permuted(array, "rad", to)


def fetch_all(strip, side, shard, shift_rad, hops, cores):
    n_rad, n_z = lax.axis_size("rad"), lax.axis_size("azi") // cores
    first_z = first_part = 0
    split = n_z <= 4 and n_rad % 2 == 0
    if split:
        first_z = lax.axis_index("azi") // cores
        first_part = lax.axis_index("rad") % 2
        share = shard.shape[0] // 2
        half = lax.dynamic_slice_in_dim(shard, first_part * share, share, 0)
        mine = [half] + [over_z(cores)(half, lambda n: (n - d) % n_z) for d in range(1, n_z)]
    else:
        groups = [list(range(core, n_z * cores, cores)) for core in range(cores)]
        mine = [lax.all_gather(shard, "azi", axis=0, axis_index_groups=groups)]
    side = beside(side, False)
    main = radial_strip(strip, shift_rad, hops, False)
    main, side, mine = lax.optimization_barrier((main, side, mine))
    following = beside(main, False)
    if split:
        mine = jnp.stack(mine)
        mine = [mine, over_rad(mine, lambda n: n // 2 * 2 + (n + 1) % 2)]
    weights = mine + [over_core(cores)(part, lambda n: (n + 1) % cores) for part in mine]
    return main, following, side, weights, first_z, first_part


def on_device(tokens, cotangent, ln_gain, qkv_weight, out_weight, shear_offset, window_shift):
    rows_dev, cols_dev, depth, width = tokens.shape
    assert depth == WZ
    number = rows_dev * cols_dev * depth
    n_rad = lax.axis_size("rad")
    n_azi = lax.axis_size("azi")
    at_rad = lax.axis_index("rad")
    total_cols = cols_dev * n_azi
    rim_rows, rim_cols = WR - 1, WA - 1
    shift_rad = window_shift[0]
    shift_azi = window_shift[1]
    offset = shear_offset[0]
    amount = (offset + shift_azi) % total_cols
    hops = amount // cols_dev
    cores = 2
    assert n_azi % cores == 0
    shard = jnp.concatenate([qkv_weight, out_weight], axis=1)
    side = jnp.stack([tokens[:, :rim_cols], cotangent[:, :rim_cols]])
    strip = jnp.stack([tokens[:rim_rows], cotangent[:rim_rows]])
    main, following, side, weights, first_z, first_part = fetch_all(
        strip, side, shard, shift_rad, hops, cores
    )
    last = at_rad == n_rad - 1
    wrap_col = jnp.where(last, amount % cols_dev, shift_azi)
    at_core = lax.axis_index("azi") % cores
    info = [shift_rad, shift_azi, wrap_col, first_z, at_core, first_part]
    info += [at_rad, lax.axis_index("azi") // cores]
    info = jnp.stack([jnp.asarray(value, jnp.int32) for value in info])
    part_rows = width // n_azi // n_rad
    placed = part_rows % 16 == 0
    pieces_shape = (n_rad, n_azi // cores, part_rows, 4 * width + LANES)
    y, dx, strip, side, term, given, gain = block_pass(
        info, tokens, cotangent, side, main, following, ln_gain.reshape(1, width), weights,
        pieces_shape if placed else (width, 4 * width),
    )
    following = beside(strip, True)
    following, side = lax.optimization_barrier((following, side))
    side = beside(side, True)
    col = jnp.arange(cols_dev, dtype=jnp.int32).reshape(1, 1, cols_dev, 1, 1)
    if placed:
        got = over_core(cores)(given, lambda n: (n + 1) % cores)
        term = (term.astype(jnp.float32) + got.astype(jnp.float32)).astype(term.dtype)
        strip_back = []

        def beside_strip(arrays):
            arrays, back, beside_it = lax.optimization_barrier(
                (arrays, radial_strip(strip, shift_rad, hops, True), side)
            )
            strip_back.extend((back, beside_it))
            return arrays

        term = scatter_sum(term, over_rad)
        following, term = lax.optimization_barrier((following, term))
        strip = jnp.where(col < wrap_col, following, strip)
        mine = scatter_sum(term, over_z(cores), beside_strip)
        strip, side = strip_back
    else:
        strip = jnp.where(col < wrap_col, following, strip)
        strip = radial_strip(strip, shift_rad, hops, True)
    if placed:
        others = [over_rad(mine, lambda n: (n - d) % n_rad) for d in range(1, n_rad)]
        share = jnp.roll(jnp.stack([mine] + others), at_rad, axis=0)
    col = jnp.arange(rim_cols, dtype=jnp.int32).reshape(1, rim_cols, 1, 1)
    row = jnp.arange(rim_rows, dtype=jnp.int32).reshape(rim_rows, 1, 1, 1)

    def finish(array, strip, side):
        edge = jnp.where(col < shift_azi, side, array[:, :rim_cols])
        array = lax.dynamic_update_slice(array, edge, (0, 0, 0, 0))
        edge = jnp.where(row < shift_rad, strip, array[:rim_rows])
        return lax.dynamic_update_slice(array, edge, (0, 0, 0, 0))

    block_out = finish(y, strip[0], side[0])
    grad_tokens = finish(dx, strip[1], side[1])
    if placed:
        gain = share[0, :, 4 * width:].reshape(-1)[:width].astype(jnp.float32)
        share = share[:, :, : 4 * width].reshape(n_rad * part_rows, 4 * width)
    else:
        gain = lax.psum(gain[0], BOTH)
        share = lax.psum_scatter(term, "azi", scatter_dimension=0, tiled=True)
        share = lax.psum(share, "rad")
    share = share.astype(jnp.float32)
    factor = float(number * n_rad * n_azi) ** (-0.5)
    grad_qkv = share[:, : 3 * width] * factor
    grad_out = share[:, 3 * width :] * factor
    return (block_out, grad_tokens, grad_qkv, grad_out, gain * factor)


def solution(mesh):
    in_specs = (
        P("rad", "azi", None, None),
        P("rad", "azi", None, None),
        P(),
        P("azi", None),
        P("azi", None),
        P(),
        P(),
    )
    out_specs = (
        P("rad", "azi", None, None),
        P("rad", "azi", None, None),
        P("azi", None),
        P("azi", None),
        P(),
    )
    return jax.shard_map(
        on_device, mesh=mesh, in_specs=in_specs, out_specs=out_specs, check_vma=False
    )
```
